256 devices in a mesh: row: 16 (over z_hi, x, core), col: 16 (over y, z_lo).
Axes of the slice: x: 4, y: 4, z: 8 (z_hi: 2, z_lo: 4; z = z_hi * 4 + z_lo), core: 2. Of those that a mesh axis runs over, the one named last changes fastest.
Arguments:
- fine_state: bfloat16 [32, 128, 4096], P(None, 'row', 'col'), may hold values from -40 to 40
- coarse_state: bfloat16 [64, 64, 2048], P(None, 'row', 'col'), may hold values from -40 to 40
- fine_inject: bfloat16 [32, 128, 4096], P(None, 'row', 'col'), may hold values from -6 to 6
- coarse_inject: bfloat16 [64, 64, 2048], P(None, 'row', 'col'), may hold values from -6 to 6
- fine_cotangent: float32 [32, 128, 4096], P(None, 'row', 'col'), may hold values from -40 to 40
- coarse_cotangent: float32 [64, 64, 2048], P(None, 'row', 'col'), may hold values from -40 to 40
- fine_first: bfloat16 [9, 160, 32], replicated, may hold values from -0.375 to 0.375
- fine_second: bfloat16 [9, 32, 160], replicated, may hold values from -0.3125 to 0.3125
- coarse_first: bfloat16 [9, 320, 64], replicated, may hold values from -0.25 to 0.25
- coarse_second: bfloat16 [9, 64, 320], replicated, may hold values from -0.25 to 0.25
- fine_gain: float32 [160], replicated, may hold values from 0.1 to 1.9
- fine_shift: float32 [160], replicated, may hold values from -3 to 3
- coarse_gain: float32 [320], replicated, may hold values from 0.1 to 1.9
- coarse_shift: float32 [320], replicated, may hold values from -3 to 3
- reduction_weight: bfloat16 [2, 2, 64, 32], replicated, may hold values from -0.5 to 0.5
- weight_up: bfloat16 [32, 64], replicated, may hold values from -0.75 to 0.75
Outputs:
- adjoint_fine: float32 [32, 128, 4096], P(None, 'row', 'col')
- adjoint_coarse: float32 [64, 64, 2048], P(None, 'row', 'col')
The draws below stay inside these ranges and needn't reach their ends.
All inputs are finite; a program needn't handle non-finite values.
Results may differ from the reference program's by a relative error of at most 0.02.
Values may be sent and summed in bfloat16 or wider, within the bound.
A program may use at most 128 MiB of HBM per device.

```python
import math
import jax
import jax.numpy as jnp
from jax import lax

C1 = 32
C2 = 64
H1 = 160
H2 = 320
GROUPS = 4
ITERS = 3
HF = 8
WF = 256
HT = 128
WT = 4096
HC = 64
WC = 2048


def scaled_field(key, noise, rising, spread):
    rows = noise.shape[1]
    cols = noise.shape[2]
    row_key, col_key = jax.random.split(key)
    row_ramp = jnp.arange(rows, dtype=jnp.float32) / max(rows - 1, 1) - 0.5
    col_ramp = jnp.arange(cols, dtype=jnp.float32) / max(cols - 1, 1) - 0.5
    row_scale = jnp.exp(math.log(rising) * row_ramp + math.log(spread) * jax.random.uniform(row_key, (rows,), jnp.float32, -0.5, 0.5))
    col_scale = jnp.exp(math.log(rising) * col_ramp + math.log(spread) * jax.random.uniform(col_key, (cols,), jnp.float32, -0.5, 0.5))
    return noise * row_scale[None, :, None] * col_scale[None, None, :]


def smooth_part(key, channels, rows, cols, height):
    signs = (jax.random.randint(key, (channels,), 0, 2) * 2 - 1).astype(jnp.float32)
    ramp = jnp.arange(rows, dtype=jnp.float32) / max(rows - 1, 1)
    return height * signs[:, None, None] * ramp[None, :, None] * jnp.ones((1, 1, cols), jnp.float32)


def block_levels(key, rising, width):
    row_blocks = HT // HF
    col_blocks = WT // WF
    row_key, col_key = jax.random.split(jax.random.fold_in(key, 97))
    row_ramp = jnp.arange(row_blocks, dtype=jnp.float32) / max(row_blocks - 1, 1) - 0.5
    col_ramp = jnp.arange(col_blocks, dtype=jnp.float32) / max(col_blocks - 1, 1) - 0.5
    row_levels = jnp.exp(math.log(rising) * row_ramp + jax.random.uniform(row_key, (row_blocks,), jnp.float32, -width, width))
    col_levels = jnp.exp(math.log(rising) * col_ramp + jax.random.uniform(col_key, (col_blocks,), jnp.float32, -width, width))
    return (row_levels, col_levels)


def leveled(field, levels, block_rows, block_cols):
    row_scale = jnp.repeat(levels[0], block_rows)
    col_scale = jnp.repeat(levels[1], block_cols)
    return jnp.clip(0.3 * field * row_scale[None, :, None] * col_scale[None, None, :], -40.0, 40.0)


def draw_fine_state(key, part):
    key = jax.random.fold_in(key, 11)
    noise_key, scale_key = jax.random.split(key)
    noise = jnp.clip(jax.random.normal(noise_key, (C1, HT, WT), jnp.float32), -4.0, 4.0)
    return scaled_field(scale_key, noise, 3.0, 3.3).astype(jnp.bfloat16)


def draw_coarse_state(key, part):
    key = jax.random.fold_in(key, 23)
    noise_key, scale_key = jax.random.split(key)
    noise = jnp.clip(jax.random.normal(noise_key, (C2, HC, WC), jnp.float32), -4.0, 4.0)
    return scaled_field(scale_key, noise, 3.0, 3.3).astype(jnp.bfloat16)


def draw_fine_cotangent(key, part):
    levels = block_levels(key, 3.0, 1.2)
    key = jax.random.fold_in(key, 37)
    noise_key, scale_key, sign_key = jax.random.split(key, 3)
    noise = jnp.clip(jax.random.normal(noise_key, (C1, HT, WT), jnp.float32), -2.0, 2.0)
    noise = noise + smooth_part(sign_key, C1, HT, WT, 1.9)
    return leveled(scaled_field(scale_key, noise, 1.0, 2.0), levels, HF, WF)


def draw_coarse_cotangent(key, part):
    levels = block_levels(key, 3.0, 1.2)
    key = jax.random.fold_in(key, 41)
    noise_key, scale_key, sign_key = jax.random.split(key, 3)
    noise = jnp.clip(jax.random.normal(noise_key, (C2, HC, WC), jnp.float32), -2.0, 2.0)
    noise = noise + smooth_part(sign_key, C2, HC, WC, 1.9)
    return leveled(scaled_field(scale_key, noise, 1.0, 2.0), levels, HF // 2, WF // 2)


def draw_fine_gain(key, part):
    key = jax.random.fold_in(key, 53)
    return 1.0 + 0.18 * jnp.clip(jax.random.normal(key, (H1,), jnp.float32), -5.0, 5.0)


def draw_coarse_gain(key, part):
    key = jax.random.fold_in(key, 59)
    return 1.0 + 0.18 * jnp.clip(jax.random.normal(key, (H2,), jnp.float32), -5.0, 5.0)


def draw_fine_second(key, part):
    key = jax.random.fold_in(key, 61)
    deviation = (2.0 * H1) ** (-0.5)
    values = deviation * jax.random.normal(key, (9, C1, H1), jnp.float32)
    return jnp.clip(values, -0.3125, 0.3125).astype(jnp.bfloat16)


def draw_coarse_second(key, part):
    key = jax.random.fold_in(key, 67)
    deviation = (2.0 * H2) ** (-0.5)
    values = deviation * jax.random.normal(key, (9, C2, H2), jnp.float32)
    return jnp.clip(values, -0.25, 0.25).astype(jnp.bfloat16)


def level_of(stream_key, shape, shards, smallest, largest):
    level, own = 1.0, jax.random.fold_in(stream_key, 6)
    for dim, shards_of in shards:
        heights = jnp.exp(jax.random.uniform(jax.random.fold_in(own, dim), (shards_of,), jnp.float32, smallest / len(shards), largest / len(shards)))
        level = level * jnp.repeat(heights, shape[dim] // shards_of).reshape([-1 if axis == dim else 1 for axis in range(len(shape))])
    return level


def centred(own_key, dims, scale, limit, pieces=(), held_as=jnp.bfloat16):
    factor_of = level_of(own_key, dims, pieces, -0.22, 0.18) if pieces else 1.0
    values = jax.random.normal(own_key, dims, jnp.float32) * scale * factor_of
    return jnp.minimum(jnp.maximum(values, -limit), limit).astype(held_as)


def setup_inputs(seed: int = 0) -> dict:
    arg_keys = jax.random.split(jax.random.key(seed), 17)
    return {
        "fine_state": draw_fine_state(jax.random.fold_in(arg_keys[16], 71), 0),
        "coarse_state": draw_coarse_state(jax.random.fold_in(arg_keys[16], 71), 0),
        "fine_inject": centred(arg_keys[2], (C1, HT, WT), 1.0, 6.0, ((1, 16), (2, 16))),
        "coarse_inject": centred(arg_keys[3], (C2, HC, WC), 1.0, 6.0, ((1, 16), (2, 16))),
        "fine_cotangent": draw_fine_cotangent(jax.random.fold_in(arg_keys[16], 71), 0),
        "coarse_cotangent": draw_coarse_cotangent(jax.random.fold_in(arg_keys[16], 71), 0),
        "fine_first": centred(arg_keys[6], (9, H1, C1), (9 * C1) ** -0.5, 0.375),
        "fine_second": draw_fine_second(jax.random.fold_in(arg_keys[16], 71), 0),
        "coarse_first": centred(arg_keys[8], (9, H2, C2), (9 * C2) ** -0.5, 0.25),
        "coarse_second": draw_coarse_second(jax.random.fold_in(arg_keys[16], 71), 0),
        "fine_gain": draw_fine_gain(jax.random.fold_in(arg_keys[16], 71), 0),
        "fine_shift": centred(arg_keys[11], (H1,), 0.5, 3.0, (), jnp.float32),
        "coarse_gain": draw_coarse_gain(jax.random.fold_in(arg_keys[16], 71), 0),
        "coarse_shift": centred(arg_keys[13], (H2,), 0.5, 3.0, (), jnp.float32),
        "reduction_weight": centred(arg_keys[14], (2, 2, C2, C1), (4 * C1) ** -0.5, 0.5),
        "weight_up": centred(arg_keys[15], (C1, C2), C2 ** -0.5, 0.75),
    }


EPSILON = 1e-05

def quantized_values(field):
    return lax.optimization_barrier(field.astype(jnp.bfloat16)).astype(jnp.float32)

def pad_one(field):
    return jnp.pad(field, ((0, 0), (1, 1), (1, 1)))

def swish_derivative(value):
    sigma = jax.nn.sigmoid(value)
    return sigma * (1.0 + value * (1.0 - sigma))

def conv_valid(padded, weights):
    height = padded.shape[1] - 2
    width = padded.shape[2] - 2
    total = jnp.zeros((weights.shape[1], height, width), jnp.float32)
    for tap in range(9):
        row_shift = tap // 3
        col_shift = tap % 3
        window = padded[:, row_shift:row_shift + height, col_shift:col_shift + width]
        total = total + jnp.einsum('oc,chw->ohw', weights[tap].astype(jnp.float32), window)
    return total

def conv_back(padded, weights):
    height = padded.shape[1] - 2
    width = padded.shape[2] - 2
    total = jnp.zeros((weights.shape[2], height, width), jnp.float32)
    for tap in range(9):
        row_shift = tap // 3
        col_shift = tap % 3
        window = padded[:, 2 - row_shift:2 - row_shift + height, 2 - col_shift:2 - col_shift + width]
        total = total + jnp.einsum('oc,ohw->chw', weights[tap].astype(jnp.float32), window)
    return total

def reduce_resolution(fine_tensor, reduction_weight):
    channels, rows, cols = fine_tensor.shape
    blocks = fine_tensor.reshape(channels, rows // 2, 2, cols // 2, 2)
    return jnp.einsum('aboc,chawb->ohw', reduction_weight.astype(jnp.float32), blocks)

def reduce_resolution_reverse(coarse_tensor, reduction_weight):
    spread = jnp.einsum('aboc,ohw->chawb', reduction_weight.astype(jnp.float32), coarse_tensor)
    return spread.reshape(spread.shape[0], spread.shape[1] * 2, spread.shape[3] * 2)

def upsample(coarse_tensor, weight_up):
    projected = jnp.einsum('co,ohw->chw', weight_up.astype(jnp.float32), coarse_tensor)
    channels, rows, cols = projected.shape
    wide = jnp.broadcast_to(projected[:, :, None, :, None], (channels, rows, 2, cols, 2))
    return wide.reshape(channels, rows * 2, cols * 2)

def upsample_back(fine_tensor, weight_up):
    channels, rows, cols = fine_tensor.shape
    blocks = fine_tensor.reshape(channels, rows // 2, 2, cols // 2, 2)
    return jnp.einsum('co,chawb->ohw', weight_up.astype(jnp.float32), blocks)

def per_channel(values, channels):
    return jnp.repeat(values, channels // values.shape[0])[:, None, None]

def group_sums(field):
    return lax.optimization_barrier(jnp.sum(field.reshape(GROUPS, -1), axis=1))

def inner(first, second):
    return jnp.sum(first[0] * second[0]) + jnp.sum(first[1] * second[1])

def combine(first, second, factor):
    return (first[0] + factor * second[0], first[1] + factor * second[1])

def stream_forward(state, inject, first, second, gain, shift):
    pre = conv_valid(pad_one(state.astype(jnp.float32)), first)
    channels = pre.shape[0]
    count = pre.size // GROUPS
    mean = group_sums(pre) / count
    variance = group_sums(pre * pre) / count - mean * mean
    inverse = lax.rsqrt(variance + EPSILON)
    normed = (pre - per_channel(mean, channels)) * per_channel(inverse, channels)
    level = normed * gain[:, None, None] + shift[:, None, None]
    hidden = quantized_values(jax.nn.silu(level))
    mixed = conv_valid(pad_one(hidden), second) + inject.astype(jnp.float32)
    return (mixed, normed, inverse, swish_derivative(level))

def stream_adjoint(total, first, second, gain, normed, inverse, level_slope):
    channels = normed.shape[0]
    count = normed.size // GROUPS
    scaled = conv_back(pad_one(quantized_values(total)), second) * level_slope * gain[:, None, None]
    first_mean = per_channel(group_sums(scaled) / count, channels)
    second_mean = per_channel(group_sums(scaled * normed) / count, channels)
    pre_grad = per_channel(inverse, channels) * (scaled - first_mean - normed * second_mean)
    return conv_back(pad_one(quantized_values(pre_grad)), first)

def reference(fine_state, coarse_state, fine_inject, coarse_inject, fine_cotangent, coarse_cotangent, fine_first, fine_second, coarse_first, coarse_second, fine_gain, fine_shift, coarse_gain, coarse_shift, reduction_weight, weight_up):
    fine_blended, fine_normed, fine_inverse, fine_level = stream_forward(fine_state, fine_inject, fine_first, fine_second, fine_gain, fine_shift)
    coarse_blended, coarse_normed, coarse_inverse, coarse_level = stream_forward(coarse_state, coarse_inject, coarse_first, coarse_second, coarse_gain, coarse_shift)
    fine_slope = swish_derivative(fine_blended + upsample(quantized_values(coarse_blended), weight_up))
    coarse_derivative = swish_derivative(coarse_blended + reduce_resolution(quantized_values(fine_blended), reduction_weight))

    def adjoint(direction):
        fine_gradient = direction[0] * fine_slope
        coarse_gradient = direction[1] * coarse_derivative
        fine_combined = fine_gradient + reduce_resolution_reverse(quantized_values(coarse_gradient), reduction_weight)
        coarse_total = coarse_gradient + upsample_back(quantized_values(fine_gradient), weight_up)
        fine_image = stream_adjoint(fine_combined, fine_first, fine_second, fine_gain, fine_normed, fine_inverse, fine_level)
        coarse_image = stream_adjoint(coarse_total, coarse_first, coarse_second, coarse_gain, coarse_normed, coarse_inverse, coarse_level)
        return (fine_image, coarse_image)
    cotangent = (fine_cotangent, coarse_cotangent)
    solution = (jnp.zeros_like(fine_cotangent), jnp.zeros_like(coarse_cotangent))
    previous = cotangent
    update = cotangent
    lefts = []
    rights = []
    for step in range(ITERS):
        moved = update
        solution = combine(solution, moved, 1.0)
        image = adjoint(solution)
        now = combine(combine(image, cotangent, 1.0), solution, -1.0)
        if step + 1 < ITERS:
            change = combine(now, previous, -1.0)
            back = (-change[0], -change[1])
            row_term = (-moved[0], -moved[1])
            for left, right in zip(lefts, rights):
                back = combine(back, left, inner(right, change))
                row_term = combine(row_term, right, inner(moved, left))
            denominator = jnp.maximum(inner(row_term, change), 0.25 * inner(moved, moved))
            difference = combine(moved, back, -1.0)
            lefts.append((difference[0] / denominator, difference[1] / denominator))
            rights.append(row_term)
            update = now
            for left, right in zip(lefts, rights):
                update = combine(update, left, -inner(right, now))
            previous = now
    return (solution[0], solution[1])
```

```python
import functools

import jax
import jax.numpy as jnp
from jax import lax
from jax.experimental import pallas as pl
from jax.experimental.pallas import tpu as pltpu
from jax.sharding import PartitionSpec as P

GROUPS = 4
EPSILON = 1e-05
MESH = pl.DeviceIdType.MESH
F32 = jnp.float32
BF16 = jnp.bfloat16
DIRS = [(dr, dc) for dr in (-1, 0, 1) for dc in (-1, 0, 1) if dr or dc]
STATE, COT, TOTAL0, TOTAL1, IMAGE = range(5)


class Stream:
    def __init__(self, n, w, rows, cols):
        self.n, self.w, self.R, self.W = n, w, rows, cols
        self.gs = w // GROUPS
        self.main = (rows + 2) * cols
        self.NL = self.main + 128
        self.cells = rows * cols
        self.own = slice(2 * cols, 2 * cols + rows * cols)


def dot(a, b):
    return jnp.dot(a, b, preferred_element_type=F32)


def lanes_of(shape):
    return lax.broadcasted_iota(jnp.int32, shape, len(shape) - 1)


def subs_of(shape):
    return lax.broadcasted_iota(jnp.int32, shape, 0)


def roll(x, shift):
    return pltpu.roll(x, shift % x.shape[1], 1)


def wide_lanes(x, width):
    return x if width == 128 else jnp.concatenate([x] * (width // 128), axis=1)


def fold(x):
    return jnp.sum(x.reshape(x.shape[0] // 8, 8, x.shape[1]), axis=0)


def block(i, size):
    return pl.ds(pl.multiple_of(i * size, 128), size)


def swish_derivative(v):
    sigma = jax.nn.sigmoid(v)
    return sigma * (1.0 + v * (1.0 - sigma))


def to_row(accs):
    row = jnp.zeros((1, 128), F32)
    sub, lane = subs_of((8, 128)), lanes_of((8, 128))
    for first in range(0, len(accs), 8):
        stack = jnp.zeros((8, 128), F32)
        for k, acc in enumerate(accs[first : first + 8]):
            stack = jnp.where(sub == k, jnp.sum(acc, axis=0, keepdims=True), stack)
        col = jnp.sum(stack, axis=1, keepdims=True)
        row = row + jnp.sum(jnp.where(lane == sub + first, col, 0.0), axis=0, keepdims=True)
    return row


def pick(row, k):
    return jnp.sum(jnp.where(lanes_of((1, 128)) == k, row, 0.0), axis=1, keepdims=True)


def put_rows(s, rows, xm, pk):
    lane = lanes_of((s.n, 128))
    packed = jnp.zeros((s.n, 128), F32)
    for r, x in enumerate(rows):
        xm[:, (r + 2) * s.W : (r + 3) * s.W] = x.astype(BF16)
        x = x.astype(F32)
        edge = jnp.where(lane < 2, x[:, :128], jnp.where(lane >= 126, x[:, s.W - 128 :], 0.0))
        packed = packed + roll(edge, 8 * (r + 2) + 2)
    pk[...] = jnp.where(lane % 8 <= 2, packed, roll(packed, 2)).astype(BF16)


def edge_of(s, pk, pr):
    lane = lanes_of((s.n, 128))
    q = lane % 8

    def across(left, mid, right):
        return jnp.where(q <= 1, left, jnp.where(q <= 3, mid, right))

    own = (lane >= 16) & (lane < 16 + 8 * s.R)
    if pr is None:
        return jnp.where(own & (q >= 2) & (q <= 3), pk[...].astype(F32), 0.0)
    got = {d: pr[k].astype(F32) for k, d in enumerate(DIRS)}
    mid = across(got[0, -1], pk[...].astype(F32), got[0, 1])
    top = across(got[-1, -1], got[-1, 0], got[-1, 1])
    bottom = across(got[1, -1], got[1, 0], got[1, 1])
    return jnp.where(own, mid, jnp.where(lane < 16, roll(top, -8 * s.R), roll(bottom, 8 * s.R)))


def build(s, xm, edge, x3, x9, ring):
    n, W = s.n, s.W
    lane = lanes_of((n, 128))
    joined = jnp.where(lane % 8 == 0, roll(edge, -4), edge)
    lane = lanes_of((n, W))
    for k in range(s.R + 4):
        at = slice(k * W, (k + 1) * W)
        if not ring and not 2 <= k < s.R + 2:
            x3[:, at] = jnp.zeros((3 * n, W), BF16)
            continue
        x = xm[:, at]
        xf = x.astype(F32)
        t = wide_lanes(roll(joined, -(8 * k + 1)), W)
        x3[0:n, at] = jnp.where(lane == 0, t, roll(xf, 1)).astype(BF16)
        x3[n : 2 * n, at] = x
        x3[2 * n : 3 * n, at] = jnp.where(lane == W - 1, t, roll(xf, -1)).astype(BF16)
    for i in range(3):
        for j in range(3):
            x9[i, j * n : (j + 1) * n, :] = roll(edge, -(8 * i + j)).astype(BF16)


def widen(s, weights, x3, x9, out, inside=False):
    skip = s.W if inside else 0

    def step(b, _):
        total = dot(weights[0], x3[:, pl.ds(pl.multiple_of(b * 256 + skip, 128), 256)])
        for i in (1, 2):
            total = total + dot(weights[i], x3[:, pl.ds(pl.multiple_of(b * 256 + skip + i * s.W, 128), 256)])
        out[:, block(b, 256)] = total
        return 0

    lax.fori_loop(0, (s.cells if inside else s.main) // 256, step, 0)
    if not inside:
        out[:, s.main :] = dot(weights[0], x9[0]) + dot(weights[1], x9[1]) + dot(weights[2], x9[2])


def narrow(s, weights, h, z):
    n, W = s.n, s.W

    def step(b, _):
        total = dot(weights[0], h[:, block(b, 256)])
        for i in (1, 2):
            total = total + dot(weights[i], h[:, pl.ds(pl.multiple_of(b * 256 + i * W, 128), 256)])
        z[:, block(b, 256)] = total
        return 0

    lax.fori_loop(0, s.cells // 256, step, 0)
    edges = [dot(weights[i], h[:, s.main :]) for i in range(3)]
    total = edges[0] + roll(edges[1], -8) + roll(edges[2], -16)
    q = lanes_of((n, 128)) % 8
    joined = jnp.where(q == 1, roll(total[:n], 1), roll(total[2 * n :], -3))
    lane = lanes_of((n, W))

    def row(r):
        at = slice(r * W, (r + 1) * W)
        t = wide_lanes(roll(joined, -(8 * r + 1)), W)
        left = jnp.where(lane == 0, t, roll(z[0:n, at], 1))
        right = jnp.where(lane == W - 1, t, roll(z[2 * n : 3 * n, at], -1))
        return left + z[n : 2 * n, at] + right

    return row


def kernel(streams, sizes, *refs):
    f, c = streams
    (
        fine_state, coarse_state, fine_inject, coarse_inject, fine_cot, coarse_cot,
        fine_first, fine_second, coarse_first, coarse_second,
        fine_gain, fine_shift, coarse_gain, coarse_shift, reduction, up,
        fine_out, coarse_out,
        *rest,
    ) = refs
    (xm_f, xm_c, pk_f, pk_c, pr_f, pr_c, x3_f, x3_c, x9_f, x9_c,
     nm_f, nm_c, ls_f, ls_c, hg_f, hg_c, hb_f, hb_c, kc_f, kc_c, kp_f, kp_c,
     z_f, z_c, sl_f, sl_c, e_f, e_c, mk_f, mk_c, ga_f, ga_c, sh_f, sh_c,
     a1_f, a1_c, a3_f, a3_c, a4_f, a4_c, dup, split, rt, rw, u4, stack_f, stack_c, taps,
     ar_a, ar_b, halo_send, halo_recv, ar_send, ar_recv) = rest
    xm, pk, pr, x3, x9 = (xm_f, xm_c), (pk_f, pk_c), (pr_f, pr_c), (x3_f, x3_c), (x9_f, x9_c)
    nm, ls, hg, hb = (nm_f, nm_c), (ls_f, ls_c), (hg_f, hg_c), (hb_f, hb_c)
    kc, kp, zs, sl, es, mk = (kc_f, kc_c), (kp_f, kp_c), (z_f, z_c), (sl_f, sl_c), (e_f, e_c), (mk_f, mk_c)
    ga, sh, a1, a3, a4 = (ga_f, ga_c), (sh_f, sh_c), (a1_f, a1_c), (a3_f, a3_c), (a4_f, a4_c)
    first, second = (fine_first, coarse_first), (fine_second, coarse_second)
    cot, state = (fine_cot, coarse_cot), (fine_state, coarse_state)
    inject, outs = (fine_inject, coarse_inject), (fine_out, coarse_out)
    rows, cols, low_rows, low_cols = sizes
    high_rows, high_cols = rows // low_rows, cols // low_cols
    row, col = lax.axis_index("row"), lax.axis_index("col")
    both = (0, 1)

    def has(d):
        return (row + d[0] >= 0) & (row + d[0] < rows) & (col + d[1] >= 0) & (col + d[1] < cols)

    size_a, size_b = low_rows * high_cols, high_rows * low_cols
    me_a = (row % low_rows) * high_cols + col // low_cols
    me_b = (row // low_rows) * low_cols + col % low_cols

    def peer_a(k):
        p = (me_a + k) % size_a
        return ((row // low_rows) * low_rows + p // high_cols, (p % high_cols) * low_cols + col % low_cols)

    def peer_b(k):
        p = (me_b + k) % size_b
        return ((p // low_cols) * low_rows + row % low_rows, (col // low_cols) * low_cols + p % low_cols)

    def exchange_copies(s, k):
        W, R = streams[s].W, streams[s].R
        field = 2 * k + s
        made = []
        for i, d in enumerate(DIRS):
            back = DIRS.index((-d[0], -d[1]))
            made.append((pltpu.make_async_remote_copy(
                src_ref=pk[s].at[k], dst_ref=pr[s].at[k, back],
                send_sem=halo_send.at[field, i], recv_sem=halo_recv.at[field, back],
                device_id=(row + d[0], col + d[1]), device_id_type=MESH), d))
        for i, d, src, dst in ((8, (-1, 0), 2 * W, (R + 2) * W), (9, (1, 0), R * W, 0)):
            made.append((pltpu.make_async_remote_copy(
                src_ref=xm[s].at[k, :, pl.ds(src, 2 * W)], dst_ref=xm[s].at[k, :, pl.ds(dst, 2 * W)],
                send_sem=halo_send.at[field, i], recv_sem=halo_recv.at[field, i],
                device_id=(row + d[0], col), device_id_type=MESH), d))
        return made

    def exchange_start(s, k):
        for copy, d in exchange_copies(s, k):
            pl.when(has(d))(copy.start)

    def exchange_wait(s, k):
        W, R = streams[s].W, streams[s].R
        field = 2 * k + s
        for i, d in enumerate(DIRS):
            pl.when(has(d))(pltpu.make_async_copy(pk[s].at[k], pr[s].at[k, i], halo_recv.at[field, i]).wait)
        for i, d, dst in ((8, (1, 0), (R + 2) * W), (9, (-1, 0), 0)):
            ref = xm[s].at[k, :, pl.ds(dst, 2 * W)]
            pl.when(has(d))(pltpu.make_async_copy(ref, ref, halo_recv.at[field, i]).wait)

    def exchange_end(s, k):
        for copy, d in exchange_copies(s, k):
            pl.when(has(d))(copy.wait_send)

    def spread(k, stage, buf, me, size, peer):
        def send(p, _):
            pltpu.make_async_remote_copy(
                src_ref=buf.at[k, me], dst_ref=buf.at[k, me],
                send_sem=ar_send.at[k, stage], recv_sem=ar_recv.at[k, stage],
                device_id=peer(p), device_id_type=MESH).start()
            return 0

        lax.fori_loop(1, size, send, 0)

    def collect(k, stage, buf, size):
        ref = buf.at[k, pl.ds(0, size - 1)]
        pltpu.make_async_copy(ref, ref, ar_recv.at[k, stage]).wait()
        return jnp.sum(buf[k], axis=0)

    def reduce_start(k, value):
        ar_a[k, me_a] = value
        spread(k, 0, ar_a, me_a, size_a, peer_a)

    def reduce_middle(k):
        ar_b[k, me_b] = collect(k, 0, ar_a, size_a)
        spread(k, 1, ar_b, me_b, size_b, peer_b)

    def reduce_end(k):
        return collect(k, 1, ar_b, size_b)

    def reduce_drain(k):
        for stage, buf, size in ((0, ar_a, size_a), (1, ar_b, size_b)):
            ref = buf.at[k, pl.ds(0, size - 1)]
            pltpu.make_async_copy(ref, ref, ar_send.at[k, stage]).wait()

    for s in both:
        W, R = streams[s].W, streams[s].R
        for k in range(5):
            pr[s][k] = jnp.zeros(pr[s].shape[1:], BF16)
            xm[s][k, :, 0 : 2 * W] = jnp.zeros((streams[s].n, 2 * W), BF16)
            xm[s][k, :, (R + 2) * W : (R + 4) * W] = jnp.zeros((streams[s].n, 2 * W), BF16)
    barrier = pltpu.get_barrier_semaphore()

    def greet(device):
        pl.semaphore_signal(barrier, inc=1, device_id=device, device_id_type=MESH)

    for d in DIRS:
        pl.when(has(d))(functools.partial(greet, (row + d[0], col + d[1])))

    def greet_a(k, _):
        greet(peer_a(k))
        return 0

    def greet_b(k, _):
        greet(peer_b(k))
        return 0

    lax.fori_loop(1, size_a, greet_a, 0)
    lax.fori_loop(1, size_b, greet_b, 0)
    for s in both:
        put_rows(streams[s], [state[s][:, r, :].astype(F32) for r in range(streams[s].R)], xm[s].at[STATE], pk[s].at[STATE])
    beside = sum(has(d).astype(jnp.int32) for d in DIRS)
    pl.semaphore_wait(barrier, beside + (size_a + size_b - 2))
    for s in both:
        exchange_start(s, STATE)
    for s in both:
        put_rows(streams[s], [cot[s][:, r, :] for r in range(streams[s].R)], xm[s].at[COT], pk[s].at[COT])
    for s in both:
        exchange_start(s, COT)

    for s in both:
        n, w, W = streams[s].n, streams[s].w, streams[s].W
        for i in range(3):
            flipped = []
            for j in range(3):
                tap = first[s][3 * i + j].T
                taps[j * n : (j + 1) * n, 0:w] = tap
                a4[s][2 - i, (2 - j) * n : (3 - j) * n, :] = tap
            a1[s][i] = taps[0 : 3 * n, 0:w].T
            for j in range(3):
                t = 8 - (3 * i + j)
                taps[j * n : (j + 1) * n, 0:w] = second[s][t // 3, (t % 3) * n : (t % 3 + 1) * n, :]
            a3[s][i] = taps[0 : 3 * n, 0:w].T
        same = subs_of((w, w)) == lanes_of((w, w))
        for src, dst in (((fine_gain, coarse_gain)[s], ga[s]), ((fine_shift, coarse_shift)[s], sh[s])):
            dst[...] = jnp.broadcast_to(jnp.sum(jnp.where(same, src[...], 0.0), axis=1, keepdims=True), (w, 128))
        R = streams[s].R
        mk[s][...] = jnp.ones((1, streams[s].NL), F32)
        mk[s][:, 0:W] = jnp.where(row > 0, 1.0, 0.0) * jnp.ones((1, W), F32)
        mk[s][:, (R + 1) * W : (R + 2) * W] = jnp.where(row < rows - 1, 1.0, 0.0) * jnp.ones((1, W), F32)
        lane = lanes_of((1, 128))
        q, line = lane % 8, lane // 8
        good = ((q == 0) & (col > 0)) | ((q == 3) & (col < cols - 1))
        good = good & (line < R + 2) & ((line > 0) | (row > 0)) & ((line < R + 1) | (row < rows - 1))
        mk[s][:, streams[s].main :] = jnp.where(good, 1.0, 0.0)
    here, there = subs_of((128, 256)), lanes_of((128, 256))
    dup[...] = jnp.where(there // 2 == here, 1.0, 0.0).astype(BF16)
    here, there = subs_of((256, 256)), lanes_of((256, 256))
    split[...] = jnp.where(here == 2 * (there % 128) + there // 128, 1.0, 0.0).astype(BF16)
    for a in range(2):
        for b in range(2):
            at = slice((2 * a + b) * f.n, (2 * a + b + 1) * f.n)
            rt[at, :] = reduction[a, b].T
            taps[at, 0 : c.n] = up[...]
    rw[...] = rt[...].T
    u4[...] = taps[0 : 4 * f.n, 0 : c.n].T

    def load(s, k, ring=True):
        st = streams[s]
        edge = edge_of(st, pk[s].at[k], pr[s].at[k] if ring else None)
        build(st, xm[s].at[k], edge, x3[s], x9[s], ring)

    def group_loop(s, start, chunks, count, body):
        gs = streams[s].gs
        sums = []
        for g in range(GROUPS):
            at = slice(g * gs, (g + 1) * gs)

            def step(k, accs):
                return tuple(a + fold(t) for a, t in zip(accs, body(g, at, k + start)))

            sums.append(lax.fori_loop(0, chunks, step, (jnp.zeros((8, 128), F32),) * count))
        return [[sums[g][t] for g in range(GROUPS)] for t in range(count)]

    def ring_chunks(s):
        return 0, streams[s].NL // 128

    def own_chunks(s):
        return streams[s].W // 128, streams[s].cells // 128

    def flat(per_stream, t):
        return [a for s in both for a in per_stream[s][t]]

    sums = []
    for s in both:
        exchange_wait(s, STATE)
        load(s, STATE)
        widen(streams[s], a1[s], x3[s], x9[s], nm[s])

        def squares(g, at, k):
            x = nm[s][at, block(k, 128)]
            return x, x * x

        sums.append(group_loop(s, *own_chunks(s), 2, squares))
    reduce_start(0, to_row(flat(sums, 0) + flat(sums, 1)))
    for s in both:
        exchange_wait(s, COT)
        load(s, COT)
        widen(streams[s], a1[s], x3[s], x9[s], kc[s], inside=True)
    reduce_middle(0)
    stats = reduce_end(0)

    lane = lanes_of((1, 128))
    counts = [rows * cols * streams[s].cells * streams[s].gs for s in both]
    per = jnp.where(lane % 8 < GROUPS, 1.0 / counts[0], 1.0 / counts[1])
    mean_row = stats * per
    variance = roll(mean_row, -8) - mean_row * mean_row
    inverse_row = jnp.where(lane < 8, lax.rsqrt(variance + EPSILON), 0.0)
    means = [[pick(mean_row, s * GROUPS + g) for g in range(GROUPS)] for s in both]
    inverses = [[pick(inverse_row, s * GROUPS + g) for g in range(GROUPS)] for s in both]

    for s in both:
        gs = streams[s].gs
        for g in range(GROUPS):
            at = slice(g * gs, (g + 1) * gs)

            def activate(k, _):
                here = block(k, 128)
                gain, keep = ga[s][at, :], mk[s][:, here]
                normed = (nm[s][at, here] - means[s][g]) * inverses[s][g]
                level = normed * gain + sh[s][at, :]
                sigma = jax.nn.sigmoid(level)
                nm[s][at, here] = normed
                hb[s][at, here] = (level * sigma * keep).astype(BF16)
                ls[s][at, here] = sigma * (1.0 + level * (1.0 - sigma)) * gain * keep
                return 0

            lax.fori_loop(0, streams[s].NL // 128, activate, 0)

    def own_row(s, ref, r):
        return ref[:, r * streams[s].W : (r + 1) * streams[s].W]

    def halve():
        parts = dot(stack_f[...], split[...]).astype(BF16)
        lined = []
        for R in range(c.R):
            lined.append(jnp.concatenate([
                parts[(2 * R + a) * f.n : (2 * R + a + 1) * f.n, b * 128 : (b + 1) * 128]
                for a in range(2) for b in range(2)], axis=0))
        return jnp.concatenate(lined, axis=1)

    def double():
        return dot(stack_c[...], dup[...]).astype(BF16)

    for s, stack in ((0, stack_f), (1, stack_c)):
        n = streams[s].n
        got = narrow(streams[s], second[s], hb[s], zs[s])
        for r in range(streams[s].R):
            mixed = got(r) + inject[s][:, r, :].astype(F32)
            sl[s][:, r * streams[s].W : (r + 1) * streams[s].W] = mixed
            stack[r * n : (r + 1) * n, :] = mixed.astype(BF16)
    down = dot(rw[...], halve())
    wide = double()
    for R in range(c.R):
        lifted = dot(up[...], wide[R * c.n : (R + 1) * c.n, :])
        for r in (2 * R, 2 * R + 1):
            at = slice(r * f.W, (r + 1) * f.W)
            sl_f[:, at] = swish_derivative(sl_f[:, at] + lifted)
    sl_c[...] = swish_derivative(sl_c[...] + down)

    def total(field, k):
        for r in range(f.R):
            stack_f[r * f.n : (r + 1) * f.n, :] = (field(0, r) * own_row(0, sl_f, r)).astype(BF16)
        coarse_grads = [field(1, r) * own_row(1, sl_c, r) for r in range(c.R)]
        for r in range(c.R):
            stack_c[r * c.n : (r + 1) * c.n, :] = coarse_grads[r].astype(BF16)
        raised = dot(u4[...], halve())
        put_rows(c, [coarse_grads[r] + own_row(1, raised, r) for r in range(c.R)], xm_c.at[k], pk_c.at[k])
        wide = double()
        even = lanes_of((f.n, f.W)) % 2 == 0
        fine = []
        for R in range(c.R):
            spread_out = dot(rt[...], wide[R * c.n : (R + 1) * c.n, :])
            for a in range(2):
                part = [spread_out[(2 * a + b) * f.n : (2 * a + b + 1) * f.n] for b in range(2)]
                r = 2 * R + a
                fine.append(field(0, r) * own_row(0, sl_f, r) + jnp.where(even, part[0], part[1]))
        put_rows(f, fine, xm_f.at[k], pk_f.at[k])
        for s in both:
            exchange_start(s, k)

    total(lambda s, r: cot[s][:, r, :], TOTAL0)

    sums = []
    for s in both:
        load(s, TOTAL0, ring=False)
        widen(streams[s], a3[s], x3[s], x9[s], hg[s])

        def pushed(g, at, k):
            scaled = hg[s][at, block(k, 128)] * ls[s][at, block(k, 128)]
            return scaled, scaled * nm[s][at, block(k, 128)]

        sums.append(group_loop(s, *ring_chunks(s), 2, pushed))
    reduce_start(1, to_row(flat(sums, 0) + flat(sums, 1)))

    def scale(s, k):
        exchange_wait(s, k)
        load(s, k)
        widen(streams[s], a3[s], x3[s], x9[s], hg[s])

    for s in both:
        scale(s, TOTAL0)
    reduce_middle(1)
    along = []
    for s in both:

        def cot_sums(g, at, k):
            x = kc[s][at, block(k - streams[s].W // 128, 128)]
            return x, x * nm[s][at, block(k, 128)]

        along.append(group_loop(s, *own_chunks(s), 2, cot_sums))
    found = reduce_end(1)

    def image(row_sums):
        scaled_mean = row_sums * per
        got = []
        for s in both:
            gs = streams[s].gs
            for g in range(GROUPS):
                at = slice(g * gs, (g + 1) * gs)
                one, two = pick(scaled_mean, s * GROUPS + g), pick(scaled_mean, 8 + s * GROUPS + g)

                def centre(k, _):
                    here = block(k, 128)
                    scaled = hg[s][at, here] * ls[s][at, here]
                    grad = inverses[s][g] * (scaled - one - nm[s][at, here] * two)
                    hb[s][at, here] = (grad * mk[s][:, here]).astype(BF16)
                    return 0

                lax.fori_loop(0, streams[s].NL // 128, centre, 0)
            got.append(narrow(streams[s], a4[s], hb[s], zs[s]))
        return got

    got = image(found)
    for s in both:
        made = [got[s](r) for r in range(streams[s].R)]
        for r in range(streams[s].R):
            es[s][:, r * streams[s].W : (r + 1) * streams[s].W] = made[r]
        put_rows(streams[s], made, xm[s].at[IMAGE], pk[s].at[IMAGE])
        exchange_start(s, IMAGE)
    total(lambda s, r: own_row(s, es[s], r), TOTAL1)

    gram = [jnp.zeros((8, 128), F32) for _ in range(3)]
    for s in both:
        for r in range(streams[s].R):
            a, b = cot[s][:, r, :], own_row(s, es[s], r)
            for t, product in enumerate((a * a, a * b, b * b)):
                product = fold(product)
                for half in range(streams[s].W // 128):
                    gram[t] = gram[t] + product[:, half * 128 : (half + 1) * 128]
    sums = []
    crossed = [jnp.zeros((8, 128), F32) for _ in range(2)]
    for s in both:
        exchange_wait(s, IMAGE)
        load(s, IMAGE)
        widen(streams[s], a1[s], x3[s], x9[s], kp[s], inside=True)
    for s in both:
        scale(s, TOTAL1)

        def all_sums(g, at, k):
            here, inner = block(k, 128), block(k - streams[s].W // 128, 128)
            normed, lifted = nm[s][at, here], kp[s][at, inner]
            scaled = hg[s][at, here] * ls[s][at, here]
            return scaled, scaled * normed, lifted, lifted * normed, scaled * kc[s][at, inner], scaled * lifted

        sums.append(group_loop(s, *own_chunks(s), 6, all_sums))
        for g in range(GROUPS):
            for t in range(2):
                crossed[t] = crossed[t] + sums[s][4 + t][g] * inverses[s][g]
    entries = flat(sums, 0) + flat(sums, 1) + flat(along, 0) + flat(along, 1) + flat(sums, 2) + flat(sums, 3)
    reduce_start(2, to_row(entries + gram + crossed))
    reduce_middle(2)
    found = reduce_end(2)

    weight = (inverse_row + roll(inverse_row, 8)) * per
    cc, c0, g00, cq, pq = [pick(found, 48 + k) for k in range(5)]
    c1 = cq - jnp.sum(found * weight * roll(found, -16), axis=1, keepdims=True)
    g01 = pq - jnp.sum(found * weight * roll(found, -32), axis=1, keepdims=True)
    d0 = jnp.maximum(cc - c0, 0.25 * cc)
    alpha = 1.0 + c0 / d0
    kappa = alpha * g00 / d0
    turn = -alpha * (c1 - c0)
    d1 = jnp.maximum(-alpha * alpha * (g01 - g00) - kappa * alpha * (c1 - c0), 0.25 * alpha * alpha * g00)
    m0 = -((1.0 - alpha) * c0 + alpha * c1)
    m1 = -alpha * ((1.0 - alpha) * g00 + alpha * g01) + kappa * m0
    by0 = 1.0 - m0 / d0 + (m1 / d1) * (turn / d0)
    by1 = alpha * (1.0 - m1 / d1)

    got = image(found)
    for s in both:
        for r in range(streams[s].R):
            outs[s][:, r, :] = cot[s][:, r, :] + by0 * own_row(s, es[s], r) + by1 * got[s](r)

    for s in both:
        for k in range(5):
            exchange_end(s, k)
    for k in range(3):
        reduce_drain(k)


def solution(mesh):
    rows, cols = mesh.shape["row"], mesh.shape["col"]
    sizes = (rows, cols, min(rows, 8), min(cols, 4))

    def body(*args):
        fine_state, coarse_state = args[:2]
        fine_first, fine_second, coarse_first, coarse_second = args[6:10]
        f = Stream(fine_state.shape[0], fine_first.shape[1], *fine_state.shape[1:])
        c = Stream(coarse_state.shape[0], coarse_first.shape[1], *coarse_state.shape[1:])
        both = (f, c)
        args = list(args)
        for k, s in ((7, f), (9, c)):
            args[k] = args[k].reshape(3, 3 * s.n, s.w)
        for k in range(10, 14):
            args[k] = args[k].reshape(1, -1)
        vmem = pltpu.VMEM
        scratch = []
        for shape, dtype in (
            (lambda s: (5, s.n, (s.R + 4) * s.W), BF16),
            (lambda s: (5, s.n, 128), BF16),
            (lambda s: (5, 8, s.n, 128), BF16),
            (lambda s: (3 * s.n, (s.R + 4) * s.W), BF16),
            (lambda s: (3, 3 * s.n, 128), BF16),
            (lambda s: (s.w, s.NL), F32),
            (lambda s: (s.w, s.NL), F32),
            (lambda s: (s.w, s.NL), F32),
            (lambda s: (s.w, s.NL), BF16),
            (lambda s: (s.w, s.cells), F32),
            (lambda s: (s.w, s.cells), F32),
            (lambda s: (3 * s.n, s.cells), F32),
            (lambda s: (s.n, s.cells), F32),
            (lambda s: (s.n, s.cells), F32),
            (lambda s: (1, s.NL), F32),
            (lambda s: (s.w, 128), F32),
            (lambda s: (s.w, 128), F32),
            (lambda s: (3, s.w, 3 * s.n), BF16),
            (lambda s: (3, s.w, 3 * s.n), BF16),
            (lambda s: (3, 3 * s.n, s.w), BF16),
        ):
            scratch += [vmem(shape(s), dtype) for s in both]
        scratch += [
            vmem((128, 256), BF16),
            vmem((256, 256), BF16),
            vmem((4 * f.n, c.n), BF16),
            vmem((c.n, 4 * f.n), BF16),
            vmem((c.n, 4 * f.n), BF16),
            vmem((f.R * f.n, f.W), BF16),
            vmem((c.R * c.n, c.W), BF16),
            vmem((3 * c.n, c.w), BF16),
            vmem((3, sizes[2] * (cols // sizes[3]), 1, 128), F32),
            vmem((3, (rows // sizes[2]) * sizes[3], 1, 128), F32),
            pltpu.SemaphoreType.DMA((10, 10)),
            pltpu.SemaphoreType.DMA((10, 10)),
            pltpu.SemaphoreType.DMA((3, 2)),
            pltpu.SemaphoreType.DMA((3, 2)),
        ]
        return pl.pallas_call(
            functools.partial(kernel, both, sizes),
            out_shape=[jax.ShapeDtypeStruct(a.shape, F32) for a in args[4:6]],
            in_specs=[pl.BlockSpec(memory_space=pltpu.VMEM)] * 16,
            out_specs=[pl.BlockSpec(memory_space=pltpu.VMEM)] * 2,
            scratch_shapes=scratch,
            compiler_params=pltpu.CompilerParams(
                collective_id=0, has_side_effects=True, vmem_limit_bytes=56 * 1024 * 1024
            ),
        )(*args)

    field = P(None, "row", "col")
    return jax.shard_map(
        body,
        mesh=mesh,
        in_specs=(field,) * 6 + (P(),) * 10,
        out_specs=(field, field),
        check_vma=False,
    )
```

```python
import functools

import jax
import jax.numpy as jnp
from jax import lax
from jax.experimental import pallas as pl
from jax.experimental.pallas import tpu as pltpu
from jax.sharding import PartitionSpec as P

GROUPS = 4
EPSILON = 1e-05
MESH = pl.DeviceIdType.MESH
F32 = jnp.float32
BF16 = jnp.bfloat16
DIRS = [(dr, dc) for dr in (-1, 0, 1) for dc in (-1, 0, 1) if dr or dc]
STATE, COT, TOTAL0, TOTAL1, IMAGE = range(5)


class Stream:
    def __init__(self, n, w, rows, cols):
        self.n, self.w, self.R, self.W = n, w, rows, cols
        self.gs = w // GROUPS
        self.main = (rows + 2) * cols
        self.NL = self.main + 128
        self.cells = rows * cols
        self.own = slice(2 * cols, 2 * cols + rows * cols)


def dot(a, b):
    return jnp.dot(a, b, preferred_element_type=F32)


def lanes_of(shape):
    return lax.broadcasted_iota(jnp.int32, shape, len(shape) - 1)


def subs_of(shape):
    return lax.broadcasted_iota(jnp.int32, shape, 0)


def roll(x, shift):
    return pltpu.roll(x, shift % x.shape[1], 1)


def wide_lanes(x, width):
    return x if width == 128 else jnp.concatenate([x] * (width // 128), axis=1)


def fold(x):
    return jnp.sum(x.reshape(x.shape[0] // 8, 8, x.shape[1]), axis=0)


def block(i, size):
    return slice(i * size, (i + 1) * size)


def swish_derivative(v):
    sigma = jax.nn.sigmoid(v)
    return sigma * (1.0 + v * (1.0 - sigma))


def to_row(accs):
    row = jnp.zeros((1, 128), F32)
    sub, lane = subs_of((8, 128)), lanes_of((8, 128))
    for first in range(0, len(accs), 8):
        stack = jnp.zeros((8, 128), F32)
        for k, acc in enumerate(accs[first : first + 8]):
            stack = jnp.where(sub == k, jnp.sum(acc, axis=0, keepdims=True), stack)
        col = jnp.sum(stack, axis=1, keepdims=True)
        row = row + jnp.sum(jnp.where(lane == sub + first, col, 0.0), axis=0, keepdims=True)
    return row


def pick(row, k):
    return jnp.sum(jnp.where(lanes_of((1, 128)) == k, row, 0.0), axis=1, keepdims=True)


def put_rows(s, rows, xm, pk):
    lane = lanes_of((s.n, 128))
    packed = jnp.zeros((s.n, 128), F32)
    for r, x in enumerate(rows):
        xm[:, (r + 2) * s.W : (r + 3) * s.W] = x.astype(BF16)
        x = x.astype(F32)
        edge = jnp.where(lane < 2, x[:, :128], jnp.where(lane >= 126, x[:, s.W - 128 :], 0.0))
        packed = packed + roll(edge, 8 * (r + 2) + 2)
    pk[...] = jnp.where(lane % 8 <= 2, packed, roll(packed, 2)).astype(BF16)


def edge_of(s, pk, pr):
    lane = lanes_of((s.n, 128))
    q = lane % 8

    def across(left, mid, right):
        return jnp.where(q <= 1, left, jnp.where(q <= 3, mid, right))

    own = (lane >= 16) & (lane < 16 + 8 * s.R)
    if pr is None:
        return jnp.where(own & (q >= 2) & (q <= 3), pk[...].astype(F32), 0.0)
    got = {d: pr[k].astype(F32) for k, d in enumerate(DIRS)}
    mid = across(got[0, -1], pk[...].astype(F32), got[0, 1])
    top = across(got[-1, -1], got[-1, 0], got[-1, 1])
    bottom = across(got[1, -1], got[1, 0], got[1, 1])
    return jnp.where(own, mid, jnp.where(lane < 16, roll(top, -8 * s.R), roll(bottom, 8 * s.R)))


def build(s, xm, edge, x3, x9, ring):
    n, W = s.n, s.W
    lane = lanes_of((n, 128))
    joined = jnp.where(lane % 8 == 0, roll(edge, -4), edge)
    lane = lanes_of((n, W))
    for k in range(s.R + 4):
        at = slice(k * W, (k + 1) * W)
        if not ring and not 2 <= k < s.R + 2:
            x3[:, at] = jnp.zeros((3 * n, W), BF16)
            continue
        x = xm[:, at]
        xf = x.astype(F32)
        t = wide_lanes(roll(joined, -(8 * k + 1)), W)
        x3[0:n, at] = jnp.where(lane == 0, t, roll(xf, 1)).astype(BF16)
        x3[n : 2 * n, at] = x
        x3[2 * n : 3 * n, at] = jnp.where(lane == W - 1, t, roll(xf, -1)).astype(BF16)
    for i in range(3):
        for j in range(3):
            x9[i, j * n : (j + 1) * n, :] = roll(edge, -(8 * i + j)).astype(BF16)


def widen(s, weights, x3, x9, out, inside=False):
    start, size = (s.W, s.cells) if inside else (0, s.main)
    taps = [x3[:, start + i * s.W : start + i * s.W + size] for i in range(3)]
    out[:, 0:size] = dot(weights[...], jnp.concatenate(taps, axis=0))
    if not inside:
        out[:, s.main :] = dot(weights[...], jnp.concatenate([x9[i] for i in range(3)], axis=0))


def narrow(s, weights, h, z):
    n, W = s.n, s.W

    for b in range(0, s.cells, 256):
        total = dot(weights[0], h[:, b : b + 256])
        for i in (1, 2):
            total = total + dot(weights[i], h[:, b + i * W : b + i * W + 256])
        z[:, b : b + 256] = total
    edges = [dot(weights[i], h[:, s.main :]) for i in range(3)]
    total = edges[0] + roll(edges[1], -8) + roll(edges[2], -16)
    q = lanes_of((n, 128)) % 8
    joined = jnp.where(q == 1, roll(total[:n], 1), roll(total[2 * n :], -3))
    lane = lanes_of((n, W))

    def row(r):
        at = slice(r * W, (r + 1) * W)
        t = wide_lanes(roll(joined, -(8 * r + 1)), W)
        left = jnp.where(lane == 0, t, roll(z[0:n, at], 1))
        right = jnp.where(lane == W - 1, t, roll(z[2 * n : 3 * n, at], -1))
        return left + z[n : 2 * n, at] + right

    return row


def kernel(streams, sizes, *refs):
    f, c = streams
    (
        fine_state, coarse_state, fine_inject, coarse_inject, fine_cot, coarse_cot,
        fine_first, fine_second, coarse_first, coarse_second,
        fine_gain, fine_shift, coarse_gain, coarse_shift, reduction, up,
        fine_out, coarse_out,
        *rest,
    ) = refs
    (xm_f, xm_c, pk_f, pk_c, pr_f, pr_c, x3_f, x3_c, x9_f, x9_c,
     nm_f, nm_c, ls_f, ls_c, hg_f, hg_c, hb_f, hb_c, kc_f, kc_c, kp_f, kp_c,
     z_f, z_c, sl_f, sl_c, e_f, e_c, mk_f, mk_c, ga_f, ga_c, sh_f, sh_c,
     a1_f, a1_c, a3_f, a3_c, a4_f, a4_c, dup, split, rt, rw, u4, stack_f, stack_c, taps,
     ar_a, ar_b, halo_send, halo_recv, ar_send, ar_recv) = rest
    xm, pk, pr, x3, x9 = (xm_f, xm_c), (pk_f, pk_c), (pr_f, pr_c), (x3_f, x3_c), (x9_f, x9_c)
    nm, ls, hg, hb = (nm_f, nm_c), (ls_f, ls_c), (hg_f, hg_c), (hb_f, hb_c)
    kc, kp, zs, sl, es, mk = (kc_f, kc_c), (kp_f, kp_c), (z_f, z_c), (sl_f, sl_c), (e_f, e_c), (mk_f, mk_c)
    ga, sh, a1, a3, a4 = (ga_f, ga_c), (sh_f, sh_c), (a1_f, a1_c), (a3_f, a3_c), (a4_f, a4_c)
    first, second = (fine_first, coarse_first), (fine_second, coarse_second)
    cot, state = (fine_cot, coarse_cot), (fine_state, coarse_state)
    inject, outs = (fine_inject, coarse_inject), (fine_out, coarse_out)
    rows, cols, low_rows, low_cols = sizes
    high_rows, high_cols = rows // low_rows, cols // low_cols
    row, col = lax.axis_index("row"), lax.axis_index("col")
    both = (0, 1)

    def has(d):
        return (row + d[0] >= 0) & (row + d[0] < rows) & (col + d[1] >= 0) & (col + d[1] < cols)

    size_a, size_b = low_rows * high_cols, high_rows * low_cols
    me_a = (row % low_rows) * high_cols + col // low_cols
    me_b = (row // low_rows) * low_cols + col % low_cols

    def peer_a(k):
        p = (me_a + k) % size_a
        return ((row // low_rows) * low_rows + p // high_cols, (p % high_cols) * low_cols + col % low_cols)

    def peer_b(k):
        p = (me_b + k) % size_b
        return ((p // low_cols) * low_rows + row % low_rows, (col // low_cols) * low_cols + p % low_cols)

    def exchange_copies(s, k):
        W, R = streams[s].W, streams[s].R
        field = 2 * k + s
        made = []
        for i, d in enumerate(DIRS):
            back = DIRS.index((-d[0], -d[1]))
            made.append((pltpu.make_async_remote_copy(
                src_ref=pk[s].at[k], dst_ref=pr[s].at[k, back],
                send_sem=halo_send.at[field, i], recv_sem=halo_recv.at[field, back],
                device_id=(row + d[0], col + d[1]), device_id_type=MESH), d))
        for i, d, src, dst in ((8, (-1, 0), 2 * W, (R + 2) * W), (9, (1, 0), R * W, 0)):
            made.append((pltpu.make_async_remote_copy(
                src_ref=xm[s].at[k, :, pl.ds(src, 2 * W)], dst_ref=xm[s].at[k, :, pl.ds(dst, 2 * W)],
                send_sem=halo_send.at[field, i], recv_sem=halo_recv.at[field, i],
                device_id=(row + d[0], col), device_id_type=MESH), d))
        return made

    def exchange_start(s, k):
        for copy, d in exchange_copies(s, k):
            pl.when(has(d))(copy.start)

    def exchange_wait(s, k):
        W, R = streams[s].W, streams[s].R
        field = 2 * k + s
        for i, d in enumerate(DIRS):
            pl.when(has(d))(pltpu.make_async_copy(pk[s].at[k], pr[s].at[k, i], halo_recv.at[field, i]).wait)
        for i, d, dst in ((8, (1, 0), (R + 2) * W), (9, (-1, 0), 0)):
            ref = xm[s].at[k, :, pl.ds(dst, 2 * W)]
            pl.when(has(d))(pltpu.make_async_copy(ref, ref, halo_recv.at[field, i]).wait)

    def exchange_end(s, k):
        for copy, d in exchange_copies(s, k):
            pl.when(has(d))(copy.wait_send)

    def spread(k, stage, buf, me, size, peer):
        def send(p, _):
            pltpu.make_async_remote_copy(
                src_ref=buf.at[k, me], dst_ref=buf.at[k, me],
                send_sem=ar_send.at[k, stage], recv_sem=ar_recv.at[k, stage],
                device_id=peer(p), device_id_type=MESH).start()
            return 0

        lax.fori_loop(1, size, send, 0)

    def collect(k, stage, buf, size):
        ref = buf.at[k, pl.ds(0, size - 1)]
        pltpu.make_async_copy(ref, ref, ar_recv.at[k, stage]).wait()
        return jnp.sum(buf[k], axis=0)

    def reduce_start(k, value):
        ar_a[k, me_a] = value
        spread(k, 0, ar_a, me_a, size_a, peer_a)

    def reduce_middle(k):
        ar_b[k, me_b] = collect(k, 0, ar_a, size_a)
        spread(k, 1, ar_b, me_b, size_b, peer_b)

    def reduce_end(k):
        return collect(k, 1, ar_b, size_b)

    def reduce_drain(k):
        for stage, buf, size in ((0, ar_a, size_a), (1, ar_b, size_b)):
            ref = buf.at[k, pl.ds(0, size - 1)]
            pltpu.make_async_copy(ref, ref, ar_send.at[k, stage]).wait()

    for s in both:
        W, R = streams[s].W, streams[s].R
        for k in range(5):
            pr[s][k] = jnp.zeros(pr[s].shape[1:], BF16)
            xm[s][k, :, 0 : 2 * W] = jnp.zeros((streams[s].n, 2 * W), BF16)
            xm[s][k, :, (R + 2) * W : (R + 4) * W] = jnp.zeros((streams[s].n, 2 * W), BF16)
    barrier = pltpu.get_barrier_semaphore()

    def greet(device):
        pl.semaphore_signal(barrier, inc=1, device_id=device, device_id_type=MESH)

    for d in DIRS:
        pl.when(has(d))(functools.partial(greet, (row + d[0], col + d[1])))

    def greet_a(k, _):
        greet(peer_a(k))
        return 0

    def greet_b(k, _):
        greet(peer_b(k))
        return 0

    lax.fori_loop(1, size_a, greet_a, 0)
    lax.fori_loop(1, size_b, greet_b, 0)
    for s in both:
        put_rows(streams[s], [state[s][:, r, :].astype(F32) for r in range(streams[s].R)], xm[s].at[STATE], pk[s].at[STATE])
    beside = sum(has(d).astype(jnp.int32) for d in DIRS)
    pl.semaphore_wait(barrier, beside + (size_a + size_b - 2))
    for s in both:
        exchange_start(s, STATE)
    for s in both:
        put_rows(streams[s], [cot[s][:, r, :] for r in range(streams[s].R)], xm[s].at[COT], pk[s].at[COT])
    for s in both:
        exchange_start(s, COT)

    for s in both:
        n, w, W = streams[s].n, streams[s].w, streams[s].W
        for t in range(9):
            back = slice((8 - t) * n, (9 - t) * n)
            a4[s][(8 - t) // 3, (8 - t) % 3 * n : ((8 - t) % 3 + 1) * n, :] = first[s][t * n : (t + 1) * n, :]
            taps[back, 0:w] = second[s][t // 3, (t % 3) * n : (t % 3 + 1) * n, :]
        a1[s][...] = first[s][...].T
        a3[s][...] = taps[0 : 9 * n, 0:w].T
        same = subs_of((w, w)) == lanes_of((w, w))
        for src, dst in (((fine_gain, coarse_gain)[s], ga[s]), ((fine_shift, coarse_shift)[s], sh[s])):
            dst[...] = jnp.broadcast_to(jnp.sum(jnp.where(same, src[...][None, :], 0.0), axis=1, keepdims=True), (w, 128))
        R = streams[s].R
        mk[s][...] = jnp.ones((1, streams[s].NL), F32)
        mk[s][:, 0:W] = jnp.where(row > 0, 1.0, 0.0) * jnp.ones((1, W), F32)
        mk[s][:, (R + 1) * W : (R + 2) * W] = jnp.where(row < rows - 1, 1.0, 0.0) * jnp.ones((1, W), F32)
        lane = lanes_of((1, 128))
        q, line = lane % 8, lane // 8
        good = ((q == 0) & (col > 0)) | ((q == 3) & (col < cols - 1))
        good = good & (line < R + 2) & ((line > 0) | (row > 0)) & ((line < R + 1) | (row < rows - 1))
        mk[s][:, streams[s].main :] = jnp.where(good, 1.0, 0.0)
    here, there = subs_of((128, 256)), lanes_of((128, 256))
    dup[...] = jnp.where(there // 2 == here, 1.0, 0.0).astype(BF16)
    here, there = subs_of((256, 256)), lanes_of((256, 256))
    split[...] = jnp.where(here == 2 * (there % 128) + there // 128, 1.0, 0.0).astype(BF16)
    for a in range(2):
        for b in range(2):
            at = slice((2 * a + b) * f.n, (2 * a + b + 1) * f.n)
            rt[at, :] = reduction[at, :]
            taps[at, 0 : c.n] = up[...]
    rw[...] = rt[...].T
    u4[...] = taps[0 : 4 * f.n, 0 : c.n].T

    def load(s, k, ring=True):
        st = streams[s]
        edge = edge_of(st, pk[s].at[k], pr[s].at[k] if ring else None)
        build(st, xm[s].at[k], edge, x3[s], x9[s], ring)

    def group_loop(s, start, chunks, count, body):
        gs = streams[s].gs
        sums = []
        for g in range(GROUPS):
            at = slice(g * gs, (g + 1) * gs)

            accs = [jnp.zeros((8, 128), F32)] * count
            for k in range(start, start + chunks):
                accs = [a + fold(t) for a, t in zip(accs, body(g, at, k))]
            sums.append(accs)
        return [[sums[g][t] for g in range(GROUPS)] for t in range(count)]

    def ring_chunks(s):
        return 0, streams[s].NL // 128

    def own_chunks(s):
        return streams[s].W // 128, streams[s].cells // 128

    def flat(per_stream, t):
        return [a for s in both for a in per_stream[s][t]]

    sums = []
    for s in both:
        exchange_wait(s, STATE)
        load(s, STATE)
        widen(streams[s], a1[s], x3[s], x9[s], nm[s])

        def squares(g, at, k):
            x = nm[s][at, block(k, 128)]
            return x, x * x

        sums.append(group_loop(s, *own_chunks(s), 2, squares))
    reduce_start(0, to_row(flat(sums, 0) + flat(sums, 1)))
    for s in both:
        exchange_wait(s, COT)
        load(s, COT)
        widen(streams[s], a1[s], x3[s], x9[s], kc[s], inside=True)
    reduce_middle(0)
    stats = reduce_end(0)

    lane = lanes_of((1, 128))
    counts = [rows * cols * streams[s].cells * streams[s].gs for s in both]
    per = jnp.where(lane % 8 < GROUPS, 1.0 / counts[0], 1.0 / counts[1])
    mean_row = stats * per
    variance = roll(mean_row, -8) - mean_row * mean_row
    inverse_row = jnp.where(lane < 8, lax.rsqrt(variance + EPSILON), 0.0)
    means = [[pick(mean_row, s * GROUPS + g) for g in range(GROUPS)] for s in both]
    inverses = [[pick(inverse_row, s * GROUPS + g) for g in range(GROUPS)] for s in both]

    for s in both:
        gs = streams[s].gs
        for g in range(GROUPS):
            at = slice(g * gs, (g + 1) * gs)

            for k in range(streams[s].NL // 128):
                here = block(k, 128)
                gain, keep = ga[s][at, :], mk[s][:, here]
                normed = (nm[s][at, here] - means[s][g]) * inverses[s][g]
                level = normed * gain + sh[s][at, :]
                sigma = jax.nn.sigmoid(level)
                nm[s][at, here] = normed
                hb[s][at, here] = (level * sigma * keep).astype(BF16)
                ls[s][at, here] = sigma * (1.0 + level * (1.0 - sigma)) * gain * keep

    def own_row(s, ref, r):
        return ref[:, r * streams[s].W : (r + 1) * streams[s].W]

    def halve():
        parts = dot(stack_f[...], split[...]).astype(BF16)
        lined = []
        for R in range(c.R):
            lined.append(jnp.concatenate([
                parts[(2 * R + a) * f.n : (2 * R + a + 1) * f.n, b * 128 : (b + 1) * 128]
                for a in range(2) for b in range(2)], axis=0))
        return jnp.concatenate(lined, axis=1)

    def double():
        return dot(stack_c[...], dup[...]).astype(BF16)

    for s, stack in ((0, stack_f), (1, stack_c)):
        n = streams[s].n
        got = narrow(streams[s], second[s], hb[s], zs[s])
        for r in range(streams[s].R):
            mixed = got(r) + inject[s][:, r, :].astype(F32)
            sl[s][:, r * streams[s].W : (r + 1) * streams[s].W] = mixed
            stack[r * n : (r + 1) * n, :] = mixed.astype(BF16)
    down = dot(rw[...], halve())
    wide = double()
    for R in range(c.R):
        lifted = dot(up[...], wide[R * c.n : (R + 1) * c.n, :])
        for r in (2 * R, 2 * R + 1):
            at = slice(r * f.W, (r + 1) * f.W)
            sl_f[:, at] = swish_derivative(sl_f[:, at] + lifted)
    sl_c[...] = swish_derivative(sl_c[...] + down)

    def total(field, k):
        for r in range(f.R):
            stack_f[r * f.n : (r + 1) * f.n, :] = (field(0, r) * own_row(0, sl_f, r)).astype(BF16)
        coarse_grads = [field(1, r) * own_row(1, sl_c, r) for r in range(c.R)]
        for r in range(c.R):
            stack_c[r * c.n : (r + 1) * c.n, :] = coarse_grads[r].astype(BF16)
        raised = dot(u4[...], halve())
        put_rows(c, [coarse_grads[r] + own_row(1, raised, r) for r in range(c.R)], xm_c.at[k], pk_c.at[k])
        wide = double()
        even = lanes_of((f.n, f.W)) % 2 == 0
        fine = []
        for R in range(c.R):
            spread_out = dot(rt[...], wide[R * c.n : (R + 1) * c.n, :])
            for a in range(2):
                part = [spread_out[(2 * a + b) * f.n : (2 * a + b + 1) * f.n] for b in range(2)]
                r = 2 * R + a
                fine.append(field(0, r) * own_row(0, sl_f, r) + jnp.where(even, part[0], part[1]))
        put_rows(f, fine, xm_f.at[k], pk_f.at[k])
        for s in both:
            exchange_start(s, k)

    total(lambda s, r: cot[s][:, r, :], TOTAL0)

    sums = []
    for s in both:
        load(s, TOTAL0, ring=False)
        widen(streams[s], a3[s], x3[s], x9[s], hg[s])

        def pushed(g, at, k):
            scaled = hg[s][at, block(k, 128)] * ls[s][at, block(k, 128)]
            return scaled, scaled * nm[s][at, block(k, 128)]

        sums.append(group_loop(s, *ring_chunks(s), 2, pushed))
    reduce_start(1, to_row(flat(sums, 0) + flat(sums, 1)))

    def scale(s, k):
        exchange_wait(s, k)
        load(s, k)
        widen(streams[s], a3[s], x3[s], x9[s], hg[s])

    for s in both:
        scale(s, TOTAL0)
    reduce_middle(1)
    along = []
    for s in both:

        def cot_sums(g, at, k):
            x = kc[s][at, block(k - streams[s].W // 128, 128)]
            return x, x * nm[s][at, block(k, 128)]

        along.append(group_loop(s, *own_chunks(s), 2, cot_sums))
    found = reduce_end(1)

    def image(row_sums):
        scaled_mean = row_sums * per
        got = []
        for s in both:
            gs = streams[s].gs
            for g in range(GROUPS):
                at = slice(g * gs, (g + 1) * gs)
                one, two = pick(scaled_mean, s * GROUPS + g), pick(scaled_mean, 8 + s * GROUPS + g)

                for k in range(streams[s].NL // 128):
                    here = block(k, 128)
                    scaled = hg[s][at, here] * ls[s][at, here]
                    grad = inverses[s][g] * (scaled - one - nm[s][at, here] * two)
                    hb[s][at, here] = (grad * mk[s][:, here]).astype(BF16)
            got.append(narrow(streams[s], a4[s], hb[s], zs[s]))
        return got

    got = image(found)
    for s in both:
        made = [got[s](r) for r in range(streams[s].R)]
        for r in range(streams[s].R):
            es[s][:, r * streams[s].W : (r + 1) * streams[s].W] = made[r]
        put_rows(streams[s], made, xm[s].at[IMAGE], pk[s].at[IMAGE])
        exchange_start(s, IMAGE)
    total(lambda s, r: own_row(s, es[s], r), TOTAL1)

    gram = [jnp.zeros((8, 128), F32) for _ in range(3)]
    for s in both:
        for r in range(streams[s].R):
            a, b = cot[s][:, r, :], own_row(s, es[s], r)
            for t, product in enumerate((a * a, a * b, b * b)):
                product = fold(product)
                for half in range(streams[s].W // 128):
                    gram[t] = gram[t] + product[:, half * 128 : (half + 1) * 128]
    sums = []
    crossed = [jnp.zeros((8, 128), F32) for _ in range(2)]
    for s in both:
        exchange_wait(s, IMAGE)
        load(s, IMAGE)
        widen(streams[s], a1[s], x3[s], x9[s], kp[s], inside=True)
    for s in both:
        scale(s, TOTAL1)

        def all_sums(g, at, k):
            here, inner = block(k, 128), block(k - streams[s].W // 128, 128)
            normed, lifted = nm[s][at, here], kp[s][at, inner]
            scaled = hg[s][at, here] * ls[s][at, here]
            return scaled, scaled * normed, lifted, lifted * normed, scaled * kc[s][at, inner], scaled * lifted

        sums.append(group_loop(s, *own_chunks(s), 6, all_sums))
        for g in range(GROUPS):
            for t in range(2):
                crossed[t] = crossed[t] + sums[s][4 + t][g] * inverses[s][g]
    entries = flat(sums, 0) + flat(sums, 1) + flat(along, 0) + flat(along, 1) + flat(sums, 2) + flat(sums, 3)
    reduce_start(2, to_row(entries + gram + crossed))
    reduce_middle(2)
    found = reduce_end(2)

    weight = (inverse_row + roll(inverse_row, 8)) * per
    cc, c0, g00, cq, pq = [pick(found, 48 + k) for k in range(5)]
    c1 = cq - jnp.sum(found * weight * roll(found, -16), axis=1, keepdims=True)
    g01 = pq - jnp.sum(found * weight * roll(found, -32), axis=1, keepdims=True)
    d0 = jnp.maximum(cc - c0, 0.25 * cc)
    alpha = 1.0 + c0 / d0
    kappa = alpha * g00 / d0
    turn = -alpha * (c1 - c0)
    d1 = jnp.maximum(-alpha * alpha * (g01 - g00) - kappa * alpha * (c1 - c0), 0.25 * alpha * alpha * g00)
    m0 = -((1.0 - alpha) * c0 + alpha * c1)
    m1 = -alpha * ((1.0 - alpha) * g00 + alpha * g01) + kappa * m0
    by0 = 1.0 - m0 / d0 + (m1 / d1) * (turn / d0)
    by1 = alpha * (1.0 - m1 / d1)

    got = image(found)
    for s in both:
        for r in range(streams[s].R):
            outs[s][:, r, :] = cot[s][:, r, :] + by0 * own_row(s, es[s], r) + by1 * got[s](r)

    for s in both:
        for k in range(5):
            exchange_end(s, k)
    for k in range(3):
        reduce_drain(k)


def solution(mesh):
    rows, cols = mesh.shape["row"], mesh.shape["col"]
    sizes = (rows, cols, min(rows, 8), min(cols, 4))

    def body(*args):
        fine_state, coarse_state = args[:2]
        fine_first, fine_second, coarse_first, coarse_second = args[6:10]
        f = Stream(fine_state.shape[0], fine_first.shape[1], *fine_state.shape[1:])
        c = Stream(coarse_state.shape[0], coarse_first.shape[1], *coarse_state.shape[1:])
        both = (f, c)
        args = list(args)
        for k, s in ((6, f), (8, c)):
            args[k] = args[k].transpose(0, 2, 1).reshape(9 * s.n, s.w)
            args[k + 1] = args[k + 1].reshape(3, 3 * s.n, s.w)
        args[14] = args[14].transpose(0, 1, 3, 2).reshape(4 * f.n, c.n)
        vmem = pltpu.VMEM
        scratch = []
        for shape, dtype in (
            (lambda s: (5, s.n, (s.R + 4) * s.W), BF16),
            (lambda s: (5, s.n, 128), BF16),
            (lambda s: (5, 8, s.n, 128), BF16),
            (lambda s: (3 * s.n, (s.R + 4) * s.W), BF16),
            (lambda s: (3, 3 * s.n, 128), BF16),
            (lambda s: (s.w, s.NL), F32),
            (lambda s: (s.w, s.NL), F32),
            (lambda s: (s.w, s.NL), F32),
            (lambda s: (s.w, s.NL), BF16),
            (lambda s: (s.w, s.cells), F32),
            (lambda s: (s.w, s.cells), F32),
            (lambda s: (3 * s.n, s.cells), F32),
            (lambda s: (s.n, s.cells), F32),
            (lambda s: (s.n, s.cells), F32),
            (lambda s: (1, s.NL), F32),
            (lambda s: (s.w, 128), F32),
            (lambda s: (s.w, 128), F32),
            (lambda s: (s.w, 9 * s.n), BF16),
            (lambda s: (s.w, 9 * s.n), BF16),
            (lambda s: (3, 3 * s.n, s.w), BF16),
        ):
            scratch += [vmem(shape(s), dtype) for s in both]
        scratch += [
            vmem((128, 256), BF16),
            vmem((256, 256), BF16),
            vmem((4 * f.n, c.n), BF16),
            vmem((c.n, 4 * f.n), BF16),
            vmem((c.n, 4 * f.n), BF16),
            vmem((f.R * f.n, f.W), BF16),
            vmem((c.R * c.n, c.W), BF16),
            vmem((9 * c.n, c.w), BF16),
            vmem((3, sizes[2] * (cols // sizes[3]), 1, 128), F32),
            vmem((3, (rows // sizes[2]) * sizes[3], 1, 128), F32),
            pltpu.SemaphoreType.DMA((10, 10)),
            pltpu.SemaphoreType.DMA((10, 10)),
            pltpu.SemaphoreType.DMA((3, 2)),
            pltpu.SemaphoreType.DMA((3, 2)),
        ]
        return pl.pallas_call(
            functools.partial(kernel, both, sizes),
            out_shape=[jax.ShapeDtypeStruct(a.shape, F32) for a in args[4:6]],
            in_specs=[pl.BlockSpec(memory_space=pltpu.VMEM)] * 16,
            out_specs=[pl.BlockSpec(memory_space=pltpu.VMEM)] * 2,
            scratch_shapes=scratch,
            compiler_params=pltpu.CompilerParams(
                collective_id=0, has_side_effects=True, vmem_limit_bytes=56 * 1024 * 1024
            ),
        )(*args)

    field = P(None, "row", "col")
    return jax.shard_map(
        body,
        mesh=mesh,
        in_specs=(field,) * 6 + (P(),) * 10,
        out_specs=(field, field),
        check_vma=False,
    )
```

```python
import functools

import jax
import jax.numpy as jnp
from jax import lax
from jax.experimental import pallas as pl
from jax.experimental.pallas import tpu as pltpu
from jax.sharding import PartitionSpec as P

GROUPS = 4
EPSILON = 1e-05
MESH = pl.DeviceIdType.MESH
F32 = jnp.float32
BF16 = jnp.bfloat16
DIRS = [(dr, dc) for dr in (-1, 0, 1) for dc in (-1, 0, 1) if dr or dc]
DIAGONALS = [(-1, -1), (-1, 1), (1, -1), (1, 1)]
STATE, TOTAL0, TOTAL1, COT, IMAGE = range(5)
SENT = 3


class Stream:
    def __init__(self, n, w, rows, cols):
        self.n, self.w, self.R, self.W = n, w, rows, cols
        self.gs = w // GROUPS
        self.main = (rows + 2) * cols
        self.NL = self.main + 128
        self.cells = rows * cols
        self.own = slice(2 * cols, 2 * cols + rows * cols)


def dot(a, b):
    return jnp.dot(a, b, preferred_element_type=F32)


def lanes_of(shape):
    return lax.broadcasted_iota(jnp.int32, shape, len(shape) - 1)


def subs_of(shape):
    return lax.broadcasted_iota(jnp.int32, shape, 0)


def roll(x, shift):
    return pltpu.roll(x, shift % x.shape[1], 1)


def wide_lanes(x, width):
    return x if width == 128 else jnp.concatenate([x] * (width // 128), axis=1)


def fold(x):
    return jnp.sum(x.reshape(x.shape[0] // 8, 8, x.shape[1]), axis=0)


def block(i, size):
    return slice(i * size, (i + 1) * size)


def swish_derivative(v):
    sigma = jax.nn.sigmoid(v)
    return sigma * (1.0 + v * (1.0 - sigma))


def to_row(accs):
    row = jnp.zeros((1, 128), F32)
    sub, lane = subs_of((8, 128)), lanes_of((8, 128))
    for first in range(0, len(accs), 8):
        stack = jnp.zeros((8, 128), F32)
        for k, acc in enumerate(accs[first : first + 8]):
            stack = jnp.where(sub == k, jnp.sum(acc, axis=0, keepdims=True), stack)
        col = jnp.sum(stack, axis=1, keepdims=True)
        row = row + jnp.sum(jnp.where(lane == sub + first, col, 0.0), axis=0, keepdims=True)
    return row


def pick(row, k):
    return jnp.sum(jnp.where(lanes_of((1, 128)) == k, row, 0.0), axis=1, keepdims=True)


def put_rows(s, rows, xm):
    for r, x in enumerate(rows):
        xm[:, (r + 2) * s.W : (r + 3) * s.W] = x.astype(BF16)


def pack(s, xm, lines):
    lane = lanes_of((s.n, 128))
    packed = jnp.zeros((s.n, 128), F32)
    for k in lines:
        left, right = xm[:, k * s.W : k * s.W + 128], xm[:, (k + 1) * s.W - 128 : (k + 1) * s.W]
        x = jnp.where(lane < 2, left.astype(F32), jnp.where(lane >= 126, right.astype(F32), 0.0))
        packed = packed + roll(x, 8 * k + 2)
    return jnp.where(lane % 8 <= 2, packed, roll(packed, 2))


def build(s, xm, edge, x3, x9, ring):
    n, W = s.n, s.W
    lane = lanes_of((n, 128))
    joined = jnp.where(lane % 8 == 0, roll(edge, -4), edge)
    lane = lanes_of((n, W))
    for k in range(s.R + 4):
        at = slice(k * W, (k + 1) * W)
        if not ring and not 2 <= k < s.R + 2:
            x3[:, at] = jnp.zeros((3 * n, W), BF16)
            continue
        x = xm[:, at]
        xf = x.astype(F32)
        t = wide_lanes(roll(joined, -(8 * k + 1)), W)
        x3[0:n, at] = jnp.where(lane == 0, t, roll(xf, 1)).astype(BF16)
        x3[n : 2 * n, at] = x
        x3[2 * n : 3 * n, at] = jnp.where(lane == W - 1, t, roll(xf, -1)).astype(BF16)
    for i in range(3):
        for j in range(3):
            x9[i, j * n : (j + 1) * n, :] = roll(edge, -(8 * i + j)).astype(BF16)


def widen(s, weights, x3, x9, out):
    taps = [x3[:, i * s.W : i * s.W + s.main] for i in range(3)]
    out[:, 0 : s.main] = dot(weights[...], jnp.concatenate(taps, axis=0))
    out[:, s.main :] = dot(weights[...], jnp.concatenate([x9[i] for i in range(3)], axis=0))


def narrow(s, weights, h, z):
    n, W = s.n, s.W

    for b in range(0, s.cells, 256):
        total = dot(weights[0], h[:, b : b + 256])
        for i in (1, 2):
            total = total + dot(weights[i], h[:, b + i * W : b + i * W + 256])
        z[:, b : b + 256] = total
    edges = [dot(weights[i], h[:, s.main :]) for i in range(3)]
    total = edges[0] + roll(edges[1], -8) + roll(edges[2], -16)
    q = lanes_of((n, 128)) % 8
    joined = jnp.where(q == 1, roll(total[:n], 1), roll(total[2 * n :], -3))
    lane = lanes_of((n, W))

    def row(r):
        at = slice(r * W, (r + 1) * W)
        t = wide_lanes(roll(joined, -(8 * r + 1)), W)
        left = jnp.where(lane == 0, t, roll(z[0:n, at], 1))
        right = jnp.where(lane == W - 1, t, roll(z[2 * n : 3 * n, at], -1))
        return left + z[n : 2 * n, at] + right

    return row


def kernel(streams, sizes, *refs):
    f, c = streams
    (
        fine_state, coarse_state, fine_inject, coarse_inject, fine_cot, coarse_cot,
        fine_first, fine_second, coarse_first, coarse_second,
        fine_gain, fine_shift, coarse_gain, coarse_shift, reduction, up,
        fine_out, coarse_out,
        *rest,
    ) = refs
    (xm_f, xm_c, x3_f, x3_c, x9_f, x9_c,
     nm_f, nm_c, ls_f, ls_c, hg_f, hg_c, hb_f, hb_c, kc_f, kc_c, kp_f, kp_c,
     z_f, z_c, sl_f, sl_c, e_f, e_c, mk_f, mk_c, ga_f, ga_c, sh_f, sh_c,
     a1_f, a1_c, a3_f, a3_c, a4_f, a4_c, dup, split, rt, rw, u4, stack_f, stack_c, taps,
     pk, pr, corner, corners, ar_a, ar_b, halo_send, halo_recv, ar_send, ar_recv) = rest
    xm, x3, x9 = (xm_f, xm_c), (x3_f, x3_c), (x9_f, x9_c)
    nm, ls, hg, hb = (nm_f, nm_c), (ls_f, ls_c), (hg_f, hg_c), (hb_f, hb_c)
    kc, kp, zs, sl, es, mk = (kc_f, kc_c), (kp_f, kp_c), (z_f, z_c), (sl_f, sl_c), (e_f, e_c), (mk_f, mk_c)
    ga, sh, a1, a3, a4 = (ga_f, ga_c), (sh_f, sh_c), (a1_f, a1_c), (a3_f, a3_c), (a4_f, a4_c)
    first, second = (fine_first, coarse_first), (fine_second, coarse_second)
    cot, state = (fine_cot, coarse_cot), (fine_state, coarse_state)
    inject, outs = (fine_inject, coarse_inject), (fine_out, coarse_out)
    rows, cols, low_rows, low_cols = sizes
    high_rows, high_cols = rows // low_rows, cols // low_cols
    row, col = lax.axis_index("row"), lax.axis_index("col")
    both = (0, 1)
    own_part = (slice(0, f.n), slice(f.n, f.n + c.n))

    def has(d):
        return (row + d[0] >= 0) & (row + d[0] < rows) & (col + d[1] >= 0) & (col + d[1] < cols)

    size_a, size_b = low_rows * high_cols, high_rows * low_cols
    me_a = (row % low_rows) * high_cols + col // low_cols
    me_b = (row // low_rows) * low_cols + col % low_cols

    def peer_a(k):
        p = (me_a + k) % size_a
        return ((row // low_rows) * low_rows + p // high_cols, (p % high_cols) * low_cols + col % low_cols)

    def peer_b(k):
        p = (me_b + k) % size_b
        return ((p // low_cols) * low_rows + row % low_rows, (col // low_cols) * low_cols + p % low_cols)

    def strips(k):
        made = []
        for s in both:
            W, R = streams[s].W, streams[s].R
            for i, d, src, dst in ((s, (-1, 0), 2 * W, (R + 2) * W), (2 + s, (1, 0), R * W, 0)):
                made.append((pltpu.make_async_remote_copy(
                    src_ref=xm[s].at[k, :, pl.ds(src, 2 * W)], dst_ref=xm[s].at[k, :, pl.ds(dst, 2 * W)],
                    send_sem=halo_send.at[k, i], recv_sem=halo_recv.at[k, i],
                    device_id=(row + d[0], col), device_id_type=MESH), d))
        return made

    def packs(k):
        made = []
        for i, dc in ((4, -1), (5, 1)):
            made.append((pltpu.make_async_remote_copy(
                src_ref=pk.at[k], dst_ref=pr.at[k, i - 4],
                send_sem=halo_send.at[k, i], recv_sem=halo_recv.at[k, i],
                device_id=(row, col + dc), device_id_type=MESH), (0, dc)))
        for i, (dr, dc) in enumerate(DIAGONALS):
            made.append((pltpu.make_async_remote_copy(
                src_ref=corner.at[k, (dr + 1) // 2], dst_ref=corners.at[k, i],
                send_sem=halo_send.at[k, 6 + i], recv_sem=halo_recv.at[k, 6 + i],
                device_id=(row + dr, col + dc), device_id_type=MESH), (dr, dc)))
        return made

    def pack_own(k):
        for s in both:
            R = streams[s].R
            pk[k, own_part[s], :] = pack(streams[s], xm[s].at[k], range(2, R + 2)).astype(BF16)

    def exchange_start(k):
        for copy, d in strips(k):
            pl.when(has(d))(copy.start)
        pack_own(k)
        own = pk[k].astype(F32)
        shift = 8 * (f.R - c.R)
        low = jnp.concatenate([own[: f.n], roll(own[f.n :], shift)], axis=0)
        lane = lanes_of(own.shape)
        cells = jnp.where(lane < 8 * (c.R + 2), own, low)
        cells = jnp.concatenate([cells, jnp.zeros((128 - f.n - c.n, 128), F32)], axis=0).T
        corner[k, 0] = cells[16:32].astype(BF16)
        corner[k, 1] = cells[8 * f.R : 8 * f.R + 16].astype(BF16)
        for copy, d in packs(k):
            pl.when(has(d))(copy.start)

    def exchange_wait(k):
        for copy, d in strips(k) + packs(k):
            pl.when(has((-d[0], -d[1])))(copy.wait_recv)

    def exchange_end(k):
        for copy, d in strips(k) + packs(k):
            pl.when(has(d))(copy.wait_send)

    def edges(k, ring):
        lane = lanes_of((f.n + c.n, 128))
        q = lane % 8
        own = pk[k].astype(F32)
        if ring:
            sides = jnp.where(q <= 1, pr[k, 1].astype(F32), jnp.where(q <= 3, own, pr[k, 0].astype(F32)))
            sub = subs_of((16, 128)) % 8
            got = [corners[k, i].astype(F32) for i in range(4)]
            above = jnp.where(sub <= 3, got[DIAGONALS.index((1, 1))], got[DIAGONALS.index((1, -1))])
            below = jnp.where(sub <= 3, got[DIAGONALS.index((-1, 1))], got[DIAGONALS.index((-1, -1))])
            low = 8 * (f.R + 2)
            blank = [jnp.zeros((low - 16, 128), F32), jnp.zeros((112 - low, 128), F32)]
            cells = jnp.concatenate([above, blank[0], below, blank[1]], axis=0).T
        else:
            sides = jnp.where((q >= 2) & (q <= 3), own, 0.0)
        made = []
        for s in both:
            n, R = streams[s].n, streams[s].R
            lane = lanes_of((n, 128))
            q = lane % 8
            outside = jnp.zeros((n, 128), F32)
            if ring:
                outer = cells[own_part[s]]
                outer = jnp.where(lane < 16, outer, roll(outer, 8 * (R - f.R)))
                lines = pack(streams[s], xm[s].at[k], (0, 1, R + 2, R + 3))
                outside = jnp.where((q >= 2) & (q <= 3), lines, outer)
            inside = (lane >= 16) & (lane < 16 + 8 * R)
            made.append(jnp.where(inside, sides[own_part[s]], outside))
        return made

    def spread(k, stage, buf, me, size, peer):
        def send(p, _):
            pltpu.make_async_remote_copy(
                src_ref=buf.at[k, me], dst_ref=buf.at[k, me],
                send_sem=ar_send.at[k, stage], recv_sem=ar_recv.at[k, stage],
                device_id=peer(p), device_id_type=MESH).start()
            return 0

        lax.fori_loop(1, size, send, 0)

    def collect(k, stage, buf, size):
        ref = buf.at[k, pl.ds(0, size - 1)]
        pltpu.make_async_copy(ref, ref, ar_recv.at[k, stage]).wait()
        return jnp.sum(buf[k], axis=0)

    def reduce_start(k, value):
        ar_a[k, me_a] = value
        spread(k, 0, ar_a, me_a, size_a, peer_a)

    def reduce_middle(k):
        ar_b[k, me_b] = collect(k, 0, ar_a, size_a)
        spread(k, 1, ar_b, me_b, size_b, peer_b)

    def reduce_end(k):
        return collect(k, 1, ar_b, size_b)

    def reduce_drain(k):
        for stage, buf, size in ((0, ar_a, size_a), (1, ar_b, size_b)):
            ref = buf.at[k, pl.ds(0, size - 1)]
            pltpu.make_async_copy(ref, ref, ar_send.at[k, stage]).wait()

    for s in both:
        W, R = streams[s].W, streams[s].R
        for k in range(SENT):
            xm[s][k, :, 0 : 2 * W] = jnp.zeros((streams[s].n, 2 * W), BF16)
            xm[s][k, :, (R + 2) * W : (R + 4) * W] = jnp.zeros((streams[s].n, 2 * W), BF16)
    pr[...] = jnp.zeros(pr.shape, BF16)
    corners[...] = jnp.zeros(corners.shape, BF16)
    barrier = pltpu.get_barrier_semaphore()

    def greet(device):
        pl.semaphore_signal(barrier, inc=1, device_id=device, device_id_type=MESH)

    for d in DIRS:
        pl.when(has(d))(functools.partial(greet, (row + d[0], col + d[1])))

    def greet_a(k, _):
        greet(peer_a(k))
        return 0

    def greet_b(k, _):
        greet(peer_b(k))
        return 0

    lax.fori_loop(1, size_a, greet_a, 0)
    lax.fori_loop(1, size_b, greet_b, 0)
    for s in both:
        put_rows(streams[s], [state[s][:, r, :] for r in range(streams[s].R)], xm[s].at[STATE])
    beside = sum(has(d).astype(jnp.int32) for d in DIRS)
    pl.semaphore_wait(barrier, beside + (size_a + size_b - 2))
    exchange_start(STATE)
    for s in both:
        put_rows(streams[s], [cot[s][:, r, :] for r in range(streams[s].R)], xm[s].at[COT])
    pack_own(COT)

    for s in both:
        n, w, W = streams[s].n, streams[s].w, streams[s].W
        for t in range(9):
            back = slice((8 - t) * n, (9 - t) * n)
            a4[s][(8 - t) // 3, (8 - t) % 3 * n : ((8 - t) % 3 + 1) * n, :] = first[s][t * n : (t + 1) * n, :]
            taps[back, 0:w] = second[s][t // 3, (t % 3) * n : (t % 3 + 1) * n, :]
        a1[s][...] = first[s][...].T
        a3[s][...] = taps[0 : 9 * n, 0:w].T
        same = subs_of((w, w)) == lanes_of((w, w))
        for src, dst in (((fine_gain, coarse_gain)[s], ga[s]), ((fine_shift, coarse_shift)[s], sh[s])):
            dst[...] = jnp.broadcast_to(jnp.sum(jnp.where(same, src[...][None, :], 0.0), axis=1, keepdims=True), (w, 128))
        R = streams[s].R
        mk[s][...] = jnp.ones((1, streams[s].NL), F32)
        mk[s][:, 0:W] = jnp.where(row > 0, 1.0, 0.0) * jnp.ones((1, W), F32)
        mk[s][:, (R + 1) * W : (R + 2) * W] = jnp.where(row < rows - 1, 1.0, 0.0) * jnp.ones((1, W), F32)
        lane = lanes_of((1, 128))
        q, line = lane % 8, lane // 8
        good = ((q == 0) & (col > 0)) | ((q == 3) & (col < cols - 1))
        good = good & (line < R + 2) & ((line > 0) | (row > 0)) & ((line < R + 1) | (row < rows - 1))
        mk[s][:, streams[s].main :] = jnp.where(good, 1.0, 0.0)
    here, there = subs_of((128, 256)), lanes_of((128, 256))
    dup[...] = jnp.where(there // 2 == here, 1.0, 0.0).astype(BF16)
    here, there = subs_of((256, 256)), lanes_of((256, 256))
    split[...] = jnp.where(here == 2 * (there % 128) + there // 128, 1.0, 0.0).astype(BF16)
    for a in range(2):
        for b in range(2):
            at = slice((2 * a + b) * f.n, (2 * a + b + 1) * f.n)
            rt[at, :] = reduction[at, :]
            taps[at, 0 : c.n] = up[...]
    rw[...] = rt[...].T
    u4[...] = taps[0 : 4 * f.n, 0 : c.n].T

    def spread_wide(k, weights, outs, ring=True):
        if ring:
            exchange_wait(k)
        tiles = edges(k, ring)
        for s in both:
            build(streams[s], xm[s].at[k], tiles[s], x3[s], x9[s], ring)
            widen(streams[s], weights[s], x3[s], x9[s], outs[s])

    def masked(s, k, x):
        W, R = streams[s].W, streams[s].R
        return x if W <= 128 * k < (R + 1) * W else x * mk[s][:, block(k, 128)]

    def group_loop(s, start, chunks, count, body):
        gs = streams[s].gs
        sums = []
        for g in range(GROUPS):
            at = slice(g * gs, (g + 1) * gs)

            accs = [jnp.zeros((8, 128), F32)] * count
            for k in range(start, start + chunks):
                accs = [a + fold(t) for a, t in zip(accs, body(g, at, k))]
            sums.append(accs)
        return [[sums[g][t] for g in range(GROUPS)] for t in range(count)]

    def ring_chunks(s):
        return 0, streams[s].NL // 128

    def own_chunks(s):
        return streams[s].W // 128, streams[s].cells // 128

    def flat(per_stream, t):
        return [a for s in both for a in per_stream[s][t]]

    sums = []
    spread_wide(STATE, a1, nm)
    for s in both:

        def squares(g, at, k):
            x = nm[s][at, block(k, 128)]
            return x, x * x

        sums.append(group_loop(s, *own_chunks(s), 2, squares))
    reduce_start(0, to_row(flat(sums, 0) + flat(sums, 1)))
    spread_wide(COT, a1, kc, ring=False)
    reduce_middle(0)
    stats = reduce_end(0)

    lane = lanes_of((1, 128))
    counts = [rows * cols * streams[s].cells * streams[s].gs for s in both]
    per = jnp.where(lane % 8 < GROUPS, 1.0 / counts[0], 1.0 / counts[1])
    mean_row = stats * per
    variance = roll(mean_row, -8) - mean_row * mean_row
    inverse_row = jnp.where(lane < 8, lax.rsqrt(variance + EPSILON), 0.0)
    means = [[pick(mean_row, s * GROUPS + g) for g in range(GROUPS)] for s in both]
    inverses = [[pick(inverse_row, s * GROUPS + g) for g in range(GROUPS)] for s in both]

    for s in both:
        gs = streams[s].gs
        for g in range(GROUPS):
            at = slice(g * gs, (g + 1) * gs)

            for k in range(streams[s].NL // 128):
                here = block(k, 128)
                gain, keep = ga[s][at, :], mk[s][:, here]
                normed = (nm[s][at, here] - means[s][g]) * inverses[s][g]
                level = normed * gain + sh[s][at, :]
                sigma = jax.nn.sigmoid(level)
                nm[s][at, here] = normed
                hb[s][at, here] = (level * sigma * keep).astype(BF16)
                ls[s][at, here] = sigma * (1.0 + level * (1.0 - sigma)) * gain * keep

    def own_row(s, ref, r):
        return ref[:, r * streams[s].W : (r + 1) * streams[s].W]

    def halve():
        parts = dot(stack_f[...], split[...]).astype(BF16)
        lined = []
        for R in range(c.R):
            lined.append(jnp.concatenate([
                parts[(2 * R + a) * f.n : (2 * R + a + 1) * f.n, b * 128 : (b + 1) * 128]
                for a in range(2) for b in range(2)], axis=0))
        return jnp.concatenate(lined, axis=1)

    def double():
        return dot(stack_c[...], dup[...]).astype(BF16)

    for s, stack in ((0, stack_f), (1, stack_c)):
        n = streams[s].n
        got = narrow(streams[s], second[s], hb[s], zs[s])
        for r in range(streams[s].R):
            mixed = got(r) + inject[s][:, r, :].astype(F32)
            sl[s][:, r * streams[s].W : (r + 1) * streams[s].W] = mixed
            stack[r * n : (r + 1) * n, :] = mixed.astype(BF16)
    down = dot(rw[...], halve())
    wide = double()
    for R in range(c.R):
        lifted = dot(up[...], wide[R * c.n : (R + 1) * c.n, :])
        for r in (2 * R, 2 * R + 1):
            at = slice(r * f.W, (r + 1) * f.W)
            sl_f[:, at] = swish_derivative(sl_f[:, at] + lifted)
    sl_c[...] = swish_derivative(sl_c[...] + down)

    def total(field, k):
        for r in range(f.R):
            stack_f[r * f.n : (r + 1) * f.n, :] = (field(0, r) * own_row(0, sl_f, r)).astype(BF16)
        coarse_grads = [field(1, r) * own_row(1, sl_c, r) for r in range(c.R)]
        for r in range(c.R):
            stack_c[r * c.n : (r + 1) * c.n, :] = coarse_grads[r].astype(BF16)
        raised = dot(u4[...], halve())
        put_rows(c, [coarse_grads[r] + own_row(1, raised, r) for r in range(c.R)], xm_c.at[k])
        wide = double()
        even = lanes_of((f.n, f.W)) % 2 == 0
        fine = []
        for R in range(c.R):
            spread_out = dot(rt[...], wide[R * c.n : (R + 1) * c.n, :])
            for a in range(2):
                part = [spread_out[(2 * a + b) * f.n : (2 * a + b + 1) * f.n] for b in range(2)]
                r = 2 * R + a
                fine.append(field(0, r) * own_row(0, sl_f, r) + jnp.where(even, part[0], part[1]))
        put_rows(f, fine, xm_f.at[k])
        exchange_start(k)

    total(lambda s, r: cot[s][:, r, :], TOTAL0)

    sums = []
    spread_wide(TOTAL0, a3, hg, ring=False)
    for s in both:

        def pushed(g, at, k):
            scaled = hg[s][at, block(k, 128)] * ls[s][at, block(k, 128)]
            return scaled, scaled * nm[s][at, block(k, 128)]

        sums.append(group_loop(s, *ring_chunks(s), 2, pushed))
    reduce_start(1, to_row(flat(sums, 0) + flat(sums, 1)))

    spread_wide(TOTAL0, a3, hg)
    reduce_middle(1)
    along = []
    for s in both:

        def cot_sums(g, at, k):
            x = masked(s, k, kc[s][at, block(k, 128)])
            return x, x * nm[s][at, block(k, 128)]

        along.append(group_loop(s, *ring_chunks(s), 2, cot_sums))
    found = reduce_end(1)

    def image(row_sums):
        scaled_mean = row_sums * per
        got = []
        for s in both:
            gs = streams[s].gs
            for g in range(GROUPS):
                at = slice(g * gs, (g + 1) * gs)
                one, two = pick(scaled_mean, s * GROUPS + g), pick(scaled_mean, 8 + s * GROUPS + g)

                for k in range(streams[s].NL // 128):
                    here = block(k, 128)
                    scaled = hg[s][at, here] * ls[s][at, here]
                    grad = inverses[s][g] * (scaled - one - nm[s][at, here] * two)
                    hb[s][at, here] = (grad * mk[s][:, here]).astype(BF16)
            got.append(narrow(streams[s], a4[s], hb[s], zs[s]))
        return got

    got = image(found)
    for s in both:
        made = [got[s](r) for r in range(streams[s].R)]
        for r in range(streams[s].R):
            es[s][:, r * streams[s].W : (r + 1) * streams[s].W] = made[r]
        put_rows(streams[s], made, xm[s].at[IMAGE])
    total(lambda s, r: own_row(s, es[s], r), TOTAL1)

    gram = [jnp.zeros((8, 128), F32) for _ in range(3)]
    for s in both:
        for r in range(streams[s].R):
            a, b = cot[s][:, r, :], own_row(s, es[s], r)
            for t, product in enumerate((a * a, a * b, b * b)):
                product = fold(product)
                for half in range(streams[s].W // 128):
                    gram[t] = gram[t] + product[:, half * 128 : (half + 1) * 128]
    pack_own(IMAGE)
    spread_wide(IMAGE, a1, kp, ring=False)
    image_sums = []
    for s in both:

        def lifted_sums(g, at, k):
            x = masked(s, k, kp[s][at, block(k, 128)])
            return x, x * nm[s][at, block(k, 128)]

        image_sums.append(group_loop(s, *ring_chunks(s), 2, lifted_sums))
    spread_wide(TOTAL1, a3, hg)
    sums, pairs = [], []
    crossed = [jnp.zeros((8, 128), F32) for _ in range(2)]
    for s in both:

        def own_sums(g, at, k):
            here = block(k, 128)
            scaled = hg[s][at, here] * ls[s][at, here]
            return scaled, scaled * nm[s][at, here]

        def pair_sums(g, at, k):
            here = block(k, 128)
            scaled = hg[s][at, here] * ls[s][at, here]
            return scaled * kc[s][at, here], scaled * kp[s][at, here]

        sums.append(group_loop(s, *own_chunks(s), 2, own_sums))
        pairs.append(group_loop(s, *ring_chunks(s), 2, pair_sums))
        for g in range(GROUPS):
            for t in range(2):
                crossed[t] = crossed[t] + pairs[s][t][g] * inverses[s][g]
    entries = flat(sums, 0) + flat(sums, 1) + flat(along, 0) + flat(along, 1) + flat(image_sums, 0) + flat(image_sums, 1)
    reduce_start(2, to_row(entries + gram + crossed))
    reduce_middle(2)
    found = reduce_end(2)

    weight = (inverse_row + roll(inverse_row, 8)) * per
    cc, c0, g00, cq, pq = [pick(found, 48 + k) for k in range(5)]
    c1 = cq - jnp.sum(found * weight * roll(found, -16), axis=1, keepdims=True)
    g01 = pq - jnp.sum(found * weight * roll(found, -32), axis=1, keepdims=True)
    d0 = jnp.maximum(cc - c0, 0.25 * cc)
    alpha = 1.0 + c0 / d0
    kappa = alpha * g00 / d0
    turn = -alpha * (c1 - c0)
    d1 = jnp.maximum(-alpha * alpha * (g01 - g00) - kappa * alpha * (c1 - c0), 0.25 * alpha * alpha * g00)
    m0 = -((1.0 - alpha) * c0 + alpha * c1)
    m1 = -alpha * ((1.0 - alpha) * g00 + alpha * g01) + kappa * m0
    by0 = 1.0 - m0 / d0 + (m1 / d1) * (turn / d0)
    by1 = alpha * (1.0 - m1 / d1)

    got = image(found)
    for s in both:
        for r in range(streams[s].R):
            outs[s][:, r, :] = cot[s][:, r, :] + by0 * own_row(s, es[s], r) + by1 * got[s](r)

    for k in range(SENT):
        exchange_end(k)
    for k in range(3):
        reduce_drain(k)


def solution(mesh):
    rows, cols = mesh.shape["row"], mesh.shape["col"]
    sizes = (rows, cols, min(rows, 8), min(cols, 4))

    def body(*args):
        fine_state, coarse_state = args[:2]
        fine_first, fine_second, coarse_first, coarse_second = args[6:10]
        f = Stream(fine_state.shape[0], fine_first.shape[1], *fine_state.shape[1:])
        c = Stream(coarse_state.shape[0], coarse_first.shape[1], *coarse_state.shape[1:])
        both = (f, c)
        args = list(args)
        for k, s in ((6, f), (8, c)):
            args[k] = args[k].transpose(0, 2, 1).reshape(9 * s.n, s.w)
            args[k + 1] = args[k + 1].reshape(3, 3 * s.n, s.w)
        args[14] = args[14].transpose(0, 1, 3, 2).reshape(4 * f.n, c.n)
        vmem = pltpu.VMEM
        scratch = []
        for shape, dtype in (
            (lambda s: (5, s.n, (s.R + 4) * s.W), BF16),
            (lambda s: (3 * s.n, (s.R + 4) * s.W), BF16),
            (lambda s: (3, 3 * s.n, 128), BF16),
            (lambda s: (s.w, s.NL), F32),
            (lambda s: (s.w, s.NL), F32),
            (lambda s: (s.w, s.NL), F32),
            (lambda s: (s.w, s.NL), BF16),
            (lambda s: (s.w, s.NL), F32),
            (lambda s: (s.w, s.NL), F32),
            (lambda s: (3 * s.n, s.cells), F32),
            (lambda s: (s.n, s.cells), F32),
            (lambda s: (s.n, s.cells), F32),
            (lambda s: (1, s.NL), F32),
            (lambda s: (s.w, 128), F32),
            (lambda s: (s.w, 128), F32),
            (lambda s: (s.w, 9 * s.n), BF16),
            (lambda s: (s.w, 9 * s.n), BF16),
            (lambda s: (3, 3 * s.n, s.w), BF16),
        ):
            scratch += [vmem(shape(s), dtype) for s in both]
        scratch += [
            vmem((128, 256), BF16),
            vmem((256, 256), BF16),
            vmem((4 * f.n, c.n), BF16),
            vmem((c.n, 4 * f.n), BF16),
            vmem((c.n, 4 * f.n), BF16),
            vmem((f.R * f.n, f.W), BF16),
            vmem((c.R * c.n, c.W), BF16),
            vmem((9 * c.n, c.w), BF16),
            vmem((5, f.n + c.n, 128), BF16),
            vmem((SENT, 2, f.n + c.n, 128), BF16),
            vmem((SENT, 2, 16, 128), BF16),
            vmem((SENT, 4, 16, 128), BF16),
            vmem((3, sizes[2] * (cols // sizes[3]), 1, 128), F32),
            vmem((3, (rows // sizes[2]) * sizes[3], 1, 128), F32),
            pltpu.SemaphoreType.DMA((SENT, 10)),
            pltpu.SemaphoreType.DMA((SENT, 10)),
            pltpu.SemaphoreType.DMA((3, 2)),
            pltpu.SemaphoreType.DMA((3, 2)),
        ]
        return pl.pallas_call(
            functools.partial(kernel, both, sizes),
            out_shape=[jax.ShapeDtypeStruct(a.shape, F32) for a in args[4:6]],
            in_specs=[pl.BlockSpec(memory_space=pltpu.VMEM)] * 16,
            out_specs=[pl.BlockSpec(memory_space=pltpu.VMEM)] * 2,
            scratch_shapes=scratch,
            compiler_params=pltpu.CompilerParams(
                collective_id=0, has_side_effects=True, vmem_limit_bytes=56 * 1024 * 1024
            ),
        )(*args)

    field = P(None, "row", "col")
    return jax.shard_map(
        body,
        mesh=mesh,
        in_specs=(field,) * 6 + (P(),) * 10,
        out_specs=(field, field),
        check_vma=False,
    )
```

```python
import functools

import jax
import jax.numpy as jnp
from jax import lax
from jax.experimental import pallas as pl
from jax.experimental.pallas import tpu as pltpu
from jax.sharding import PartitionSpec as P

GROUPS = 4
EPSILON = 1e-05
MESH = pl.DeviceIdType.MESH
F32 = jnp.float32
BF16 = jnp.bfloat16
DIRS = [(dr, dc) for dr in (-1, 0, 1) for dc in (-1, 0, 1) if dr or dc]
DIAGONALS = [(-1, -1), (-1, 1), (1, -1), (1, 1)]
STATE, TOTAL0, TOTAL1, COT, IMAGE = range(5)
SENT = 3


class Stream:
    def __init__(self, n, w, rows, cols):
        self.n, self.w, self.R, self.W = n, w, rows, cols
        self.gs = w // GROUPS
        self.main = (rows + 2) * cols
        self.NL = self.main + 128
        self.cells = rows * cols
        self.own = slice(2 * cols, 2 * cols + rows * cols)


def dot(a, b):
    return jnp.dot(a, b, preferred_element_type=F32)


def lanes_of(shape):
    return lax.broadcasted_iota(jnp.int32, shape, len(shape) - 1)


def subs_of(shape):
    return lax.broadcasted_iota(jnp.int32, shape, 0)


def roll(x, shift):
    return pltpu.roll(x, shift % x.shape[1], 1)


def wide_lanes(x, width):
    return x if width == 128 else jnp.concatenate([x] * (width // 128), axis=1)


def fold(x):
    return jnp.sum(x.reshape(x.shape[0] // 8, 8, x.shape[1]), axis=0)


def block(i, size):
    return slice(i * size, (i + 1) * size)


def swish_derivative(v):
    sigma = jax.nn.sigmoid(v)
    return sigma * (1.0 + v * (1.0 - sigma))


def to_row(accs):
    row = jnp.zeros((1, 128), F32)
    sub, lane = subs_of((8, 128)), lanes_of((8, 128))
    for first in range(0, len(accs), 8):
        stack = jnp.zeros((8, 128), F32)
        for k, acc in enumerate(accs[first : first + 8]):
            stack = jnp.where(sub == k, jnp.sum(acc, axis=0, keepdims=True), stack)
        col = jnp.sum(stack, axis=1, keepdims=True)
        row = row + jnp.sum(jnp.where(lane == sub + first, col, 0.0), axis=0, keepdims=True)
    return row


def pick(row, k):
    return jnp.sum(jnp.where(lanes_of((1, 128)) == k, row, 0.0), axis=1, keepdims=True)


def put_rows(s, rows, xm):
    for r, x in enumerate(rows):
        xm[:, (r + 2) * s.W : (r + 3) * s.W] = x.astype(BF16)


def pack(s, xm, lines):
    lane = lanes_of((s.n, 128))
    packed = jnp.zeros((s.n, 128), F32)
    for k in lines:
        left, right = xm[:, k * s.W : k * s.W + 128], xm[:, (k + 1) * s.W - 128 : (k + 1) * s.W]
        x = jnp.where(lane < 2, left.astype(F32), jnp.where(lane >= 126, right.astype(F32), 0.0))
        packed = packed + roll(x, 8 * k + 2)
    return jnp.where(lane % 8 <= 2, packed, roll(packed, 2))


def build(s, xm, edge, x3, x9, ring):
    n, W = s.n, s.W
    lane = lanes_of((n, 128))
    joined = jnp.where(lane % 8 == 0, roll(edge, -4), edge)
    lane = lanes_of((n, W))
    for k in range(s.R + 4):
        at = slice(k * W, (k + 1) * W)
        if not ring and not 2 <= k < s.R + 2:
            x3[:, at] = jnp.zeros((3 * n, W), BF16)
            continue
        x = xm[:, at]
        xf = x.astype(F32)
        t = wide_lanes(roll(joined, -(8 * k + 1)), W)
        x3[0:n, at] = jnp.where(lane == 0, t, roll(xf, 1)).astype(BF16)
        x3[n : 2 * n, at] = x
        x3[2 * n : 3 * n, at] = jnp.where(lane == W - 1, t, roll(xf, -1)).astype(BF16)
    for i in range(3):
        for j in range(3):
            x9[i, j * n : (j + 1) * n, :] = roll(edge, -(8 * i + j)).astype(BF16)


def widen(s, weights, x3, x9, out):
    taps = [x3[:, i * s.W : i * s.W + s.main] for i in range(3)]
    out[:, 0 : s.main] = dot(weights[...], jnp.concatenate(taps, axis=0))
    out[:, s.main :] = dot(weights[...], jnp.concatenate([x9[i] for i in range(3)], axis=0))


def narrow(s, weights, h, z):
    n, W = s.n, s.W
    for b in range(0, s.cells, 256):
        total = dot(weights[0], h[:, b : b + 256])
        for i in (1, 2):
            total = total + dot(weights[i], h[:, b + i * W : b + i * W + 256])
        z[0 : total.shape[0], b : b + 256] = total
    edges = [dot(weights[i], h[:, s.main :]) for i in range(3)]
    total = edges[0] + roll(edges[1], -8) + roll(edges[2], -16)
    q = lanes_of((n, 128)) % 8
    joined = []
    for g in range(0, total.shape[0], 3 * n):
        joined.append(jnp.where(q == 1, roll(total[g : g + n], 1), roll(total[g + 2 * n : g + 3 * n], -3)))
    lane = lanes_of((n, W))

    def row(r, g=0):
        at, base = slice(r * W, (r + 1) * W), 3 * n * g
        t = wide_lanes(roll(joined[g], -(8 * r + 1)), W)
        left = jnp.where(lane == 0, t, roll(z[base : base + n, at], 1))
        right = jnp.where(lane == W - 1, t, roll(z[base + 2 * n : base + 3 * n, at], -1))
        return left + z[base + n : base + 2 * n, at] + right

    return row


def kernel(streams, sizes, *refs):
    f, c = streams
    (
        fine_state, coarse_state, fine_inject, coarse_inject, fine_cot, coarse_cot,
        fine_first, fine_second, coarse_first, coarse_second,
        fine_gain, fine_shift, coarse_gain, coarse_shift, reduction, up,
        fine_out, coarse_out,
        *rest,
    ) = refs
    (xm_f, xm_c, x3_f, x3_c, x9_f, x9_c,
     nm_f, nm_c, ls_f, ls_c, hg_f, hg_c, hb_f, hb_c, kc_f, kc_c, kp_f, kp_c,
     z_f, z_c, sl_f, sl_c, e_f, e_c, zn_f, zn_c, mk_f, mk_c, ga_f, ga_c, sh_f, sh_c,
     a1_f, a1_c, a3_f, a3_c, a4_f, a4_c, ag_f, ag_c, zg_f, zg_c, one_f, one_c, two_f, two_c, dup, split, rt, rw, u4, stack_f, stack_c, taps,
     pk, pr, corner, corners, ar_a, ar_b, halo_send, halo_recv, ar_send, ar_recv) = rest
    xm, x3, x9 = (xm_f, xm_c), (x3_f, x3_c), (x9_f, x9_c)
    nm, ls, hg, hb = (nm_f, nm_c), (ls_f, ls_c), (hg_f, hg_c), (hb_f, hb_c)
    kc, kp, zs, sl, es, mk = (kc_f, kc_c), (kp_f, kp_c), (z_f, z_c), (sl_f, sl_c), (e_f, e_c), (mk_f, mk_c)
    ga, sh, a1, a3, a4 = (ga_f, ga_c), (sh_f, sh_c), (a1_f, a1_c), (a3_f, a3_c), (a4_f, a4_c)
    zn = (zn_f, zn_c)
    ag, zg, one, two = (ag_f, ag_c), (zg_f, zg_c), (one_f, one_c), (two_f, two_c)
    first, second = (fine_first, coarse_first), (fine_second, coarse_second)
    cot, state = (fine_cot, coarse_cot), (fine_state, coarse_state)
    inject, outs = (fine_inject, coarse_inject), (fine_out, coarse_out)
    rows, cols, low_rows, low_cols = sizes
    high_rows, high_cols = rows // low_rows, cols // low_cols
    row, col = lax.axis_index("row"), lax.axis_index("col")
    both = (0, 1)
    own_part = (slice(0, f.n), slice(f.n, f.n + c.n))

    def has(d):
        return (row + d[0] >= 0) & (row + d[0] < rows) & (col + d[1] >= 0) & (col + d[1] < cols)

    size_a, size_b = low_rows * high_cols, high_rows * low_cols
    me_a = (row % low_rows) * high_cols + col // low_cols
    me_b = (row // low_rows) * low_cols + col % low_cols

    def peer_a(k):
        p = (me_a + k) % size_a
        return ((row // low_rows) * low_rows + p // high_cols, (p % high_cols) * low_cols + col % low_cols)

    def peer_b(k):
        p = (me_b + k) % size_b
        return ((p // low_cols) * low_rows + row % low_rows, (col // low_cols) * low_cols + p % low_cols)

    def strips(k):
        made = []
        for s in both:
            W, R = streams[s].W, streams[s].R
            for i, d, src, dst in ((s, (-1, 0), 2 * W, (R + 2) * W), (2 + s, (1, 0), R * W, 0)):
                made.append((pltpu.make_async_remote_copy(
                    src_ref=xm[s].at[k, :, pl.ds(src, 2 * W)], dst_ref=xm[s].at[k, :, pl.ds(dst, 2 * W)],
                    send_sem=halo_send.at[k, i], recv_sem=halo_recv.at[k, i],
                    device_id=(row + d[0], col), device_id_type=MESH), d))
        return made

    def packs(k):
        made = []
        for i, dc in ((4, -1), (5, 1)):
            made.append((pltpu.make_async_remote_copy(
                src_ref=pk.at[k], dst_ref=pr.at[k, i - 4],
                send_sem=halo_send.at[k, i], recv_sem=halo_recv.at[k, i],
                device_id=(row, col + dc), device_id_type=MESH), (0, dc)))
        for i, (dr, dc) in enumerate(DIAGONALS):
            made.append((pltpu.make_async_remote_copy(
                src_ref=corner.at[k, (dr + 1) // 2], dst_ref=corners.at[k, i],
                send_sem=halo_send.at[k, 6 + i], recv_sem=halo_recv.at[k, 6 + i],
                device_id=(row + dr, col + dc), device_id_type=MESH), (dr, dc)))
        return made

    def pack_own(k):
        for s in both:
            R = streams[s].R
            pk[k, own_part[s], :] = pack(streams[s], xm[s].at[k], range(2, R + 2)).astype(BF16)

    def exchange_start(k):
        for copy, d in strips(k):
            pl.when(has(d))(copy.start)
        pack_own(k)
        own = pk[k].astype(F32)
        shift = 8 * (f.R - c.R)
        low = jnp.concatenate([own[: f.n], roll(own[f.n :], shift)], axis=0)
        lane = lanes_of(own.shape)
        cells = jnp.where(lane < 8 * (c.R + 2), own, low)
        cells = jnp.concatenate([cells, jnp.zeros((128 - f.n - c.n, 128), F32)], axis=0).T
        corner[k, 0] = cells[16:32].astype(BF16)
        corner[k, 1] = cells[8 * f.R : 8 * f.R + 16].astype(BF16)
        for copy, d in packs(k):
            pl.when(has(d))(copy.start)

    def exchange_wait(k):
        for copy, d in strips(k) + packs(k):
            pl.when(has((-d[0], -d[1])))(copy.wait_recv)

    def exchange_end(k):
        for copy, d in strips(k) + packs(k):
            pl.when(has(d))(copy.wait_send)

    def edges(k, ring):
        lane = lanes_of((f.n + c.n, 128))
        q = lane % 8
        own = pk[k].astype(F32)
        if ring:
            sides = jnp.where(q <= 1, pr[k, 1].astype(F32), jnp.where(q <= 3, own, pr[k, 0].astype(F32)))
            sub = subs_of((16, 128)) % 8
            got = [corners[k, i].astype(F32) for i in range(4)]
            above = jnp.where(sub <= 3, got[DIAGONALS.index((1, 1))], got[DIAGONALS.index((1, -1))])
            below = jnp.where(sub <= 3, got[DIAGONALS.index((-1, 1))], got[DIAGONALS.index((-1, -1))])
            low = 8 * (f.R + 2)
            blank = [jnp.zeros((low - 16, 128), F32), jnp.zeros((112 - low, 128), F32)]
            cells = jnp.concatenate([above, blank[0], below, blank[1]], axis=0).T
        else:
            sides = jnp.where((q >= 2) & (q <= 3), own, 0.0)
        made = []
        for s in both:
            n, R = streams[s].n, streams[s].R
            lane = lanes_of((n, 128))
            q = lane % 8
            outside = jnp.zeros((n, 128), F32)
            if ring:
                outer = cells[own_part[s]]
                outer = jnp.where(lane < 16, outer, roll(outer, 8 * (R - f.R)))
                lines = pack(streams[s], xm[s].at[k], (0, 1, R + 2, R + 3))
                outside = jnp.where((q >= 2) & (q <= 3), lines, outer)
            inside = (lane >= 16) & (lane < 16 + 8 * R)
            made.append(jnp.where(inside, sides[own_part[s]], outside))
        return made

    def spread(k, stage, buf, me, size, peer):
        def send(p, _):
            pltpu.make_async_remote_copy(
                src_ref=buf.at[k, me], dst_ref=buf.at[k, me],
                send_sem=ar_send.at[k, stage], recv_sem=ar_recv.at[k, stage],
                device_id=peer(p), device_id_type=MESH).start()
            return 0

        lax.fori_loop(1, size, send, 0)

    def collect(k, stage, buf, size):
        ref = buf.at[k, pl.ds(0, size - 1)]
        pltpu.make_async_copy(ref, ref, ar_recv.at[k, stage]).wait()
        return jnp.sum(buf[k], axis=0)

    def reduce_start(k, value):
        ar_a[k, me_a] = value
        spread(k, 0, ar_a, me_a, size_a, peer_a)

    def reduce_middle(k):
        ar_b[k, me_b] = collect(k, 0, ar_a, size_a)
        spread(k, 1, ar_b, me_b, size_b, peer_b)

    def reduce_end(k):
        return collect(k, 1, ar_b, size_b)

    def reduce_drain(k):
        for stage, buf, size in ((0, ar_a, size_a), (1, ar_b, size_b)):
            ref = buf.at[k, pl.ds(0, size - 1)]
            pltpu.make_async_copy(ref, ref, ar_send.at[k, stage]).wait()

    for s in both:
        W, R = streams[s].W, streams[s].R
        for k in range(SENT):
            xm[s][k, :, 0 : 2 * W] = jnp.zeros((streams[s].n, 2 * W), BF16)
            xm[s][k, :, (R + 2) * W : (R + 4) * W] = jnp.zeros((streams[s].n, 2 * W), BF16)
    pr[...] = jnp.zeros(pr.shape, BF16)
    corners[...] = jnp.zeros(corners.shape, BF16)
    barrier = pltpu.get_barrier_semaphore()

    def greet(device):
        pl.semaphore_signal(barrier, inc=1, device_id=device, device_id_type=MESH)

    for d in DIRS:
        pl.when(has(d))(functools.partial(greet, (row + d[0], col + d[1])))

    def greet_a(k, _):
        greet(peer_a(k))
        return 0

    def greet_b(k, _):
        greet(peer_b(k))
        return 0

    lax.fori_loop(1, size_a, greet_a, 0)
    lax.fori_loop(1, size_b, greet_b, 0)
    for s in both:
        put_rows(streams[s], [state[s][:, r, :] for r in range(streams[s].R)], xm[s].at[STATE])
    beside = sum(has(d).astype(jnp.int32) for d in DIRS)
    pl.semaphore_wait(barrier, beside + (size_a + size_b - 2))
    exchange_start(STATE)
    for s in both:
        put_rows(streams[s], [cot[s][:, r, :] for r in range(streams[s].R)], xm[s].at[COT])
    pack_own(COT)

    for s in both:
        n, w, W = streams[s].n, streams[s].w, streams[s].W
        for t in range(9):
            back = slice((8 - t) * n, (9 - t) * n)
            a4[s][(8 - t) // 3, (8 - t) % 3 * n : ((8 - t) % 3 + 1) * n, :] = first[s][t * n : (t + 1) * n, :]
            taps[back, 0:w] = second[s][t // 3, (t % 3) * n : (t % 3 + 1) * n, :]
        group = lanes_of((1, w)) // streams[s].gs
        for g in range(GROUPS):
            chosen = jnp.where(group == g, 1.0, 0.0).astype(BF16)
            for i in range(3):
                ag[s][i, 3 * n * g : 3 * n * (g + 1), :] = a4[s][i] * chosen
        a1[s][...] = first[s][...].T
        a3[s][...] = taps[0 : 9 * n, 0:w].T
        same = subs_of((w, w)) == lanes_of((w, w))
        for src, dst in (((fine_gain, coarse_gain)[s], ga[s]), ((fine_shift, coarse_shift)[s], sh[s])):
            dst[...] = jnp.broadcast_to(jnp.sum(jnp.where(same, src[...][None, :], 0.0), axis=1, keepdims=True), (w, 128))
        R = streams[s].R
        mk[s][...] = jnp.ones((1, streams[s].NL), F32)
        mk[s][:, 0:W] = jnp.where(row > 0, 1.0, 0.0) * jnp.ones((1, W), F32)
        mk[s][:, (R + 1) * W : (R + 2) * W] = jnp.where(row < rows - 1, 1.0, 0.0) * jnp.ones((1, W), F32)
        lane = lanes_of((1, 128))
        q, line = lane % 8, lane // 8
        good = ((q == 0) & (col > 0)) | ((q == 3) & (col < cols - 1))
        good = good & (line < R + 2) & ((line > 0) | (row > 0)) & ((line < R + 1) | (row < rows - 1))
        mk[s][:, streams[s].main :] = jnp.where(good, 1.0, 0.0)
    here, there = subs_of((128, 256)), lanes_of((128, 256))
    dup[...] = jnp.where(there // 2 == here, 1.0, 0.0).astype(BF16)
    here, there = subs_of((256, 256)), lanes_of((256, 256))
    split[...] = jnp.where(here == 2 * (there % 128) + there // 128, 1.0, 0.0).astype(BF16)
    for a in range(2):
        for b in range(2):
            at = slice((2 * a + b) * f.n, (2 * a + b + 1) * f.n)
            rt[at, :] = reduction[at, :]
            taps[at, 0 : c.n] = up[...]
    rw[...] = rt[...].T
    u4[...] = taps[0 : 4 * f.n, 0 : c.n].T

    def spread_wide(k, weights, outs, ring=True):
        if ring:
            exchange_wait(k)
        tiles = edges(k, ring)
        for s in both:
            build(streams[s], xm[s].at[k], tiles[s], x3[s], x9[s], ring)
            widen(streams[s], weights[s], x3[s], x9[s], outs[s])

    def masked(s, k, x):
        W, R = streams[s].W, streams[s].R
        return x if W <= 128 * k < (R + 1) * W else x * mk[s][:, block(k, 128)]

    def group_loop(s, start, chunks, count, body):
        gs = streams[s].gs
        sums = []
        for g in range(GROUPS):
            at = slice(g * gs, (g + 1) * gs)

            accs = [jnp.zeros((8, 128), F32)] * count
            for k in range(start, start + chunks):
                accs = [a + fold(t) for a, t in zip(accs, body(g, at, k))]
            sums.append(accs)
        return [[sums[g][t] for g in range(GROUPS)] for t in range(count)]

    def ring_chunks(s):
        return 0, streams[s].NL // 128

    def own_chunks(s):
        return streams[s].W // 128, streams[s].cells // 128

    def flat(per_stream, t):
        return [a for s in both for a in per_stream[s][t]]

    sums = []
    spread_wide(STATE, a1, nm)
    for s in both:

        def squares(g, at, k):
            x = nm[s][at, block(k, 128)]
            return x, x * x

        sums.append(group_loop(s, *own_chunks(s), 2, squares))
    reduce_start(0, to_row(flat(sums, 0) + flat(sums, 1)))
    spread_wide(COT, a1, kc, ring=False)

    def group_images(fields):
        for s in both:
            got = narrow(streams[s], ag[s], hb[s], zg[s])
            for g in range(GROUPS):
                for r in range(streams[s].R):
                    fields[s][g, :, r * streams[s].W : (r + 1) * streams[s].W] = got(r, g)

    reduce_middle(0)
    for s in both:
        hb[s][...] = jnp.broadcast_to(mk[s][...], hb[s].shape).astype(BF16)
    group_images(one)
    stats = reduce_end(0)

    lane = lanes_of((1, 128))
    counts = [rows * cols * streams[s].cells * streams[s].gs for s in both]
    per = jnp.where(lane % 8 < GROUPS, 1.0 / counts[0], 1.0 / counts[1])
    mean_row = stats * per
    variance = roll(mean_row, -8) - mean_row * mean_row
    inverse_row = jnp.where(lane < 8, lax.rsqrt(variance + EPSILON), 0.0)
    weight = (inverse_row + roll(inverse_row, 8)) * per
    means = [[pick(mean_row, s * GROUPS + g) for g in range(GROUPS)] for s in both]
    inverses = [[pick(inverse_row, s * GROUPS + g) for g in range(GROUPS)] for s in both]

    for s in both:
        gs = streams[s].gs
        for g in range(GROUPS):
            at = slice(g * gs, (g + 1) * gs)

            for k in range(streams[s].NL // 128):
                here = block(k, 128)
                gain, keep = ga[s][at, :], mk[s][:, here]
                normed = (nm[s][at, here] - means[s][g]) * inverses[s][g]
                level = normed * gain + sh[s][at, :]
                sigma = jax.nn.sigmoid(level)
                nm[s][at, here] = normed
                hb[s][at, here] = (level * sigma * keep).astype(BF16)
                ls[s][at, here] = sigma * (1.0 + level * (1.0 - sigma)) * gain * keep

    def own_row(s, ref, r):
        return ref[:, r * streams[s].W : (r + 1) * streams[s].W]

    def halve():
        parts = dot(stack_f[...], split[...]).astype(BF16)
        lined = []
        for R in range(c.R):
            lined.append(jnp.concatenate([
                parts[(2 * R + a) * f.n : (2 * R + a + 1) * f.n, b * 128 : (b + 1) * 128]
                for a in range(2) for b in range(2)], axis=0))
        return jnp.concatenate(lined, axis=1)

    def double():
        return dot(stack_c[...], dup[...]).astype(BF16)

    for s, stack in ((0, stack_f), (1, stack_c)):
        n = streams[s].n
        got = narrow(streams[s], second[s], hb[s], zs[s])
        for r in range(streams[s].R):
            mixed = got(r) + inject[s][:, r, :].astype(F32)
            sl[s][:, r * streams[s].W : (r + 1) * streams[s].W] = mixed
            stack[r * n : (r + 1) * n, :] = mixed.astype(BF16)
    down = dot(rw[...], halve())
    wide = double()
    for R in range(c.R):
        lifted = dot(up[...], wide[R * c.n : (R + 1) * c.n, :])
        for r in (2 * R, 2 * R + 1):
            at = slice(r * f.W, (r + 1) * f.W)
            sl_f[:, at] = swish_derivative(sl_f[:, at] + lifted)
    sl_c[...] = swish_derivative(sl_c[...] + down)

    def total(field, k):
        for r in range(f.R):
            stack_f[r * f.n : (r + 1) * f.n, :] = (field(0, r) * own_row(0, sl_f, r)).astype(BF16)
        coarse_grads = [field(1, r) * own_row(1, sl_c, r) for r in range(c.R)]
        for r in range(c.R):
            stack_c[r * c.n : (r + 1) * c.n, :] = coarse_grads[r].astype(BF16)
        raised = dot(u4[...], halve())
        put_rows(c, [coarse_grads[r] + own_row(1, raised, r) for r in range(c.R)], xm_c.at[k])
        wide = double()
        even = lanes_of((f.n, f.W)) % 2 == 0
        fine = []
        for R in range(c.R):
            spread_out = dot(rt[...], wide[R * c.n : (R + 1) * c.n, :])
            for a in range(2):
                part = [spread_out[(2 * a + b) * f.n : (2 * a + b + 1) * f.n] for b in range(2)]
                r = 2 * R + a
                fine.append(field(0, r) * own_row(0, sl_f, r) + jnp.where(even, part[0], part[1]))
        put_rows(f, fine, xm_f.at[k])
        exchange_start(k)

    total(lambda s, r: cot[s][:, r, :], TOTAL0)

    sums = []
    spread_wide(TOTAL0, a3, hg, ring=False)
    for s in both:

        def pushed(g, at, k):
            scaled = hg[s][at, block(k, 128)] * ls[s][at, block(k, 128)]
            return scaled, scaled * nm[s][at, block(k, 128)]

        sums.append(group_loop(s, *ring_chunks(s), 2, pushed))
    reduce_start(1, to_row(flat(sums, 0) + flat(sums, 1)))

    for s in both:
        for g in range(GROUPS):
            at = slice(g * streams[s].gs, (g + 1) * streams[s].gs)
            for k in range(streams[s].NL // 128):
                hb[s][at, block(k, 128)] = masked(s, k, nm[s][at, block(k, 128)]).astype(BF16)
    group_images(two)

    reduce_middle(1)
    spread_wide(TOTAL0, a3, hg)
    along = []
    for s in both:

        def cot_sums(g, at, k):
            x = masked(s, k, kc[s][at, block(k, 128)])
            return x, x * nm[s][at, block(k, 128)]

        along.append(group_loop(s, *ring_chunks(s), 2, cot_sums))

    def uncentred():
        for s in both:
            gs = streams[s].gs
            for g in range(GROUPS):
                at = slice(g * gs, (g + 1) * gs)
                for k in range(streams[s].NL // 128):
                    here = block(k, 128)
                    hb[s][at, here] = (inverses[s][g] * (hg[s][at, here] * ls[s][at, here])).astype(BF16)
            got = narrow(streams[s], a4[s], hb[s], zs[s])
            for r in range(streams[s].R):
                zn[s][:, r * streams[s].W : (r + 1) * streams[s].W] = got(r)

    def centred(row_sums):
        scaled_mean = row_sums * weight
        picked = [[[pick(scaled_mean, 8 * t + s * GROUPS + g) for g in range(GROUPS)] for t in range(2)] for s in both]

        def rows_of(s, r):
            at = slice(r * streams[s].W, (r + 1) * streams[s].W)
            value = zn[s][:, at]
            for g in range(GROUPS):
                value = value - picked[s][0][g] * one[s][g, :, at] - picked[s][1][g] * two[s][g, :, at]
            return value

        return rows_of

    uncentred()
    rows_of = centred(reduce_end(1))
    for s in both:
        for r in range(streams[s].R):
            es[s][:, r * streams[s].W : (r + 1) * streams[s].W] = rows_of(s, r)
        put_rows(streams[s], [own_row(s, es[s], r) for r in range(streams[s].R)], xm[s].at[IMAGE])
    total(lambda s, r: own_row(s, es[s], r), TOTAL1)

    gram = [jnp.zeros((8, 128), F32) for _ in range(3)]
    for s in both:
        for r in range(streams[s].R):
            a, b = cot[s][:, r, :], own_row(s, es[s], r)
            for t, product in enumerate((a * a, a * b, b * b)):
                product = fold(product)
                for half in range(streams[s].W // 128):
                    gram[t] = gram[t] + product[:, half * 128 : (half + 1) * 128]
    pack_own(IMAGE)
    spread_wide(IMAGE, a1, kp, ring=False)
    image_sums = []
    for s in both:

        def lifted_sums(g, at, k):
            x = masked(s, k, kp[s][at, block(k, 128)])
            return x, x * nm[s][at, block(k, 128)]

        image_sums.append(group_loop(s, *ring_chunks(s), 2, lifted_sums))
    spread_wide(TOTAL1, a3, hg)
    sums, pairs = [], []
    crossed = [jnp.zeros((8, 128), F32) for _ in range(2)]
    for s in both:

        def own_sums(g, at, k):
            here = block(k, 128)
            scaled = hg[s][at, here] * ls[s][at, here]
            return scaled, scaled * nm[s][at, here]

        def pair_sums(g, at, k):
            here = block(k, 128)
            scaled = hg[s][at, here] * ls[s][at, here]
            return scaled * kc[s][at, here], scaled * kp[s][at, here]

        sums.append(group_loop(s, *own_chunks(s), 2, own_sums))
        pairs.append(group_loop(s, *ring_chunks(s), 2, pair_sums))
        for g in range(GROUPS):
            for t in range(2):
                crossed[t] = crossed[t] + pairs[s][t][g] * inverses[s][g]
    entries = flat(sums, 0) + flat(sums, 1) + flat(along, 0) + flat(along, 1) + flat(image_sums, 0) + flat(image_sums, 1)
    reduce_start(2, to_row(entries + gram + crossed))
    uncentred()
    reduce_middle(2)
    found = reduce_end(2)

    cc, c0, g00, cq, pq = [pick(found, 48 + k) for k in range(5)]
    c1 = cq - jnp.sum(found * weight * roll(found, -16), axis=1, keepdims=True)
    g01 = pq - jnp.sum(found * weight * roll(found, -32), axis=1, keepdims=True)
    d0 = jnp.maximum(cc - c0, 0.25 * cc)
    alpha = 1.0 + c0 / d0
    kappa = alpha * g00 / d0
    turn = -alpha * (c1 - c0)
    d1 = jnp.maximum(-alpha * alpha * (g01 - g00) - kappa * alpha * (c1 - c0), 0.25 * alpha * alpha * g00)
    m0 = -((1.0 - alpha) * c0 + alpha * c1)
    m1 = -alpha * ((1.0 - alpha) * g00 + alpha * g01) + kappa * m0
    by0 = 1.0 - m0 / d0 + (m1 / d1) * (turn / d0)
    by1 = alpha * (1.0 - m1 / d1)

    rows_of = centred(found)
    for s in both:
        for r in range(streams[s].R):
            outs[s][:, r, :] = cot[s][:, r, :] + by0 * own_row(s, es[s], r) + by1 * rows_of(s, r)

    for k in range(SENT):
        exchange_end(k)
    for k in range(3):
        reduce_drain(k)


def solution(mesh):
    rows, cols = mesh.shape["row"], mesh.shape["col"]
    sizes = (rows, cols, min(rows, 8), min(cols, 4))

    def body(*args):
        fine_state, coarse_state = args[:2]
        fine_first, fine_second, coarse_first, coarse_second = args[6:10]
        f = Stream(fine_state.shape[0], fine_first.shape[1], *fine_state.shape[1:])
        c = Stream(coarse_state.shape[0], coarse_first.shape[1], *coarse_state.shape[1:])
        both = (f, c)
        args = list(args)
        for k, s in ((6, f), (8, c)):
            args[k] = args[k].transpose(0, 2, 1).reshape(9 * s.n, s.w)
            args[k + 1] = args[k + 1].reshape(3, 3 * s.n, s.w)
        args[14] = args[14].transpose(0, 1, 3, 2).reshape(4 * f.n, c.n)
        vmem = pltpu.VMEM
        scratch = []
        for shape, dtype in (
            (lambda s: (5, s.n, (s.R + 4) * s.W), BF16),
            (lambda s: (3 * s.n, (s.R + 4) * s.W), BF16),
            (lambda s: (3, 3 * s.n, 128), BF16),
            (lambda s: (s.w, s.NL), F32),
            (lambda s: (s.w, s.NL), F32),
            (lambda s: (s.w, s.NL), F32),
            (lambda s: (s.w, s.NL), BF16),
            (lambda s: (s.w, s.NL), F32),
            (lambda s: (s.w, s.NL), F32),
            (lambda s: (3 * s.n, s.cells), F32),
            (lambda s: (s.n, s.cells), F32),
            (lambda s: (s.n, s.cells), F32),
            (lambda s: (s.n, s.cells), F32),
            (lambda s: (1, s.NL), F32),
            (lambda s: (s.w, 128), F32),
            (lambda s: (s.w, 128), F32),
            (lambda s: (s.w, 9 * s.n), BF16),
            (lambda s: (s.w, 9 * s.n), BF16),
            (lambda s: (3, 3 * s.n, s.w), BF16),
            (lambda s: (3, GROUPS * 3 * s.n, s.w), BF16),
            (lambda s: (GROUPS * 3 * s.n, s.cells), F32),
            (lambda s: (GROUPS, s.n, s.cells), F32),
            (lambda s: (GROUPS, s.n, s.cells), F32),
        ):
            scratch += [vmem(shape(s), dtype) for s in both]
        scratch += [
            vmem((128, 256), BF16),
            vmem((256, 256), BF16),
            vmem((4 * f.n, c.n), BF16),
            vmem((c.n, 4 * f.n), BF16),
            vmem((c.n, 4 * f.n), BF16),
            vmem((f.R * f.n, f.W), BF16),
            vmem((c.R * c.n, c.W), BF16),
            vmem((9 * c.n, c.w), BF16),
            vmem((5, f.n + c.n, 128), BF16),
            vmem((SENT, 2, f.n + c.n, 128), BF16),
            vmem((SENT, 2, 16, 128), BF16),
            vmem((SENT, 4, 16, 128), BF16),
            vmem((3, sizes[2] * (cols // sizes[3]), 1, 128), F32),
            vmem((3, (rows // sizes[2]) * sizes[3], 1, 128), F32),
            pltpu.SemaphoreType.DMA((SENT, 10)),
            pltpu.SemaphoreType.DMA((SENT, 10)),
            pltpu.SemaphoreType.DMA((3, 2)),
            pltpu.SemaphoreType.DMA((3, 2)),
        ]
        return pl.pallas_call(
            functools.partial(kernel, both, sizes),
            out_shape=[jax.ShapeDtypeStruct(a.shape, F32) for a in args[4:6]],
            in_specs=[pl.BlockSpec(memory_space=pltpu.VMEM)] * 16,
            out_specs=[pl.BlockSpec(memory_space=pltpu.VMEM)] * 2,
            scratch_shapes=scratch,
            compiler_params=pltpu.CompilerParams(
                collective_id=0, has_side_effects=True, vmem_limit_bytes=56 * 1024 * 1024
            ),
        )(*args)
    field = P(None, "row", "col")
    return jax.shard_map(
        body,
        mesh=mesh,
        in_specs=(field,) * 6 + (P(),) * 10,
        out_specs=(field, field),
        check_vma=False,
    )
```

```python
import functools

import jax
import jax.numpy as jnp
from jax import lax
from jax.experimental import pallas as pl
from jax.experimental.pallas import tpu as pltpu
from jax.sharding import PartitionSpec as P

GROUPS = 4
EPSILON = 1e-05
MESH = pl.DeviceIdType.MESH
F32 = jnp.float32
BF16 = jnp.bfloat16
DIRS = [(dr, dc) for dr in (-1, 0, 1) for dc in (-1, 0, 1) if dr or dc]
DIAGONALS = [(-1, -1), (-1, 1), (1, -1), (1, 1)]
STATE, TOTAL0, TOTAL1, COT, IMAGE = range(5)
SENT = 3


class Stream:
    def __init__(self, n, w, rows, cols):
        self.n, self.w, self.R, self.W = n, w, rows, cols
        self.gs = w // GROUPS
        self.main = (rows + 2) * cols
        self.NL = self.main + 128
        self.cells = rows * cols
        self.own = slice(2 * cols, 2 * cols + rows * cols)


def dot(a, b):
    return jnp.dot(a, b, preferred_element_type=F32)


def lanes_of(shape):
    return lax.broadcasted_iota(jnp.int32, shape, len(shape) - 1)


def subs_of(shape):
    return lax.broadcasted_iota(jnp.int32, shape, 0)


def roll(x, shift):
    return pltpu.roll(x, shift % x.shape[1], 1)


def wide_lanes(x, width):
    return x if width == 128 else jnp.concatenate([x] * (width // 128), axis=1)


def fold(x):
    return jnp.sum(x.reshape(x.shape[0] // 8, 8, x.shape[1]), axis=0)


def block(i, size):
    return slice(i * size, (i + 1) * size)


def swish_derivative(v):
    sigma = jax.nn.sigmoid(v)
    return sigma * (1.0 + v * (1.0 - sigma))


def to_row(accs):
    row = jnp.zeros((1, 128), F32)
    sub, lane = subs_of((8, 128)), lanes_of((8, 128))
    for first in range(0, len(accs), 8):
        stack = jnp.zeros((8, 128), F32)
        for k, acc in enumerate(accs[first : first + 8]):
            stack = jnp.where(sub == k, jnp.sum(acc, axis=0, keepdims=True), stack)
        col = jnp.sum(stack, axis=1, keepdims=True)
        row = row + jnp.sum(jnp.where(lane == sub + first, col, 0.0), axis=0, keepdims=True)
    return row


def pick(row, k):
    return jnp.sum(jnp.where(lanes_of((1, 128)) == k, row, 0.0), axis=1, keepdims=True)


def put_rows(s, rows, xm):
    for r, x in enumerate(rows):
        xm[:, (r + 2) * s.W : (r + 3) * s.W] = x.astype(BF16)


def pack(s, xm, lines):
    lane = lanes_of((s.n, 128))
    packed = jnp.zeros((s.n, 128), F32)
    for k in lines:
        left, right = xm[:, k * s.W : k * s.W + 128], xm[:, (k + 1) * s.W - 128 : (k + 1) * s.W]
        x = jnp.where(lane < 2, left.astype(F32), jnp.where(lane >= 126, right.astype(F32), 0.0))
        packed = packed + roll(x, 8 * k + 2)
    return jnp.where(lane % 8 <= 2, packed, roll(packed, 2))


def build(s, xm, edge, x3, x9, ring):
    n, W = s.n, s.W
    lane = lanes_of((n, 128))
    joined = jnp.where(lane % 8 == 0, roll(edge, -4), edge)
    lane = lanes_of((n, W))
    for k in range(s.R + 4):
        at = slice(k * W, (k + 1) * W)
        if not ring and not 2 <= k < s.R + 2:
            x3[:, at] = jnp.zeros((3 * n, W), BF16)
            continue
        x = xm[:, at]
        xf = x.astype(F32)
        t = wide_lanes(roll(joined, -(8 * k + 1)), W)
        x3[0:n, at] = jnp.where(lane == 0, t, roll(xf, 1)).astype(BF16)
        x3[n : 2 * n, at] = x
        x3[2 * n : 3 * n, at] = jnp.where(lane == W - 1, t, roll(xf, -1)).astype(BF16)
    for i in range(3):
        for j in range(3):
            x9[i, j * n : (j + 1) * n, :] = roll(edge, -(8 * i + j)).astype(BF16)


def widen(s, weights, x3, x9, out):
    taps = [x3[:, i * s.W : i * s.W + s.main] for i in range(3)]
    out[:, 0 : s.main] = dot(weights[...], jnp.concatenate(taps, axis=0))
    out[:, s.main :] = dot(weights[...], jnp.concatenate([x9[i] for i in range(3)], axis=0))


def narrow(s, weights, h, z):
    n, W = s.n, s.W
    for b in range(0, s.cells, 256):
        total = dot(weights[0], h[:, b : b + 256])
        for i in (1, 2):
            total = total + dot(weights[i], h[:, b + i * W : b + i * W + 256])
        z[0 : total.shape[0], b : b + 256] = total
    edges = [dot(weights[i], h[:, s.main :]) for i in range(3)]
    total = edges[0] + roll(edges[1], -8) + roll(edges[2], -16)
    q = lanes_of((n, 128)) % 8
    joined = []
    for g in range(0, total.shape[0], 3 * n):
        joined.append(jnp.where(q == 1, roll(total[g : g + n], 1), roll(total[g + 2 * n : g + 3 * n], -3)))
    lane = lanes_of((n, W))

    def row(r, g=0):
        at, base = slice(r * W, (r + 1) * W), 3 * n * g
        t = wide_lanes(roll(joined[g], -(8 * r + 1)), W)
        left = jnp.where(lane == 0, t, roll(z[base : base + n, at], 1))
        right = jnp.where(lane == W - 1, t, roll(z[base + 2 * n : base + 3 * n, at], -1))
        return left + z[base + n : base + 2 * n, at] + right

    return row


def kernel(streams, sizes, *refs):
    f, c = streams
    far, refs = refs[:10], refs[10:]
    (
        fine_gain, fine_shift, coarse_gain, coarse_shift, reduction, up,
        fine_out, coarse_out,
        *rest,
    ) = refs
    near, load_sem, rest = rest[:10], rest[10], rest[11:]
    (
        fine_state, coarse_state, fine_inject, coarse_inject, fine_cot, coarse_cot,
        fine_first, fine_second, coarse_first, coarse_second,
    ) = near
    (xm_f, xm_c, x3_f, x3_c, x9_f, x9_c,
     nm_f, nm_c, ls_f, ls_c, hg_f, hg_c, hb_f, hb_c, kc_f, kc_c, kp_f, kp_c,
     z_f, z_c, sl_f, sl_c, e_f, e_c, zn_f, zn_c, mk_f, mk_c, ga_f, ga_c, sh_f, sh_c,
     a1_f, a1_c, a3_f, a3_c, a4_f, a4_c, ag_f, ag_c, zg_f, zg_c, one_f, one_c, two_f, two_c, dup, split, rt, rw, u4, stack_f, stack_c, taps,
     pk, pr, corner, corners, ar_a, ar_b, halo_send, halo_recv, ar_send, ar_recv) = rest
    xm, x3, x9 = (xm_f, xm_c), (x3_f, x3_c), (x9_f, x9_c)
    nm, ls, hg, hb = (nm_f, nm_c), (ls_f, ls_c), (hg_f, hg_c), (hb_f, hb_c)
    kc, kp, zs, sl, es, mk = (kc_f, kc_c), (kp_f, kp_c), (z_f, z_c), (sl_f, sl_c), (e_f, e_c), (mk_f, mk_c)
    ga, sh, a1, a3, a4 = (ga_f, ga_c), (sh_f, sh_c), (a1_f, a1_c), (a3_f, a3_c), (a4_f, a4_c)
    zn = (zn_f, zn_c)
    ag, zg, one, two = (ag_f, ag_c), (zg_f, zg_c), (one_f, one_c), (two_f, two_c)
    first, second = (fine_first, coarse_first), (fine_second, coarse_second)
    cot, state = (fine_cot, coarse_cot), (fine_state, coarse_state)
    inject, outs = (fine_inject, coarse_inject), (fine_out, coarse_out)
    rows, cols, low_rows, low_cols = sizes
    high_rows, high_cols = rows // low_rows, cols // low_cols
    row, col = lax.axis_index("row"), lax.axis_index("col")
    both = (0, 1)
    own_part = (slice(0, f.n), slice(f.n, f.n + c.n))

    def has(d):
        return (row + d[0] >= 0) & (row + d[0] < rows) & (col + d[1] >= 0) & (col + d[1] < cols)

    size_a, size_b = low_rows * high_cols, high_rows * low_cols
    me_a = (row % low_rows) * high_cols + col // low_cols
    me_b = (row // low_rows) * low_cols + col % low_cols

    def peer_a(k):
        p = (me_a + k) % size_a
        return ((row // low_rows) * low_rows + p // high_cols, (p % high_cols) * low_cols + col % low_cols)

    def peer_b(k):
        p = (me_b + k) % size_b
        return ((p // low_cols) * low_rows + row % low_rows, (col // low_cols) * low_cols + p % low_cols)

    def strips(k):
        made = []
        for s in both:
            W, R = streams[s].W, streams[s].R
            for i, d, src, dst in ((s, (-1, 0), 2 * W, (R + 2) * W), (2 + s, (1, 0), R * W, 0)):
                made.append((pltpu.make_async_remote_copy(
                    src_ref=xm[s].at[k, :, pl.ds(src, 2 * W)], dst_ref=xm[s].at[k, :, pl.ds(dst, 2 * W)],
                    send_sem=halo_send.at[k, i], recv_sem=halo_recv.at[k, i],
                    device_id=(row + d[0], col), device_id_type=MESH), d))
        return made

    def packs(k):
        made = []
        for i, dc in ((4, -1), (5, 1)):
            made.append((pltpu.make_async_remote_copy(
                src_ref=pk.at[k], dst_ref=pr.at[k, i - 4],
                send_sem=halo_send.at[k, i], recv_sem=halo_recv.at[k, i],
                device_id=(row, col + dc), device_id_type=MESH), (0, dc)))
        for i, (dr, dc) in enumerate(DIAGONALS):
            made.append((pltpu.make_async_remote_copy(
                src_ref=corner.at[k, (dr + 1) // 2], dst_ref=corners.at[k, i],
                send_sem=halo_send.at[k, 6 + i], recv_sem=halo_recv.at[k, 6 + i],
                device_id=(row + dr, col + dc), device_id_type=MESH), (dr, dc)))
        return made

    def pack_own(k):
        for s in both:
            R = streams[s].R
            pk[k, own_part[s], :] = pack(streams[s], xm[s].at[k], range(2, R + 2)).astype(BF16)

    def exchange_start(k):
        for copy, d in strips(k):
            pl.when(has(d))(copy.start)
        pack_own(k)
        own = pk[k].astype(F32)
        shift = 8 * (f.R - c.R)
        low = jnp.concatenate([own[: f.n], roll(own[f.n :], shift)], axis=0)
        lane = lanes_of(own.shape)
        cells = jnp.where(lane < 8 * (c.R + 2), own, low)
        cells = jnp.concatenate([cells, jnp.zeros((128 - f.n - c.n, 128), F32)], axis=0).T
        corner[k, 0] = cells[16:32].astype(BF16)
        corner[k, 1] = cells[8 * f.R : 8 * f.R + 16].astype(BF16)
        for copy, d in packs(k):
            pl.when(has(d))(copy.start)

    def exchange_wait(k):
        for copy, d in strips(k) + packs(k):
            pl.when(has((-d[0], -d[1])))(copy.wait_recv)

    def exchange_end(k):
        for copy, d in strips(k) + packs(k):
            pl.when(has(d))(copy.wait_send)

    def edges(k, ring):
        lane = lanes_of((f.n + c.n, 128))
        q = lane % 8
        own = pk[k].astype(F32)
        if ring:
            sides = jnp.where(q <= 1, pr[k, 1].astype(F32), jnp.where(q <= 3, own, pr[k, 0].astype(F32)))
            sub = subs_of((16, 128)) % 8
            got = [corners[k, i].astype(F32) for i in range(4)]
            above = jnp.where(sub <= 3, got[DIAGONALS.index((1, 1))], got[DIAGONALS.index((1, -1))])
            below = jnp.where(sub <= 3, got[DIAGONALS.index((-1, 1))], got[DIAGONALS.index((-1, -1))])
            low = 8 * (f.R + 2)
            blank = [jnp.zeros((low - 16, 128), F32), jnp.zeros((112 - low, 128), F32)]
            cells = jnp.concatenate([above, blank[0], below, blank[1]], axis=0).T
        else:
            sides = jnp.where((q >= 2) & (q <= 3), own, 0.0)
        made = []
        for s in both:
            n, R = streams[s].n, streams[s].R
            lane = lanes_of((n, 128))
            q = lane % 8
            outside = jnp.zeros((n, 128), F32)
            if ring:
                outer = cells[own_part[s]]
                outer = jnp.where(lane < 16, outer, roll(outer, 8 * (R - f.R)))
                lines = pack(streams[s], xm[s].at[k], (0, 1, R + 2, R + 3))
                outside = jnp.where((q >= 2) & (q <= 3), lines, outer)
            inside = (lane >= 16) & (lane < 16 + 8 * R)
            made.append(jnp.where(inside, sides[own_part[s]], outside))
        return made

    def spread(k, stage, buf, me, size, peer):
        def send(p, _):
            pltpu.make_async_remote_copy(
                src_ref=buf.at[k, me], dst_ref=buf.at[k, me],
                send_sem=ar_send.at[k, stage], recv_sem=ar_recv.at[k, stage],
                device_id=peer(p), device_id_type=MESH).start()
            return 0

        lax.fori_loop(1, size, send, 0)

    def collect(k, stage, buf, size):
        ref = buf.at[k, pl.ds(0, size - 1)]
        pltpu.make_async_copy(ref, ref, ar_recv.at[k, stage]).wait()
        return jnp.sum(buf[k], axis=0)

    def reduce_start(k, value):
        ar_a[k, me_a] = value
        spread(k, 0, ar_a, me_a, size_a, peer_a)

    def reduce_middle(k):
        ar_b[k, me_b] = collect(k, 0, ar_a, size_a)
        spread(k, 1, ar_b, me_b, size_b, peer_b)

    def reduce_end(k):
        return collect(k, 1, ar_b, size_b)

    def reduce_drain(k):
        for stage, buf, size in ((0, ar_a, size_a), (1, ar_b, size_b)):
            ref = buf.at[k, pl.ds(0, size - 1)]
            pltpu.make_async_copy(ref, ref, ar_send.at[k, stage]).wait()

    loads = [pltpu.make_async_copy(a, b, load_sem.at[k]) for k, (a, b) in enumerate(zip(far, near))]
    for copy in loads:
        copy.start()
    for s in both:
        W, R = streams[s].W, streams[s].R
        for k in range(SENT):
            xm[s][k, :, 0 : 2 * W] = jnp.zeros((streams[s].n, 2 * W), BF16)
            xm[s][k, :, (R + 2) * W : (R + 4) * W] = jnp.zeros((streams[s].n, 2 * W), BF16)
    pr[...] = jnp.zeros(pr.shape, BF16)
    corners[...] = jnp.zeros(corners.shape, BF16)
    barrier = pltpu.get_barrier_semaphore()

    def greet(device):
        pl.semaphore_signal(barrier, inc=1, device_id=device, device_id_type=MESH)

    for d in DIRS:
        pl.when(has(d))(functools.partial(greet, (row + d[0], col + d[1])))

    def greet_a(k, _):
        greet(peer_a(k))
        return 0

    def greet_b(k, _):
        greet(peer_b(k))
        return 0

    lax.fori_loop(1, size_a, greet_a, 0)
    lax.fori_loop(1, size_b, greet_b, 0)
    for copy in loads[:2]:
        copy.wait()
    for s in both:
        put_rows(streams[s], [state[s][:, r, :] for r in range(streams[s].R)], xm[s].at[STATE])
    beside = sum(has(d).astype(jnp.int32) for d in DIRS)
    pl.semaphore_wait(barrier, beside + (size_a + size_b - 2))
    exchange_start(STATE)
    for copy in loads[2:]:
        copy.wait()
    for s in both:
        put_rows(streams[s], [cot[s][:, r, :] for r in range(streams[s].R)], xm[s].at[COT])
    pack_own(COT)

    for s in both:
        n, w, W = streams[s].n, streams[s].w, streams[s].W
        for t in range(9):
            back = slice((8 - t) * n, (9 - t) * n)
            a4[s][(8 - t) // 3, (8 - t) % 3 * n : ((8 - t) % 3 + 1) * n, :] = first[s][t * n : (t + 1) * n, :]
            taps[back, 0:w] = second[s][t // 3, (t % 3) * n : (t % 3 + 1) * n, :]
        group = lanes_of((1, w)) // streams[s].gs
        for g in range(GROUPS):
            chosen = jnp.where(group == g, 1.0, 0.0).astype(BF16)
            for i in range(3):
                ag[s][i, 3 * n * g : 3 * n * (g + 1), :] = a4[s][i] * chosen
        a1[s][...] = first[s][...].T
        a3[s][...] = taps[0 : 9 * n, 0:w].T
        same = subs_of((w, w)) == lanes_of((w, w))
        for src, dst in (((fine_gain, coarse_gain)[s], ga[s]), ((fine_shift, coarse_shift)[s], sh[s])):
            dst[...] = jnp.broadcast_to(jnp.sum(jnp.where(same, src[...][None, :], 0.0), axis=1, keepdims=True), (w, 128))
        R = streams[s].R
        mk[s][...] = jnp.ones((1, streams[s].NL), F32)
        mk[s][:, 0:W] = jnp.where(row > 0, 1.0, 0.0) * jnp.ones((1, W), F32)
        mk[s][:, (R + 1) * W : (R + 2) * W] = jnp.where(row < rows - 1, 1.0, 0.0) * jnp.ones((1, W), F32)
        lane = lanes_of((1, 128))
        q, line = lane % 8, lane // 8
        good = ((q == 0) & (col > 0)) | ((q == 3) & (col < cols - 1))
        good = good & (line < R + 2) & ((line > 0) | (row > 0)) & ((line < R + 1) | (row < rows - 1))
        mk[s][:, streams[s].main :] = jnp.where(good, 1.0, 0.0)
    here, there = subs_of((128, 256)), lanes_of((128, 256))
    dup[...] = jnp.where(there // 2 == here, 1.0, 0.0).astype(BF16)
    here, there = subs_of((256, 256)), lanes_of((256, 256))
    split[...] = jnp.where(here == 2 * (there % 128) + there // 128, 1.0, 0.0).astype(BF16)
    for a in range(2):
        for b in range(2):
            at = slice((2 * a + b) * f.n, (2 * a + b + 1) * f.n)
            rt[at, :] = reduction[at, :]
            taps[at, 0 : c.n] = up[...]
    rw[...] = rt[...].T
    u4[...] = taps[0 : 4 * f.n, 0 : c.n].T

    def spread_wide(k, weights, outs, ring=True):
        if ring:
            exchange_wait(k)
        tiles = edges(k, ring)
        for s in both:
            build(streams[s], xm[s].at[k], tiles[s], x3[s], x9[s], ring)
            widen(streams[s], weights[s], x3[s], x9[s], outs[s])

    def masked(s, k, x):
        W, R = streams[s].W, streams[s].R
        return x if W <= 128 * k < (R + 1) * W else x * mk[s][:, block(k, 128)]

    def group_loop(s, start, chunks, count, body):
        gs = streams[s].gs
        sums = []
        for g in range(GROUPS):
            at = slice(g * gs, (g + 1) * gs)

            accs = [jnp.zeros((8, 128), F32)] * count
            for k in range(start, start + chunks):
                accs = [a + fold(t) for a, t in zip(accs, body(g, at, k))]
            sums.append(accs)
        return [[sums[g][t] for g in range(GROUPS)] for t in range(count)]

    def ring_chunks(s):
        return 0, streams[s].NL // 128

    def own_chunks(s):
        return streams[s].W // 128, streams[s].cells // 128

    def flat(per_stream, t):
        return [a for s in both for a in per_stream[s][t]]

    sums = []
    spread_wide(STATE, a1, nm)
    for s in both:

        def squares(g, at, k):
            x = nm[s][at, block(k, 128)]
            return x, x * x

        sums.append(group_loop(s, *own_chunks(s), 2, squares))
    reduce_start(0, to_row(flat(sums, 0) + flat(sums, 1)))
    spread_wide(COT, a1, kc, ring=False)

    def group_images(fields):
        for s in both:
            got = narrow(streams[s], ag[s], hb[s], zg[s])
            for g in range(GROUPS):
                for r in range(streams[s].R):
                    fields[s][g, :, r * streams[s].W : (r + 1) * streams[s].W] = got(r, g)

    reduce_middle(0)
    for s in both:
        hb[s][...] = jnp.broadcast_to(mk[s][...], hb[s].shape).astype(BF16)
    group_images(one)
    stats = reduce_end(0)

    lane = lanes_of((1, 128))
    counts = [rows * cols * streams[s].cells * streams[s].gs for s in both]
    per = jnp.where(lane % 8 < GROUPS, 1.0 / counts[0], 1.0 / counts[1])
    mean_row = stats * per
    variance = roll(mean_row, -8) - mean_row * mean_row
    inverse_row = jnp.where(lane < 8, lax.rsqrt(variance + EPSILON), 0.0)
    weight = (inverse_row + roll(inverse_row, 8)) * per
    means = [[pick(mean_row, s * GROUPS + g) for g in range(GROUPS)] for s in both]
    inverses = [[pick(inverse_row, s * GROUPS + g) for g in range(GROUPS)] for s in both]

    for s in both:
        gs = streams[s].gs
        for g in range(GROUPS):
            at = slice(g * gs, (g + 1) * gs)

            for k in range(streams[s].NL // 128):
                here = block(k, 128)
                gain, keep = ga[s][at, :], mk[s][:, here]
                normed = (nm[s][at, here] - means[s][g]) * inverses[s][g]
                level = normed * gain + sh[s][at, :]
                sigma = jax.nn.sigmoid(level)
                nm[s][at, here] = normed
                hb[s][at, here] = (level * sigma * keep).astype(BF16)
                ls[s][at, here] = sigma * (1.0 + level * (1.0 - sigma)) * gain * keep

    def own_row(s, ref, r):
        return ref[:, r * streams[s].W : (r + 1) * streams[s].W]

    def halve():
        parts = dot(stack_f[...], split[...]).astype(BF16)
        lined = []
        for R in range(c.R):
            lined.append(jnp.concatenate([
                parts[(2 * R + a) * f.n : (2 * R + a + 1) * f.n, b * 128 : (b + 1) * 128]
                for a in range(2) for b in range(2)], axis=0))
        return jnp.concatenate(lined, axis=1)

    def double():
        return dot(stack_c[...], dup[...]).astype(BF16)

    for s, stack in ((0, stack_f), (1, stack_c)):
        n = streams[s].n
        got = narrow(streams[s], second[s], hb[s], zs[s])
        for r in range(streams[s].R):
            mixed = got(r) + inject[s][:, r, :].astype(F32)
            sl[s][:, r * streams[s].W : (r + 1) * streams[s].W] = mixed
            stack[r * n : (r + 1) * n, :] = mixed.astype(BF16)
    down = dot(rw[...], halve())
    wide = double()
    for R in range(c.R):
        lifted = dot(up[...], wide[R * c.n : (R + 1) * c.n, :])
        for r in (2 * R, 2 * R + 1):
            at = slice(r * f.W, (r + 1) * f.W)
            sl_f[:, at] = swish_derivative(sl_f[:, at] + lifted)
    sl_c[...] = swish_derivative(sl_c[...] + down)

    def total(field, k):
        for r in range(f.R):
            stack_f[r * f.n : (r + 1) * f.n, :] = (field(0, r) * own_row(0, sl_f, r)).astype(BF16)
        coarse_grads = [field(1, r) * own_row(1, sl_c, r) for r in range(c.R)]
        for r in range(c.R):
            stack_c[r * c.n : (r + 1) * c.n, :] = coarse_grads[r].astype(BF16)
        raised = dot(u4[...], halve())
        put_rows(c, [coarse_grads[r] + own_row(1, raised, r) for r in range(c.R)], xm_c.at[k])
        wide = double()
        even = lanes_of((f.n, f.W)) % 2 == 0
        fine = []
        for R in range(c.R):
            spread_out = dot(rt[...], wide[R * c.n : (R + 1) * c.n, :])
            for a in range(2):
                part = [spread_out[(2 * a + b) * f.n : (2 * a + b + 1) * f.n] for b in range(2)]
                r = 2 * R + a
                fine.append(field(0, r) * own_row(0, sl_f, r) + jnp.where(even, part[0], part[1]))
        put_rows(f, fine, xm_f.at[k])
        exchange_start(k)

    total(lambda s, r: cot[s][:, r, :], TOTAL0)

    sums = []
    spread_wide(TOTAL0, a3, hg, ring=False)
    for s in both:

        def pushed(g, at, k):
            scaled = hg[s][at, block(k, 128)] * ls[s][at, block(k, 128)]
            return scaled, scaled * nm[s][at, block(k, 128)]

        sums.append(group_loop(s, *ring_chunks(s), 2, pushed))
    reduce_start(1, to_row(flat(sums, 0) + flat(sums, 1)))

    for s in both:
        for g in range(GROUPS):
            at = slice(g * streams[s].gs, (g + 1) * streams[s].gs)
            for k in range(streams[s].NL // 128):
                hb[s][at, block(k, 128)] = masked(s, k, nm[s][at, block(k, 128)]).astype(BF16)
    group_images(two)

    reduce_middle(1)
    spread_wide(TOTAL0, a3, hg)
    along = []
    for s in both:

        def cot_sums(g, at, k):
            x = masked(s, k, kc[s][at, block(k, 128)])
            return x, x * nm[s][at, block(k, 128)]

        along.append(group_loop(s, *ring_chunks(s), 2, cot_sums))

    def uncentred():
        for s in both:
            gs = streams[s].gs
            for g in range(GROUPS):
                at = slice(g * gs, (g + 1) * gs)
                for k in range(streams[s].NL // 128):
                    here = block(k, 128)
                    hb[s][at, here] = (inverses[s][g] * (hg[s][at, here] * ls[s][at, here])).astype(BF16)
            got = narrow(streams[s], a4[s], hb[s], zs[s])
            for r in range(streams[s].R):
                zn[s][:, r * streams[s].W : (r + 1) * streams[s].W] = got(r)

    def centred(row_sums):
        scaled_mean = row_sums * weight
        picked = [[[pick(scaled_mean, 8 * t + s * GROUPS + g) for g in range(GROUPS)] for t in range(2)] for s in both]

        def rows_of(s, r):
            at = slice(r * streams[s].W, (r + 1) * streams[s].W)
            value = zn[s][:, at]
            for g in range(GROUPS):
                value = value - picked[s][0][g] * one[s][g, :, at] - picked[s][1][g] * two[s][g, :, at]
            return value

        return rows_of

    uncentred()
    rows_of = centred(reduce_end(1))
    for s in both:
        for r in range(streams[s].R):
            es[s][:, r * streams[s].W : (r + 1) * streams[s].W] = rows_of(s, r)
        put_rows(streams[s], [own_row(s, es[s], r) for r in range(streams[s].R)], xm[s].at[IMAGE])
    total(lambda s, r: own_row(s, es[s], r), TOTAL1)

    gram = [jnp.zeros((8, 128), F32) for _ in range(3)]
    for s in both:
        for r in range(streams[s].R):
            a, b = cot[s][:, r, :], own_row(s, es[s], r)
            for t, product in enumerate((a * a, a * b, b * b)):
                product = fold(product)
                for half in range(streams[s].W // 128):
                    gram[t] = gram[t] + product[:, half * 128 : (half + 1) * 128]
    pack_own(IMAGE)
    spread_wide(IMAGE, a1, kp, ring=False)
    image_sums = []
    for s in both:

        def lifted_sums(g, at, k):
            x = masked(s, k, kp[s][at, block(k, 128)])
            return x, x * nm[s][at, block(k, 128)]

        image_sums.append(group_loop(s, *ring_chunks(s), 2, lifted_sums))
    spread_wide(TOTAL1, a3, hg)
    sums, pairs = [], []
    crossed = [jnp.zeros((8, 128), F32) for _ in range(2)]
    for s in both:

        def own_sums(g, at, k):
            here = block(k, 128)
            scaled = hg[s][at, here] * ls[s][at, here]
            return scaled, scaled * nm[s][at, here]

        def pair_sums(g, at, k):
            here = block(k, 128)
            scaled = hg[s][at, here] * ls[s][at, here]
            return scaled * kc[s][at, here], scaled * kp[s][at, here]

        sums.append(group_loop(s, *own_chunks(s), 2, own_sums))
        pairs.append(group_loop(s, *ring_chunks(s), 2, pair_sums))
        for g in range(GROUPS):
            for t in range(2):
                crossed[t] = crossed[t] + pairs[s][t][g] * inverses[s][g]
    entries = flat(sums, 0) + flat(sums, 1) + flat(along, 0) + flat(along, 1) + flat(image_sums, 0) + flat(image_sums, 1)
    reduce_start(2, to_row(entries + gram + crossed))
    uncentred()
    reduce_middle(2)
    found = reduce_end(2)

    cc, c0, g00, cq, pq = [pick(found, 48 + k) for k in range(5)]
    c1 = cq - jnp.sum(found * weight * roll(found, -16), axis=1, keepdims=True)
    g01 = pq - jnp.sum(found * weight * roll(found, -32), axis=1, keepdims=True)
    d0 = jnp.maximum(cc - c0, 0.25 * cc)
    alpha = 1.0 + c0 / d0
    kappa = alpha * g00 / d0
    turn = -alpha * (c1 - c0)
    d1 = jnp.maximum(-alpha * alpha * (g01 - g00) - kappa * alpha * (c1 - c0), 0.25 * alpha * alpha * g00)
    m0 = -((1.0 - alpha) * c0 + alpha * c1)
    m1 = -alpha * ((1.0 - alpha) * g00 + alpha * g01) + kappa * m0
    by0 = 1.0 - m0 / d0 + (m1 / d1) * (turn / d0)
    by1 = alpha * (1.0 - m1 / d1)

    rows_of = centred(found)
    for s in both:
        for r in range(streams[s].R):
            outs[s][:, r, :] = cot[s][:, r, :] + by0 * own_row(s, es[s], r) + by1 * rows_of(s, r)

    for k in range(SENT):
        exchange_end(k)
    for k in range(3):
        reduce_drain(k)


def solution(mesh):
    rows, cols = mesh.shape["row"], mesh.shape["col"]
    sizes = (rows, cols, min(rows, 8), min(cols, 4))

    def body(*args):
        fine_state, coarse_state = args[:2]
        fine_first, fine_second, coarse_first, coarse_second = args[6:10]
        f = Stream(fine_state.shape[0], fine_first.shape[1], *fine_state.shape[1:])
        c = Stream(coarse_state.shape[0], coarse_first.shape[1], *coarse_state.shape[1:])
        both = (f, c)
        args = list(args)
        for k, s in ((6, f), (8, c)):
            args[k] = args[k].transpose(0, 2, 1).reshape(9 * s.n, s.w)
            args[k + 1] = args[k + 1].reshape(3, 3 * s.n, s.w)
        args[14] = args[14].transpose(0, 1, 3, 2).reshape(4 * f.n, c.n)
        vmem = pltpu.VMEM
        scratch = [vmem(a.shape, a.dtype) for a in args[:10]] + [pltpu.SemaphoreType.DMA((10,))]
        for shape, dtype in (
            (lambda s: (5, s.n, (s.R + 4) * s.W), BF16),
            (lambda s: (3 * s.n, (s.R + 4) * s.W), BF16),
            (lambda s: (3, 3 * s.n, 128), BF16),
            (lambda s: (s.w, s.NL), F32),
            (lambda s: (s.w, s.NL), F32),
            (lambda s: (s.w, s.NL), F32),
            (lambda s: (s.w, s.NL), BF16),
            (lambda s: (s.w, s.NL), F32),
            (lambda s: (s.w, s.NL), F32),
            (lambda s: (3 * s.n, s.cells), F32),
            (lambda s: (s.n, s.cells), F32),
            (lambda s: (s.n, s.cells), F32),
            (lambda s: (s.n, s.cells), F32),
            (lambda s: (1, s.NL), F32),
            (lambda s: (s.w, 128), F32),
            (lambda s: (s.w, 128), F32),
            (lambda s: (s.w, 9 * s.n), BF16),
            (lambda s: (s.w, 9 * s.n), BF16),
            (lambda s: (3, 3 * s.n, s.w), BF16),
            (lambda s: (3, GROUPS * 3 * s.n, s.w), BF16),
            (lambda s: (GROUPS * 3 * s.n, s.cells), F32),
            (lambda s: (GROUPS, s.n, s.cells), F32),
            (lambda s: (GROUPS, s.n, s.cells), F32),
        ):
            scratch += [vmem(shape(s), dtype) for s in both]
        scratch += [
            vmem((128, 256), BF16),
            vmem((256, 256), BF16),
            vmem((4 * f.n, c.n), BF16),
            vmem((c.n, 4 * f.n), BF16),
            vmem((c.n, 4 * f.n), BF16),
            vmem((f.R * f.n, f.W), BF16),
            vmem((c.R * c.n, c.W), BF16),
            vmem((9 * c.n, c.w), BF16),
            vmem((5, f.n + c.n, 128), BF16),
            vmem((SENT, 2, f.n + c.n, 128), BF16),
            vmem((SENT, 2, 16, 128), BF16),
            vmem((SENT, 4, 16, 128), BF16),
            vmem((3, sizes[2] * (cols // sizes[3]), 1, 128), F32),
            vmem((3, (rows // sizes[2]) * sizes[3], 1, 128), F32),
            pltpu.SemaphoreType.DMA((SENT, 10)),
            pltpu.SemaphoreType.DMA((SENT, 10)),
            pltpu.SemaphoreType.DMA((3, 2)),
            pltpu.SemaphoreType.DMA((3, 2)),
        ]
        return pl.pallas_call(
            functools.partial(kernel, both, sizes),
            out_shape=[jax.ShapeDtypeStruct(a.shape, F32) for a in args[4:6]],
            in_specs=[pl.BlockSpec(memory_space=pl.ANY)] * 10 + [pl.BlockSpec(memory_space=pltpu.VMEM)] * 6,
            out_specs=[pl.BlockSpec(memory_space=pltpu.VMEM)] * 2,
            scratch_shapes=scratch,
            compiler_params=pltpu.CompilerParams(
                collective_id=0, has_side_effects=True, vmem_limit_bytes=56 * 1024 * 1024
            ),
        )(*args)
    field = P(None, "row", "col")
    return jax.shard_map(
        body,
        mesh=mesh,
        in_specs=(field,) * 6 + (P(),) * 10,
        out_specs=(field, field),
        check_vma=False,
    )
```

```python
import functools

import jax
import jax.numpy as jnp
from jax import lax
from jax.experimental import pallas as pl
from jax.experimental.pallas import tpu as pltpu
from jax.sharding import PartitionSpec as P

GROUPS = 4
EPSILON = 1e-05
MESH = pl.DeviceIdType.MESH
F32 = jnp.float32
BF16 = jnp.bfloat16
DIRS = [(dr, dc) for dr in (-1, 0, 1) for dc in (-1, 0, 1) if dr or dc]
DIAGONALS = [(-1, -1), (-1, 1), (1, -1), (1, 1)]
STATE, TOTAL0, TOTAL1, COT, IMAGE = range(5)
SENT = 3


class Stream:
    def __init__(self, n, w, rows, cols):
        self.n, self.w, self.R, self.W = n, w, rows, cols
        self.gs = w // GROUPS
        self.main = (rows + 2) * cols
        self.NL = self.main + 128
        self.cells = rows * cols
        self.own = slice(2 * cols, 2 * cols + rows * cols)


def dot(a, b):
    return jnp.dot(a, b, preferred_element_type=F32)


def lanes_of(shape):
    return lax.broadcasted_iota(jnp.int32, shape, len(shape) - 1)


def subs_of(shape):
    return lax.broadcasted_iota(jnp.int32, shape, 0)


def roll(x, shift):
    return pltpu.roll(x, shift % x.shape[1], 1)


def wide_lanes(x, width):
    return x if width == 128 else jnp.concatenate([x] * (width // 128), axis=1)


def fold(x):
    return jnp.sum(x.reshape(x.shape[0] // 8, 8, x.shape[1]), axis=0)


def block(i, size):
    return slice(i * size, (i + 1) * size)


def swish_derivative(v):
    sigma = jax.nn.sigmoid(v)
    return sigma * (1.0 + v * (1.0 - sigma))


def to_row(accs):
    row = jnp.zeros((1, 128), F32)
    sub, lane = subs_of((8, 128)), lanes_of((8, 128))
    for first in range(0, len(accs), 8):
        stack = jnp.zeros((8, 128), F32)
        for k, acc in enumerate(accs[first : first + 8]):
            stack = jnp.where(sub == k, jnp.sum(acc, axis=0, keepdims=True), stack)
        col = jnp.sum(stack, axis=1, keepdims=True)
        row = row + jnp.sum(jnp.where(lane == sub + first, col, 0.0), axis=0, keepdims=True)
    return row


def pick(row, k):
    return jnp.sum(jnp.where(lanes_of((1, 128)) == k, row, 0.0), axis=1, keepdims=True)


def put_rows(s, rows, xm):
    for r, x in enumerate(rows):
        xm[:, (r + 2) * s.W : (r + 3) * s.W] = x.astype(BF16)


def pack(s, xm, lines):
    lane = lanes_of((s.n, 128))
    packed = jnp.zeros((s.n, 128), F32)
    for k in lines:
        left, right = xm[:, k * s.W : k * s.W + 128], xm[:, (k + 1) * s.W - 128 : (k + 1) * s.W]
        x = jnp.where(lane < 2, left.astype(F32), jnp.where(lane >= 126, right.astype(F32), 0.0))
        packed = packed + roll(x, 8 * k + 2)
    return jnp.where(lane % 8 <= 2, packed, roll(packed, 2))


def build(s, xm, edge, x3, x9, ring):
    n, W = s.n, s.W
    lane = lanes_of((n, 128))
    joined = jnp.where(lane % 8 == 0, roll(edge, -4), edge)
    lane = lanes_of((n, W))
    for k in range(s.R + 4):
        at = slice(k * W, (k + 1) * W)
        if not ring and not 2 <= k < s.R + 2:
            x3[:, at] = jnp.zeros((3 * n, W), BF16)
            continue
        x = xm[:, at]
        xf = x.astype(F32)
        t = wide_lanes(roll(joined, -(8 * k + 1)), W)
        x3[0:n, at] = jnp.where(lane == 0, t, roll(xf, 1)).astype(BF16)
        x3[n : 2 * n, at] = x
        x3[2 * n : 3 * n, at] = jnp.where(lane == W - 1, t, roll(xf, -1)).astype(BF16)
    for i in range(3):
        for j in range(3):
            x9[i, j * n : (j + 1) * n, :] = roll(edge, -(8 * i + j)).astype(BF16)


def widen(s, weights, x3, x9, out):
    taps = [x3[:, i * s.W : i * s.W + s.main] for i in range(3)]
    out[:, 0 : s.main] = dot(weights[...], jnp.concatenate(taps, axis=0))
    out[:, s.main :] = dot(weights[...], jnp.concatenate([x9[i] for i in range(3)], axis=0))


def narrow(s, weights, h, z):
    n, W = s.n, s.W
    for b in range(0, s.cells, 256):
        total = dot(weights[0], h[:, b : b + 256])
        for i in (1, 2):
            total = total + dot(weights[i], h[:, b + i * W : b + i * W + 256])
        z[0 : total.shape[0], b : b + 256] = total
    edges = [dot(weights[i], h[:, s.main :]) for i in range(3)]
    total = edges[0] + roll(edges[1], -8) + roll(edges[2], -16)
    q = lanes_of((n, 128)) % 8
    joined = []
    for g in range(0, total.shape[0], 3 * n):
        joined.append(jnp.where(q == 1, roll(total[g : g + n], 1), roll(total[g + 2 * n : g + 3 * n], -3)))
    lane = lanes_of((n, W))

    def row(r, g=0):
        at, base = slice(r * W, (r + 1) * W), 3 * n * g
        t = wide_lanes(roll(joined[g], -(8 * r + 1)), W)
        left = jnp.where(lane == 0, t, roll(z[base : base + n, at], 1))
        right = jnp.where(lane == W - 1, t, roll(z[base + 2 * n : base + 3 * n, at], -1))
        return left + z[base + n : base + 2 * n, at] + right

    return row


def kernel(streams, sizes, *refs):
    f, c = streams
    far, refs = refs[:10], refs[10:]
    (
        fine_gain, fine_shift, coarse_gain, coarse_shift, reduction, up,
        fine_out, coarse_out,
        *rest,
    ) = refs
    near, load_sem, rest = rest[:10], rest[10], rest[11:]
    (
        fine_state, coarse_state, fine_inject, coarse_inject, fine_cot, coarse_cot,
        fine_first, fine_second, coarse_first, coarse_second,
    ) = near
    (xm_f, xm_c, x3_f, x3_c, x9_f, x9_c,
     nm_f, nm_c, ls_f, ls_c, hg_f, hg_c, hb_f, hb_c, kc_f, kc_c, kp_f, kp_c,
     z_f, z_c, sl_f, sl_c, e_f, e_c, zn_f, zn_c, mk_f, mk_c, ga_f, ga_c, sh_f, sh_c,
     a1_f, a1_c, a3_f, a3_c, a4_f, a4_c, ag_f, ag_c, zg_f, zg_c, one_f, one_c, two_f, two_c, dup, split, rt, rw, u4, stack_f, stack_c, taps,
     pk, pr, corner, corners, ar_a, ar_b, halo_send, halo_recv, ar_send, ar_recv) = rest
    xm, x3, x9 = (xm_f, xm_c), (x3_f, x3_c), (x9_f, x9_c)
    nm, ls, hg, hb = (nm_f, nm_c), (ls_f, ls_c), (hg_f, hg_c), (hb_f, hb_c)
    kc, kp, zs, sl, es, mk = (kc_f, kc_c), (kp_f, kp_c), (z_f, z_c), (sl_f, sl_c), (e_f, e_c), (mk_f, mk_c)
    ga, sh, a1, a3, a4 = (ga_f, ga_c), (sh_f, sh_c), (a1_f, a1_c), (a3_f, a3_c), (a4_f, a4_c)
    zn = (zn_f, zn_c)
    ag, zg, one, two = (ag_f, ag_c), (zg_f, zg_c), (one_f, one_c), (two_f, two_c)
    first, second = (fine_first, coarse_first), (fine_second, coarse_second)
    cot, state = (fine_cot, coarse_cot), (fine_state, coarse_state)
    inject, outs = (fine_inject, coarse_inject), (fine_out, coarse_out)
    rows, cols, low_rows, low_cols = sizes
    high_rows, high_cols = rows // low_rows, cols // low_cols
    row, col = lax.axis_index("row"), lax.axis_index("col")
    both = (0, 1)
    own_part = (slice(0, f.n), slice(f.n, f.n + c.n))

    def has(d):
        return (row + d[0] >= 0) & (row + d[0] < rows) & (col + d[1] >= 0) & (col + d[1] < cols)

    nx, ny = low_rows // 2, high_cols
    nz = high_rows * low_cols
    x, core, y = row % low_rows // 2, row % 2, col // low_cols
    z = row // low_rows * low_cols + col % low_cols

    def steps(n, at):
        return [(at + d) % n for d in range(n)]

    x_rows = [2 * v + core for v in steps(nx, x)]
    y_cols = [v * low_cols for v in steps(ny, y)]
    z_both = [(v // low_cols * low_rows, v % low_cols) for v in steps(nz, z)]

    def hops(d):
        return sum(min(v, n - v) for v, n in zip(d, (nx, ny, nz)))

    offsets = [(a, b, c) for a in range(nx) for b in range(ny) for c in range(nz) if a or b or c]
    offsets.sort(key=lambda d: (-hops(d), d))
    chips = [(z_both[d][0] + x_rows[a], y_cols[b] + z_both[d][1]) for a, b, d in offsets]
    partner = [(row + 1 - 2 * core, col)]
    size_a, size_b = 2, nx * ny * nz
    me_a, me_b = core, (x * ny + y) * nz + z

    def strips(k):
        made = []
        for s in both:
            W, R = streams[s].W, streams[s].R
            for i, d, src, dst in ((s, (-1, 0), 2 * W, (R + 2) * W), (2 + s, (1, 0), R * W, 0)):
                made.append((pltpu.make_async_remote_copy(
                    src_ref=xm[s].at[k, :, pl.ds(src, 2 * W)], dst_ref=xm[s].at[k, :, pl.ds(dst, 2 * W)],
                    send_sem=halo_send.at[k, i], recv_sem=halo_recv.at[k, i],
                    device_id=(row + d[0], col), device_id_type=MESH), d))
        return made

    def packs(k):
        made = []
        for i, dc in ((4, -1), (5, 1)):
            made.append((pltpu.make_async_remote_copy(
                src_ref=pk.at[k], dst_ref=pr.at[k, i - 4],
                send_sem=halo_send.at[k, i], recv_sem=halo_recv.at[k, i],
                device_id=(row, col + dc), device_id_type=MESH), (0, dc)))
        for i, (dr, dc) in enumerate(DIAGONALS):
            made.append((pltpu.make_async_remote_copy(
                src_ref=corner.at[k, (dr + 1) // 2], dst_ref=corners.at[k, i],
                send_sem=halo_send.at[k, 6 + i], recv_sem=halo_recv.at[k, 6 + i],
                device_id=(row + dr, col + dc), device_id_type=MESH), (dr, dc)))
        return made

    def pack_own(k):
        for s in both:
            R = streams[s].R
            pk[k, own_part[s], :] = pack(streams[s], xm[s].at[k], range(2, R + 2)).astype(BF16)

    def exchange_start(k):
        for copy, d in strips(k):
            pl.when(has(d))(copy.start)
        pack_own(k)
        own = pk[k].astype(F32)
        shift = 8 * (f.R - c.R)
        low = jnp.concatenate([own[: f.n], roll(own[f.n :], shift)], axis=0)
        lane = lanes_of(own.shape)
        cells = jnp.where(lane < 8 * (c.R + 2), own, low)
        cells = jnp.concatenate([cells, jnp.zeros((128 - f.n - c.n, 128), F32)], axis=0).T
        corner[k, 0] = cells[16:32].astype(BF16)
        corner[k, 1] = cells[8 * f.R : 8 * f.R + 16].astype(BF16)
        for copy, d in packs(k):
            pl.when(has(d))(copy.start)

    def exchange_wait(k):
        for copy, d in strips(k) + packs(k):
            pl.when(has((-d[0], -d[1])))(copy.wait_recv)

    def exchange_end(k):
        for copy, d in strips(k) + packs(k):
            pl.when(has(d))(copy.wait_send)

    def edges(k, ring):
        lane = lanes_of((f.n + c.n, 128))
        q = lane % 8
        own = pk[k].astype(F32)
        if ring:
            sides = jnp.where(q <= 1, pr[k, 1].astype(F32), jnp.where(q <= 3, own, pr[k, 0].astype(F32)))
            sub = subs_of((16, 128)) % 8
            got = [corners[k, i].astype(F32) for i in range(4)]
            above = jnp.where(sub <= 3, got[DIAGONALS.index((1, 1))], got[DIAGONALS.index((1, -1))])
            below = jnp.where(sub <= 3, got[DIAGONALS.index((-1, 1))], got[DIAGONALS.index((-1, -1))])
            low = 8 * (f.R + 2)
            blank = [jnp.zeros((low - 16, 128), F32), jnp.zeros((112 - low, 128), F32)]
            cells = jnp.concatenate([above, blank[0], below, blank[1]], axis=0).T
        else:
            sides = jnp.where((q >= 2) & (q <= 3), own, 0.0)
        made = []
        for s in both:
            n, R = streams[s].n, streams[s].R
            lane = lanes_of((n, 128))
            q = lane % 8
            outside = jnp.zeros((n, 128), F32)
            if ring:
                outer = cells[own_part[s]]
                outer = jnp.where(lane < 16, outer, roll(outer, 8 * (R - f.R)))
                lines = pack(streams[s], xm[s].at[k], (0, 1, R + 2, R + 3))
                outside = jnp.where((q >= 2) & (q <= 3), lines, outer)
            inside = (lane >= 16) & (lane < 16 + 8 * R)
            made.append(jnp.where(inside, sides[own_part[s]], outside))
        return made

    def spread(k, stage, buf, me, peers):
        for peer in peers:
            pltpu.make_async_remote_copy(
                src_ref=buf.at[k, me], dst_ref=buf.at[k, me],
                send_sem=ar_send.at[k, stage], recv_sem=ar_recv.at[k, stage],
                device_id=peer, device_id_type=MESH).start()

    def collect(k, stage, buf, size):
        ref = buf.at[k, pl.ds(0, size - 1)]
        pltpu.make_async_copy(ref, ref, ar_recv.at[k, stage]).wait()
        return jnp.sum(buf[k], axis=0)

    def reduce_start(k, value):
        ar_a[k, me_a] = value
        spread(k, 0, ar_a, me_a, partner)

    def reduce_middle(k):
        ar_b[k, me_b] = collect(k, 0, ar_a, size_a)
        spread(k, 1, ar_b, me_b, chips)

    def reduce_end(k):
        return collect(k, 1, ar_b, size_b)

    def reduce_drain(k):
        for stage, buf, size in ((0, ar_a, size_a), (1, ar_b, size_b)):
            ref = buf.at[k, pl.ds(0, size - 1)]
            pltpu.make_async_copy(ref, ref, ar_send.at[k, stage]).wait()

    loads = [pltpu.make_async_copy(a, b, load_sem.at[k]) for k, (a, b) in enumerate(zip(far, near))]
    for copy in loads:
        copy.start()
    for s in both:
        W, R = streams[s].W, streams[s].R
        for k in range(SENT):
            xm[s][k, :, 0 : 2 * W] = jnp.zeros((streams[s].n, 2 * W), BF16)
            xm[s][k, :, (R + 2) * W : (R + 4) * W] = jnp.zeros((streams[s].n, 2 * W), BF16)
    pr[...] = jnp.zeros(pr.shape, BF16)
    corners[...] = jnp.zeros(corners.shape, BF16)
    barrier = pltpu.get_barrier_semaphore()

    def greet(device):
        pl.semaphore_signal(barrier, inc=1, device_id=device, device_id_type=MESH)

    for d in DIRS:
        pl.when(has(d))(functools.partial(greet, (row + d[0], col + d[1])))

    for device in chips + partner:
        greet(device)
    for copy in loads[:2]:
        copy.wait()
    for s in both:
        put_rows(streams[s], [state[s][:, r, :] for r in range(streams[s].R)], xm[s].at[STATE])
    beside = sum(has(d).astype(jnp.int32) for d in DIRS)
    pl.semaphore_wait(barrier, beside + (size_a + size_b - 2))
    exchange_start(STATE)
    for copy in loads[2:]:
        copy.wait()
    for s in both:
        put_rows(streams[s], [cot[s][:, r, :] for r in range(streams[s].R)], xm[s].at[COT])
    pack_own(COT)

    for s in both:
        n, w, W = streams[s].n, streams[s].w, streams[s].W
        for t in range(9):
            back = slice((8 - t) * n, (9 - t) * n)
            a4[s][(8 - t) // 3, (8 - t) % 3 * n : ((8 - t) % 3 + 1) * n, :] = first[s][t * n : (t + 1) * n, :]
            taps[back, 0:w] = second[s][t // 3, (t % 3) * n : (t % 3 + 1) * n, :]
        group = lanes_of((1, w)) // streams[s].gs
        for g in range(GROUPS):
            chosen = jnp.where(group == g, 1.0, 0.0).astype(BF16)
            for i in range(3):
                ag[s][i, 3 * n * g : 3 * n * (g + 1), :] = a4[s][i] * chosen
        a1[s][...] = first[s][...].T
        a3[s][...] = taps[0 : 9 * n, 0:w].T
        same = subs_of((w, w)) == lanes_of((w, w))
        for src, dst in (((fine_gain, coarse_gain)[s], ga[s]), ((fine_shift, coarse_shift)[s], sh[s])):
            dst[...] = jnp.broadcast_to(jnp.sum(jnp.where(same, src[...][None, :], 0.0), axis=1, keepdims=True), (w, 128))
        R = streams[s].R
        mk[s][...] = jnp.ones((1, streams[s].NL), F32)
        mk[s][:, 0:W] = jnp.where(row > 0, 1.0, 0.0) * jnp.ones((1, W), F32)
        mk[s][:, (R + 1) * W : (R + 2) * W] = jnp.where(row < rows - 1, 1.0, 0.0) * jnp.ones((1, W), F32)
        lane = lanes_of((1, 128))
        q, line = lane % 8, lane // 8
        good = ((q == 0) & (col > 0)) | ((q == 3) & (col < cols - 1))
        good = good & (line < R + 2) & ((line > 0) | (row > 0)) & ((line < R + 1) | (row < rows - 1))
        mk[s][:, streams[s].main :] = jnp.where(good, 1.0, 0.0)
    here, there = subs_of((128, 256)), lanes_of((128, 256))
    dup[...] = jnp.where(there // 2 == here, 1.0, 0.0).astype(BF16)
    here, there = subs_of((256, 256)), lanes_of((256, 256))
    split[...] = jnp.where(here == 2 * (there % 128) + there // 128, 1.0, 0.0).astype(BF16)
    for a in range(2):
        for b in range(2):
            at = slice((2 * a + b) * f.n, (2 * a + b + 1) * f.n)
            rt[at, :] = reduction[at, :]
            taps[at, 0 : c.n] = up[...]
    rw[...] = rt[...].T
    u4[...] = taps[0 : 4 * f.n, 0 : c.n].T

    def spread_wide(k, weights, outs, ring=True):
        if ring:
            exchange_wait(k)
        tiles = edges(k, ring)
        for s in both:
            build(streams[s], xm[s].at[k], tiles[s], x3[s], x9[s], ring)
            widen(streams[s], weights[s], x3[s], x9[s], outs[s])

    def masked(s, k, x):
        W, R = streams[s].W, streams[s].R
        return x if W <= 128 * k < (R + 1) * W else x * mk[s][:, block(k, 128)]

    def group_loop(s, start, chunks, count, body):
        gs = streams[s].gs
        sums = []
        for g in range(GROUPS):
            at = slice(g * gs, (g + 1) * gs)

            accs = [jnp.zeros((8, 128), F32)] * count
            for k in range(start, start + chunks):
                accs = [a + fold(t) for a, t in zip(accs, body(g, at, k))]
            sums.append(accs)
        return [[sums[g][t] for g in range(GROUPS)] for t in range(count)]

    def ring_chunks(s):
        return 0, streams[s].NL // 128

    def own_chunks(s):
        return streams[s].W // 128, streams[s].cells // 128

    def flat(per_stream, t):
        return [a for s in both for a in per_stream[s][t]]

    sums = []
    spread_wide(STATE, a1, nm)
    for s in both:

        def squares(g, at, k):
            x = nm[s][at, block(k, 128)]
            return x, x * x

        sums.append(group_loop(s, *own_chunks(s), 2, squares))
    reduce_start(0, to_row(flat(sums, 0) + flat(sums, 1)))
    reduce_middle(0)
    spread_wide(COT, a1, kc, ring=False)

    def group_images(fields):
        for s in both:
            got = narrow(streams[s], ag[s], hb[s], zg[s])
            for g in range(GROUPS):
                for r in range(streams[s].R):
                    fields[s][g, :, r * streams[s].W : (r + 1) * streams[s].W] = got(r, g)

    for s in both:
        hb[s][...] = jnp.broadcast_to(mk[s][...], hb[s].shape).astype(BF16)
    group_images(one)
    stats = reduce_end(0)

    lane = lanes_of((1, 128))
    counts = [rows * cols * streams[s].cells * streams[s].gs for s in both]
    per = jnp.where(lane % 8 < GROUPS, 1.0 / counts[0], 1.0 / counts[1])
    mean_row = stats * per
    variance = roll(mean_row, -8) - mean_row * mean_row
    inverse_row = jnp.where(lane < 8, lax.rsqrt(variance + EPSILON), 0.0)
    weight = (inverse_row + roll(inverse_row, 8)) * per
    means = [[pick(mean_row, s * GROUPS + g) for g in range(GROUPS)] for s in both]
    inverses = [[pick(inverse_row, s * GROUPS + g) for g in range(GROUPS)] for s in both]

    for s in both:
        gs = streams[s].gs
        for g in range(GROUPS):
            at = slice(g * gs, (g + 1) * gs)

            for k in range(streams[s].NL // 128):
                here = block(k, 128)
                gain, keep = ga[s][at, :], mk[s][:, here]
                normed = (nm[s][at, here] - means[s][g]) * inverses[s][g]
                level = normed * gain + sh[s][at, :]
                sigma = jax.nn.sigmoid(level)
                nm[s][at, here] = normed
                hb[s][at, here] = (level * sigma * keep).astype(BF16)
                ls[s][at, here] = sigma * (1.0 + level * (1.0 - sigma)) * gain * keep

    def own_row(s, ref, r):
        return ref[:, r * streams[s].W : (r + 1) * streams[s].W]

    def halve():
        parts = dot(stack_f[...], split[...]).astype(BF16)
        lined = []
        for R in range(c.R):
            lined.append(jnp.concatenate([
                parts[(2 * R + a) * f.n : (2 * R + a + 1) * f.n, b * 128 : (b + 1) * 128]
                for a in range(2) for b in range(2)], axis=0))
        return jnp.concatenate(lined, axis=1)

    def double():
        return dot(stack_c[...], dup[...]).astype(BF16)

    for s, stack in ((0, stack_f), (1, stack_c)):
        n = streams[s].n
        got = narrow(streams[s], second[s], hb[s], zs[s])
        for r in range(streams[s].R):
            mixed = got(r) + inject[s][:, r, :].astype(F32)
            sl[s][:, r * streams[s].W : (r + 1) * streams[s].W] = mixed
            stack[r * n : (r + 1) * n, :] = mixed.astype(BF16)
    down = dot(rw[...], halve())
    wide = double()
    for R in range(c.R):
        lifted = dot(up[...], wide[R * c.n : (R + 1) * c.n, :])
        for r in (2 * R, 2 * R + 1):
            at = slice(r * f.W, (r + 1) * f.W)
            sl_f[:, at] = swish_derivative(sl_f[:, at] + lifted)
    sl_c[...] = swish_derivative(sl_c[...] + down)

    def total(field, k):
        for r in range(f.R):
            stack_f[r * f.n : (r + 1) * f.n, :] = (field(0, r) * own_row(0, sl_f, r)).astype(BF16)
        coarse_grads = [field(1, r) * own_row(1, sl_c, r) for r in range(c.R)]
        for r in range(c.R):
            stack_c[r * c.n : (r + 1) * c.n, :] = coarse_grads[r].astype(BF16)
        raised = dot(u4[...], halve())
        put_rows(c, [coarse_grads[r] + own_row(1, raised, r) for r in range(c.R)], xm_c.at[k])
        wide = double()
        even = lanes_of((f.n, f.W)) % 2 == 0
        fine = []
        for R in range(c.R):
            spread_out = dot(rt[...], wide[R * c.n : (R + 1) * c.n, :])
            for a in range(2):
                part = [spread_out[(2 * a + b) * f.n : (2 * a + b + 1) * f.n] for b in range(2)]
                r = 2 * R + a
                fine.append(field(0, r) * own_row(0, sl_f, r) + jnp.where(even, part[0], part[1]))
        put_rows(f, fine, xm_f.at[k])
        exchange_start(k)

    total(lambda s, r: cot[s][:, r, :], TOTAL0)

    sums = []
    spread_wide(TOTAL0, a3, hg, ring=False)
    for s in both:

        def pushed(g, at, k):
            scaled = hg[s][at, block(k, 128)] * ls[s][at, block(k, 128)]
            return scaled, scaled * nm[s][at, block(k, 128)]

        sums.append(group_loop(s, *ring_chunks(s), 2, pushed))
    reduce_start(1, to_row(flat(sums, 0) + flat(sums, 1)))

    reduce_middle(1)
    for s in both:
        for g in range(GROUPS):
            at = slice(g * streams[s].gs, (g + 1) * streams[s].gs)
            for k in range(streams[s].NL // 128):
                hb[s][at, block(k, 128)] = masked(s, k, nm[s][at, block(k, 128)]).astype(BF16)
    group_images(two)

    spread_wide(TOTAL0, a3, hg)
    along = []
    for s in both:

        def cot_sums(g, at, k):
            x = masked(s, k, kc[s][at, block(k, 128)])
            return x, x * nm[s][at, block(k, 128)]

        along.append(group_loop(s, *ring_chunks(s), 2, cot_sums))

    def uncentred():
        for s in both:
            gs = streams[s].gs
            for g in range(GROUPS):
                at = slice(g * gs, (g + 1) * gs)
                for k in range(streams[s].NL // 128):
                    here = block(k, 128)
                    hb[s][at, here] = (inverses[s][g] * (hg[s][at, here] * ls[s][at, here])).astype(BF16)
            got = narrow(streams[s], a4[s], hb[s], zs[s])
            for r in range(streams[s].R):
                zn[s][:, r * streams[s].W : (r + 1) * streams[s].W] = got(r)

    def centred(row_sums):
        scaled_mean = row_sums * weight
        picked = [[[pick(scaled_mean, 8 * t + s * GROUPS + g) for g in range(GROUPS)] for t in range(2)] for s in both]

        def rows_of(s, r):
            at = slice(r * streams[s].W, (r + 1) * streams[s].W)
            value = zn[s][:, at]
            for g in range(GROUPS):
                value = value - picked[s][0][g] * one[s][g, :, at] - picked[s][1][g] * two[s][g, :, at]
            return value

        return rows_of

    uncentred()
    rows_of = centred(reduce_end(1))
    for s in both:
        for r in range(streams[s].R):
            es[s][:, r * streams[s].W : (r + 1) * streams[s].W] = rows_of(s, r)
        put_rows(streams[s], [own_row(s, es[s], r) for r in range(streams[s].R)], xm[s].at[IMAGE])
    total(lambda s, r: own_row(s, es[s], r), TOTAL1)

    gram = [jnp.zeros((8, 128), F32) for _ in range(3)]
    for s in both:
        for r in range(streams[s].R):
            a, b = cot[s][:, r, :], own_row(s, es[s], r)
            for t, product in enumerate((a * a, a * b, b * b)):
                product = fold(product)
                for half in range(streams[s].W // 128):
                    gram[t] = gram[t] + product[:, half * 128 : (half + 1) * 128]
    pack_own(IMAGE)
    spread_wide(IMAGE, a1, kp, ring=False)
    image_sums = []
    for s in both:

        def lifted_sums(g, at, k):
            x = masked(s, k, kp[s][at, block(k, 128)])
            return x, x * nm[s][at, block(k, 128)]

        image_sums.append(group_loop(s, *ring_chunks(s), 2, lifted_sums))
    spread_wide(TOTAL1, a3, hg)
    sums, pairs = [], []
    crossed = [jnp.zeros((8, 128), F32) for _ in range(2)]
    for s in both:

        def own_sums(g, at, k):
            here = block(k, 128)
            scaled = hg[s][at, here] * ls[s][at, here]
            return scaled, scaled * nm[s][at, here]

        def pair_sums(g, at, k):
            here = block(k, 128)
            scaled = hg[s][at, here] * ls[s][at, here]
            return scaled * kc[s][at, here], scaled * kp[s][at, here]

        sums.append(group_loop(s, *own_chunks(s), 2, own_sums))
        pairs.append(group_loop(s, *ring_chunks(s), 2, pair_sums))
        for g in range(GROUPS):
            for t in range(2):
                crossed[t] = crossed[t] + pairs[s][t][g] * inverses[s][g]
    entries = flat(sums, 0) + flat(sums, 1) + flat(along, 0) + flat(along, 1) + flat(image_sums, 0) + flat(image_sums, 1)
    reduce_start(2, to_row(entries + gram + crossed))
    reduce_middle(2)
    uncentred()
    found = reduce_end(2)

    cc, c0, g00, cq, pq = [pick(found, 48 + k) for k in range(5)]
    c1 = cq - jnp.sum(found * weight * roll(found, -16), axis=1, keepdims=True)
    g01 = pq - jnp.sum(found * weight * roll(found, -32), axis=1, keepdims=True)
    d0 = jnp.maximum(cc - c0, 0.25 * cc)
    alpha = 1.0 + c0 / d0
    kappa = alpha * g00 / d0
    turn = -alpha * (c1 - c0)
    d1 = jnp.maximum(-alpha * alpha * (g01 - g00) - kappa * alpha * (c1 - c0), 0.25 * alpha * alpha * g00)
    m0 = -((1.0 - alpha) * c0 + alpha * c1)
    m1 = -alpha * ((1.0 - alpha) * g00 + alpha * g01) + kappa * m0
    by0 = 1.0 - m0 / d0 + (m1 / d1) * (turn / d0)
    by1 = alpha * (1.0 - m1 / d1)

    rows_of = centred(found)
    for s in both:
        for r in range(streams[s].R):
            outs[s][:, r, :] = cot[s][:, r, :] + by0 * own_row(s, es[s], r) + by1 * rows_of(s, r)

    for k in range(SENT):
        exchange_end(k)
    for k in range(3):
        reduce_drain(k)


def solution(mesh):
    rows, cols = mesh.shape["row"], mesh.shape["col"]
    sizes = (rows, cols, min(rows, 8), min(cols, 4))

    def body(*args):
        fine_state, coarse_state = args[:2]
        fine_first, fine_second, coarse_first, coarse_second = args[6:10]
        f = Stream(fine_state.shape[0], fine_first.shape[1], *fine_state.shape[1:])
        c = Stream(coarse_state.shape[0], coarse_first.shape[1], *coarse_state.shape[1:])
        both = (f, c)
        args = list(args)
        for k, s in ((6, f), (8, c)):
            args[k] = args[k].transpose(0, 2, 1).reshape(9 * s.n, s.w)
            args[k + 1] = args[k + 1].reshape(3, 3 * s.n, s.w)
        args[14] = args[14].transpose(0, 1, 3, 2).reshape(4 * f.n, c.n)
        vmem = pltpu.VMEM
        scratch = [vmem(a.shape, a.dtype) for a in args[:10]] + [pltpu.SemaphoreType.DMA((10,))]
        for shape, dtype in (
            (lambda s: (5, s.n, (s.R + 4) * s.W), BF16),
            (lambda s: (3 * s.n, (s.R + 4) * s.W), BF16),
            (lambda s: (3, 3 * s.n, 128), BF16),
            (lambda s: (s.w, s.NL), F32),
            (lambda s: (s.w, s.NL), F32),
            (lambda s: (s.w, s.NL), F32),
            (lambda s: (s.w, s.NL), BF16),
            (lambda s: (s.w, s.NL), F32),
            (lambda s: (s.w, s.NL), F32),
            (lambda s: (3 * s.n, s.cells), F32),
            (lambda s: (s.n, s.cells), F32),
            (lambda s: (s.n, s.cells), F32),
            (lambda s: (s.n, s.cells), F32),
            (lambda s: (1, s.NL), F32),
            (lambda s: (s.w, 128), F32),
            (lambda s: (s.w, 128), F32),
            (lambda s: (s.w, 9 * s.n), BF16),
            (lambda s: (s.w, 9 * s.n), BF16),
            (lambda s: (3, 3 * s.n, s.w), BF16),
            (lambda s: (3, GROUPS * 3 * s.n, s.w), BF16),
            (lambda s: (GROUPS * 3 * s.n, s.cells), F32),
            (lambda s: (GROUPS, s.n, s.cells), F32),
            (lambda s: (GROUPS, s.n, s.cells), F32),
        ):
            scratch += [vmem(shape(s), dtype) for s in both]
        scratch += [
            vmem((128, 256), BF16),
            vmem((256, 256), BF16),
            vmem((4 * f.n, c.n), BF16),
            vmem((c.n, 4 * f.n), BF16),
            vmem((c.n, 4 * f.n), BF16),
            vmem((f.R * f.n, f.W), BF16),
            vmem((c.R * c.n, c.W), BF16),
            vmem((9 * c.n, c.w), BF16),
            vmem((5, f.n + c.n, 128), BF16),
            vmem((SENT, 2, f.n + c.n, 128), BF16),
            vmem((SENT, 2, 16, 128), BF16),
            vmem((SENT, 4, 16, 128), BF16),
            vmem((3, 2, 1, 128), F32),
            vmem((3, rows * cols // 2, 1, 128), F32),
            pltpu.SemaphoreType.DMA((SENT, 10)),
            pltpu.SemaphoreType.DMA((SENT, 10)),
            pltpu.SemaphoreType.DMA((3, 2)),
            pltpu.SemaphoreType.DMA((3, 2)),
        ]
        return pl.pallas_call(
            functools.partial(kernel, both, sizes),
            out_shape=[jax.ShapeDtypeStruct(a.shape, F32) for a in args[4:6]],
            in_specs=[pl.BlockSpec(memory_space=pl.ANY)] * 10 + [pl.BlockSpec(memory_space=pltpu.VMEM)] * 6,
            out_specs=[pl.BlockSpec(memory_space=pltpu.VMEM)] * 2,
            scratch_shapes=scratch,
            compiler_params=pltpu.CompilerParams(
                collective_id=0, has_side_effects=True, vmem_limit_bytes=56 * 1024 * 1024
            ),
        )(*args)
    field = P(None, "row", "col")
    return jax.shard_map(
        body,
        mesh=mesh,
        in_specs=(field,) * 6 + (P(),) * 10,
        out_specs=(field, field),
        check_vma=False,
    )
```
